32 devices in a mesh: dir: 2 (over core), seq: 16 (over z, y, x).
Axes of the slice: x: 2, y: 2, z: 4, core: 2. Of those that a mesh axis runs over, the one named last changes fastest.
Arguments:
- tokens: bfloat16 [16384, 512], P('seq'), may hold values from -6 to 6
- segment_ids: int32 [16384], P('seq'), may hold values from 0 to 3, never falling along the last dimension, each value on 1 to 8192 neighbouring positions
- norm_gain: float32 [2, 512], replicated, may hold values from 0.5 to 1.5
- norm_bias: float32 [2, 512], replicated, may hold values from -3 to 3
- input_matrix: bfloat16 [2, 2, 512, 768], P(None, 'dir'), may hold values from -0.25 to 0.25
- output_matrix: bfloat16 [2, 2, 768, 512], P(None, 'dir'), may hold values from -0.21875 to 0.21875
- rate_params: float32 [2, 2, 384], P(None, 'dir'), may hold values from -9 to 3, as said below
- turn_params: float32 [2, 2, 2, 384], P(None, 'dir'), may hold values from -810 to 810, as said below
- skip_weight: float32 [2, 512], replicated, may hold values from -4 to 4
- glu_weight: bfloat16 [2, 512, 512], replicated, may hold values from -0.25 to 0.25
- glu_bias: float32 [2, 512], replicated, may hold values from -3 to 3
- cotangent: float32 [16384, 512], P('seq'), may hold values from -6 to 6
Outputs:
- block_output: float32 [16384, 512], P('seq')
- tokens_grad: float32 [16384, 512], P('seq')
- norm_gain_grad: float32 [2, 512], replicated
- norm_bias_grad: float32 [2, 512], replicated
- input_matrix_grad: float32 [2, 2, 512, 768], P(None, 'dir')
- output_matrix_grad: float32 [2, 2, 768, 512], P(None, 'dir')
- rate_params_grad: float32 [2, 2, 384], P(None, 'dir')
- turn_params_grad: float32 [2, 2, 2, 384], P(None, 'dir')
- skip_weight_grad: float32 [2, 512], replicated
- glu_weight_grad: float32 [2, 512, 512], replicated
- glu_bias_grad: float32 [2, 512], replicated
The draws below stay inside these ranges and needn't reach their ends.
Inputs may be any that keep to these rules, and one draw needn't show every extreme that they name: `segment_ids`: ids never fall along the tokens; one id covers 1 to 8192 consecutive tokens. For every direction and state the damping exp(rate_params[l,s] + turn_params[l,s,1]) lies between 2e-5 and 0.035. exp(turn_params[l,s,1]) lies between 0.0024 and 0.14.
All inputs are finite; a program needn't handle non-finite values.
Results may differ from the reference program's by a relative error of at most 0.017.
Values may be sent and summed in bfloat16 or wider, within the bound.
No kernel may reach another device: no remote copies, remote signals or barrier semaphores. Data moves between devices by JAX's collectives and lax.ppermute only.
A program may use at most 192 MiB of HBM per device.

```python
import math
import jax
import jax.numpy as jnp
import numpy as np
from jax import lax

H = 512
P_SIZE = 384
LAYERS = 2
SIDES = 2
LENGTH = 16384
ROWS = 1
TOKENS = 16384
SEGS = 4


def decay_table(key):
    keys = jax.random.split(jax.random.fold_in(key, 7), 5)
    shape = (LAYERS, SIDES, P_SIZE)
    slow_share = 0.5
    angle_reach = 1.0
    picked = jax.random.uniform(keys[0], shape) < slow_share
    slow_log = jax.random.uniform(keys[1], shape, minval=math.log(2e-05), maxval=math.log(0.00012))
    fast_log = jax.random.uniform(keys[2], shape, minval=math.log(0.02), maxval=math.log(0.035))
    log_damping = jnp.where(picked, slow_log, fast_log)
    log_step = jax.random.uniform(keys[3], shape, minval=-6.0, maxval=-2.0)
    angle = jax.random.uniform(keys[4], shape, minval=-angle_reach, maxval=angle_reach)
    log_rate = log_damping - log_step
    frequency = angle / jnp.exp(log_step)
    return (log_rate, frequency, log_step)


def draw_rate_params(key, part):
    log_rate, frequency, log_step = decay_table(key)
    return log_rate.astype(jnp.float32)


def draw_turn_params(key, part):
    log_rate, frequency, log_step = decay_table(key)
    return jnp.stack([frequency, log_step], axis=2).astype(jnp.float32)


def levels(key, shape, shards, smallest, high):
    def one(position, blocks):
        heights = jax.random.uniform(jax.random.fold_in(jax.random.fold_in(key, 6), position), (blocks,), jnp.float32, smallest / len(shards), high / len(shards))
        return jnp.repeat(jnp.exp(heights), shape[position] // blocks).reshape((-1,) + (1,) * (len(shape) - position - 1))

    level = one(*shards[0])
    for cut in shards[1:]:
        level = level * one(*cut)
    return level


def split_up(number_of, total, most, slope):
    portions = [(1 << 20) // math.isqrt(rank ** slope) + 1 for rank in range(2, number_of + 1)]
    spare, counts = total - most - (number_of - 1), [1] * (number_of - 1)
    while spare > 0:
        movable = [i for i in range(number_of - 1) if counts[i] < most]
        mass, remaining = sum([portions[i] for i in movable]), spare
        for i in movable:
            more = min(most - counts[i], max(1, remaining * portions[i] // mass), spare)
            counts[i] = counts[i] + more
            spare = spare - more
    return np.array([most] + counts)


def ragged_sizes(rng, count, total, most, slope):
    if count == 2:
        one = jax.random.randint(rng, (), max(1, total - most), min(most, total - 1) + 1)
        return jnp.stack([one, total - one])
    sizes = jnp.asarray(split_up(count, total, most, slope), jnp.int32)
    couples = (count - 1) // 2
    source_of, sink = sizes[1:1 + 2 * couples:2], sizes[2:2 + 2 * couples:2]
    room = jnp.minimum(source_of - 1, most - sink)
    shifted = jax.random.randint(jax.random.fold_in(rng, 1), (couples,), 0, 1 << 20) % (room + 1)
    sizes = sizes.at[1:1 + 2 * couples:2].set(source_of - shifted).at[2:2 + 2 * couples:2].set(sink + shifted)
    return sizes[jax.random.permutation(jax.random.fold_in(rng, 2), count)]


def noise(rng, shape, deviation, bound, cuts=(), dtype=jnp.bfloat16):
    factor_of = levels(rng, shape, cuts, -0.22, 0.18) if cuts else 1.0
    values = jax.random.normal(rng, shape, jnp.float32) * deviation * factor_of
    return jnp.minimum(jnp.maximum(values, -bound), bound).astype(dtype)


def setup_inputs(seed: int = 0) -> dict:
    key_of = jax.random.split(jax.random.key(seed), 13)
    return {
        "tokens": noise(key_of[0], (TOKENS, H), 1.0, 6.0, ((0, 16),)),
        "segment_ids": jnp.searchsorted(jnp.cumsum(ragged_sizes(key_of[1], SEGS, TOKENS, LENGTH // 2, 1)), jnp.arange(TOKENS), side="right").astype(jnp.int32),
        "norm_gain": jnp.clip(1.0 + 0.1 * jax.random.normal(key_of[2], (LAYERS, H), jnp.float32), 0.5, 1.5),
        "norm_bias": noise(key_of[3], (LAYERS, H), 0.5, 3.0, (), jnp.float32),
        "input_matrix": noise(key_of[4], (LAYERS, SIDES, H, 2 * P_SIZE), H ** -0.5, 0.25, ((1, 2),)),
        "output_matrix": noise(key_of[5], (LAYERS, SIDES, 2 * P_SIZE, H), (2 * P_SIZE) ** -0.5, 0.21875, ((1, 2),)),
        "rate_params": draw_rate_params(jax.random.fold_in(key_of[12], 71), 0),
        "turn_params": draw_turn_params(jax.random.fold_in(key_of[12], 71), 0),
        "skip_weight": noise(key_of[8], (LAYERS, H), 1.0, 4.0, (), jnp.float32),
        "glu_weight": noise(key_of[9], (LAYERS, H, H), H ** -0.5, 0.25),
        "glu_bias": noise(key_of[10], (LAYERS, H), 0.5, 3.0, (), jnp.float32),
        "cotangent": noise(key_of[11], (TOKENS, H), 1.0, 6.0, ((0, 16),), jnp.float32),
    }


@jax.custom_vjp
def low(v):
    return lax.optimization_barrier(v.astype(jnp.bfloat16)).astype(jnp.float32)

@jax.custom_vjp
def low_back(v):
    return v

def low_keep(v):
    return (low(v), None)

def low_pass(kept, grad):
    return (grad,)

def back_keep(v):
    return (v, None)

def back_low(kept, grad):
    return (low(grad),)
low.defvjp(low_keep, low_pass)
low_back.defvjp(back_keep, back_low)
eps = 1e-05
highest = lax.Precision.HIGHEST

def decay_terms(log_rate, turn):
    frequency = turn[0]
    log_step = turn[1]
    step_size = jnp.exp(log_step)
    damping = jnp.exp(log_rate + log_step)
    magnitude = jnp.exp(-damping)
    rotation = frequency * step_size
    decay_re = magnitude * jnp.cos(rotation)
    decay_im = magnitude * jnp.sin(rotation)
    scaling = jnp.sqrt(-jnp.expm1(-2.0 * damping))
    return (decay_re, decay_im, scaling)

def combine_steps(earlier, following):
    first_re, first_im, value_re, value_im = earlier
    second_re, second_im, added_re, added_im = following
    return (first_re * second_re - first_im * second_im, first_re * second_im + first_im * second_re, second_re * value_re - second_im * value_im + added_re, second_re * value_im + second_im * value_re + added_im)

def time_scan(factor_re, factor_im, drive_re, drive_im):
    results = lax.associative_scan(combine_steps, (factor_re, factor_im, drive_re, drive_im), axis=1)
    return (results[2], results[3])

def layer_forward(residual, starts, finishes, norm_scale, norm_shift, in_matrix, out_matrix, rates, turns, skip_term, gate_matrix, gate_bias):
    average = lax.optimization_barrier(jnp.mean(residual, -1, keepdims=True))
    centred = residual - average
    normed = centred * lax.rsqrt(lax.optimization_barrier(jnp.mean(centred * centred, -1, keepdims=True)) + eps)
    mixed = normed * norm_scale + norm_shift
    mixed_low = low(mixed)
    side_total = jnp.zeros(residual.shape, jnp.float32)
    for side in range(SIDES):
        decay_re, decay_im, scaling = decay_terms(rates[side], turns[side])
        projected = low_back(jnp.dot(mixed_low, in_matrix[side], precision=highest))
        driven = projected * jnp.concatenate([scaling, scaling])
        drive_re = driven[:, :P_SIZE].reshape(ROWS, LENGTH, P_SIZE)
        drive_im = driven[:, P_SIZE:].reshape(ROWS, LENGTH, P_SIZE)
        if side == 0:
            keep_mask = (1.0 - starts)[:, :, None]
            states_re, states_im = time_scan(keep_mask * decay_re, keep_mask * decay_im, drive_re, drive_im)
        else:
            keep_mask = jnp.flip(1.0 - finishes, 1)[:, :, None]
            back_re, back_im = time_scan(keep_mask * decay_re, keep_mask * decay_im, jnp.flip(drive_re, 1), jnp.flip(drive_im, 1))
            states_re = jnp.flip(back_re, 1)
            states_im = jnp.flip(back_im, 1)
        states = jnp.concatenate([states_re, states_im], 2).reshape(TOKENS, 2 * P_SIZE)
        side_total = side_total + jnp.dot(low(states), out_matrix[side], precision=highest)
    combined = low_back(side_total) + skip_term * mixed
    activation = jax.nn.gelu(combined, approximate=False)
    gate_logit = low_back(jnp.dot(low(activation), gate_matrix, precision=highest)) + gate_bias
    return residual + activation * jax.nn.sigmoid(gate_logit)

def reference(tokens, segment_ids, norm_gain, norm_bias, input_matrix, output_matrix, rate_params, turn_params, skip_weight, glu_weight, glu_bias, cotangent):
    row_ids = segment_ids.reshape(ROWS, LENGTH)
    positions = jnp.arange(LENGTH)
    before = jnp.concatenate([row_ids[:, :1], row_ids[:, :-1]], 1)
    starts = jnp.where((positions[None, :] == 0) | (row_ids != before), 1.0, 0.0).astype(jnp.float32)
    finishes = jnp.concatenate([starts[:, 1:], jnp.ones((ROWS, 1), jnp.float32)], 1)
    weights = (norm_gain, norm_bias, input_matrix.astype(jnp.float32), output_matrix.astype(jnp.float32), rate_params, turn_params, skip_weight, glu_weight.astype(jnp.float32), glu_bias)

    def forward(residual, weights):
        for layer_index in range(LAYERS):
            residual = layer_forward(residual, starts, finishes, weights[0][layer_index], weights[1][layer_index], weights[2][layer_index], weights[3][layer_index], weights[4][layer_index], weights[5][layer_index], weights[6][layer_index], weights[7][layer_index], weights[8][layer_index])
        return residual
    result, pullback = jax.vjp(forward, tokens.astype(jnp.float32), weights)
    tokens_grad, gradients = pullback(cotangent)
    return (result, tokens_grad, gradients[0], gradients[1], gradients[2], gradients[3], gradients[4], gradients[5], gradients[6], gradients[7], gradients[8])
```

```python
import functools

import jax
import jax.numpy as jnp
from jax import lax
from jax.experimental import pallas as pl
from jax.experimental.pallas import tpu as pltpu
from jax.sharding import PartitionSpec as P

LENGTH = 16384
LONGEST_RUN = 8192

eps = 1e-05
inv_root_two = 0.7071067811865476
inv_root_two_pi = 0.3989422804014327

f32 = jnp.float32
bf16 = jnp.bfloat16


LANES = 128
ELEMENT_ROWS = 32
UNROLL = 4


def core_place(row_devices):
    core = lax.axis_index("dir")
    return core, lax.rem(lax.axis_index("seq"), row_devices) * 2 + core


def dot(a, b):
    return jnp.dot(a, b, preferred_element_type=f32)


def dot_nt(a, b):
    return lax.dot_general(a, b, (((1,), (1,)), ((), ())), preferred_element_type=f32)


def dot_tn(a, b):
    return lax.dot_general(a, b, (((0,), (0,)), ((), ())), preferred_element_type=f32)


def squared(re, im, times):
    for _ in range(times):
        re, im = re * re - im * im, 2.0 * re * im
    return re, im


def over_blocks(rows, step, init=()):
    def one(i, carry):
        return step(pl.multiple_of(i * ELEMENT_ROWS, ELEMENT_ROWS), carry)

    return lax.fori_loop(0, rows // ELEMENT_ROWS, one, init)


def fold(values):
    total = values[0:8]
    for start in range(8, values.shape[0], 8):
        total = total + values[start : start + 8]
    return total


class Lanes:
    def __init__(self, rows_ref, tiles_ref, layer, adjoint, spans, rows):
        states = rows_ref.shape[2]
        self.states = states
        self.rows_ref, self.layer = rows_ref, layer
        flip = -1.0 if adjoint else 1.0
        self.step = []
        self.run = []
        self.block = []
        for side in range(2):
            row = 8 * side
            re = rows_ref[layer, row : row + 1, :]
            im = rows_ref[layer, row + 1 : row + 2, :] * flip
            self.step.append((jnp.broadcast_to(re, (8, states)), jnp.broadcast_to(im, (8, states))))
            self.run.append(squared(re, im, (spans - 1).bit_length()))
            thirds = states // LANES
            tile_re = tiles_ref[layer, 8 * side : 8 * side + thirds, :]
            tile_im = tiles_ref[layer, 8 * side + thirds : 8 * side + 2 * thirds, :] * flip
            self.block.append(squared(tile_re, tile_im, (rows - 1).bit_length()))

    def scaling(self, side):
        row = self.rows_ref[self.layer, 8 * side + 2 : 8 * side + 3, :]
        return jnp.concatenate([row, row], 1)


def sweep(first_forward, drives, masks, lanes, init, visit=None, totals=()):
    states = lanes.states
    span = drives[0].shape[0] // 8

    def step(i, carry):
        values, sums = carry
        up = pl.multiple_of(i * 8, 8)
        down = pl.multiple_of((span - 1 - i) * 8, 8)
        places = (jnp.where(first_forward, up, down), jnp.where(first_forward, down, up))
        new = []
        for side in range(2):
            rows = pl.ds(pl.multiple_of(places[side], 8), 8)
            keep = masks[side][rows, :]
            keep = jnp.concatenate([keep] * (states // LANES), 1)
            step_re, step_im = lanes.step[side]
            step_re, step_im = step_re * keep, step_im * keep
            re, im = values[side]
            drive_re = drives[side][rows, :states]
            drive_im = drives[side][rows, states:]
            re, im = (
                step_re * re - step_im * im + drive_re,
                step_re * im + step_im * re + drive_im,
            )
            new.append((re, im))
            if visit is not None:
                sums = visit(side, rows, re, im, sums)
        return tuple(new), sums

    return lax.fori_loop(0, span, step, (init, totals), unroll=UNROLL)


def run_chain(first_up, lanes, side, ends, whole, start, places):
    states = lanes.states
    power_re, power_im = lanes.run[side]
    re, im = start
    for i in range(8):
        s = jnp.where(first_up, i, 7 - i)
        row = pl.ds(s, 1)
        if places is not None:
            places[row, :states] = re
            places[row, states:] = im
        passes = whole[row, :]
        passes = jnp.concatenate([passes] * (states // LANES), 1)
        pass_re, pass_im = power_re * passes, power_im * passes
        end_re, end_im = ends[row, :states], ends[row, states:]
        re, im = (end_re + pass_re * re - pass_im * im, end_im + pass_re * im + pass_im * re)
    return re, im


def first_pass(running_up, drives, masks, wholes, lanes, ids_ref, ends, payload):
    states = lanes.states
    thirds = states // LANES
    nothing = jnp.zeros((8, states), f32)
    zero = (nothing, nothing)
    values, _ = sweep(running_up, drives, masks, lanes, (zero, zero))
    payload[...] = jnp.zeros_like(payload)
    for side in range(2):
        ends[side][:, :states] = values[side][0]
        ends[side][:, states:] = values[side][1]
        upward = running_up if side == 0 else jnp.logical_not(running_up)
        start = jnp.zeros((1, states), f32)
        re, im = run_chain(upward, lanes, side, ends[side], wholes[side], (start, start), None)
        base = jnp.where(upward, 0, 8)
        for i in range(thirds):
            payload[pl.ds(base + i, 1), :] = re[:, LANES * i : LANES * (i + 1)]
            payload[pl.ds(base + thirds + i, 1), :] = im[:, LANES * i : LANES * (i + 1)]
        payload[8 * side + 6 : 8 * side + 8, :] = ids_ref[0:2, :]


def entering(upward, place, lanes, side, gathered, ids_ref, small):
    states = lanes.states
    thirds = states // LANES
    count = gathered.shape[0]
    rows = lanes.token_rows
    block_re, block_im = lanes.block[side]
    re = jnp.zeros((thirds, LANES), f32)
    im = jnp.zeros((thirds, LANES), f32)
    base = jnp.where(upward, 0, 8)
    key = jnp.where(upward, ids_ref[0:1, :], ids_ref[1:2, :])
    for distance in range(min(count - 1, LONGEST_RUN // rows), 0, -1):
        source = jnp.where(upward, place - distance, place + distance)
        inside = jnp.logical_and(source >= 0, source < count)
        source = jnp.clip(source, 0, count - 1)
        sent_re = gathered[source, pl.ds(base, thirds), :]
        sent_im = gathered[source, pl.ds(base + thirds, thirds), :]
        sent_key = gathered[source, pl.ds(jnp.where(upward, base + 7, base + 6), 1), :]
        joined = jnp.where(jnp.logical_and(sent_key == key, inside), 1.0, 0.0)
        re, im = (
            joined * sent_re + block_re * re - block_im * im,
            joined * sent_im + block_re * im + block_im * re,
        )
    small[0:thirds, :] = re
    small[thirds : 2 * thirds, :] = im
    wide_re = jnp.concatenate([small[i : i + 1, :] for i in range(thirds)], 1)
    wide_im = jnp.concatenate([small[thirds + i : thirds + i + 1, :] for i in range(thirds)], 1)
    return wide_re, wide_im


def second_starts(running_up, place, lanes, gathered, ids_ref, ends, wholes, places, small):
    init = []
    states = lanes.states
    for side in range(2):
        upward = running_up if side == 0 else jnp.logical_not(running_up)
        start = entering(upward, place, lanes, side, gathered, ids_ref, small)
        run_chain(upward, lanes, side, ends[side], wholes[side], start, places)
        init.append((places[:, :states], places[:, states:]))
    return tuple(init)


def make_lanes(rows_ref, tiles_ref, layer, adjoint, token_rows):
    lanes = Lanes(rows_ref, tiles_ref, layer, adjoint, token_rows // 8, token_rows)
    lanes.token_rows = token_rows
    return lanes


def standardise(x):
    width = x.shape[1]
    average = jnp.sum(x, 1, keepdims=True) * (1.0 / width)
    centred = x - average
    inv_scale = lax.rsqrt(jnp.sum(centred * centred, 1, keepdims=True) * (1.0 / width) + eps)
    return centred * inv_scale, inv_scale


def fill_columns(columns, values):
    for i in range(columns.shape[0]):
        columns[i] = values[:, i * LANES : (i + 1) * LANES].astype(columns.dtype)


def tile_order(columns, first, count, span):
    tiles = [
        jnp.concatenate([columns[i, pl.ds(first + j, 8, stride=span), :] for i in range(columns.shape[0])], 1)
        for j in range(count)
    ]
    return jnp.concatenate(tiles, 0)


def store_token_order(columns, first, values, span):
    for j in range(values.shape[0] // 8):
        for i in range(columns.shape[0]):
            columns[i, pl.ds(first + j, 8, stride=span), :] = values[8 * j : 8 * j + 8, i * LANES : (i + 1) * LANES]


def join_columns(out, columns):
    for i in range(columns.shape[0]):
        out[:, i * LANES : (i + 1) * LANES] = columns[i]


def one_minus_exp(x):
    series = jnp.ones_like(x)
    for term in range(12, 1, -1):
        series = 1.0 - x * (1.0 / term) * series
    return jnp.where(x < 0.5, x * series, 1.0 - jnp.exp(-x))


def table_rows(table, layer, base, rate, turn):
    frequency = turn[layer, 0, 0:1, :]
    log_step = turn[layer, 0, 1:2, :]
    step_size = jnp.exp(log_step)
    damping = jnp.exp(rate[layer, 0:1, :] + log_step)
    magnitude = jnp.exp(-damping)
    rotation = frequency * step_size
    square = magnitude * magnitude
    rows = (
        magnitude * jnp.cos(rotation), magnitude * jnp.sin(rotation), jnp.sqrt(one_minus_exp(2.0 * damping)), damping,
        step_size, rotation, square,
    )
    for i, row in enumerate(rows):
        table[layer, base + i : base + i + 1, :] = row


def open_kernel(
    row_devices,
    tokens,
    segments,
    gain,
    bias,
    rate,
    turn,
    in_own,
    x_out,
    normed_out,
    inv_out,
    mixed_out,
    drive_out,
    keep_own,
    keep_oth,
    whole_out,
    table,
    ids,
    natural,
    rows8,
):
    core, _ = core_place(row_devices)
    rows = x_out.shape[0]
    span = rows // 8
    base = pl.multiple_of(core * rows, rows)
    fill_columns(natural, tokens[pl.ds(base, rows), :].astype(f32))
    table[...] = jnp.zeros_like(table)
    for layer in range(table.shape[0]):
        table_rows(table, layer, 0, rate, turn)

    number = segments[...].astype(f32)
    count = number.shape[0]
    lane = lax.broadcasted_iota(jnp.int32, number.shape, 1)
    row = lax.broadcasted_iota(jnp.int32, number.shape, 0)
    back = pltpu.roll(number, 1, 1)
    back = jnp.where(lane == 0, pltpu.roll(back, 1, 0), back)
    ahead = pltpu.roll(number, LANES - 1, 1)
    ahead = jnp.where(lane == LANES - 1, pltpu.roll(ahead, count - 1, 0), ahead)
    edge_first = jnp.logical_and(lane == 0, row == 0)
    edge_last = jnp.logical_and(lane == LANES - 1, row == count - 1)
    up_keep = jnp.where(jnp.logical_or(number == back, edge_first), 1.0, 0.0)
    down_keep = jnp.where(jnp.logical_or(number == ahead, edge_last), 1.0, 0.0)
    per = LANES // span
    used = 8 // per
    for side, out in ((0, keep_own), (1, keep_oth)):
        rows8[0:count, :] = jnp.where(core == side, up_keep, down_keep)
        half = rows8[pl.ds(core * used, used), :]
        runs = jnp.concatenate([half[s // per : s // per + 1] for s in range(8)], 0)
        place = lax.broadcasted_iota(jnp.int32, (8, LANES), 1)
        sub = lax.broadcasted_iota(jnp.int32, (8, LANES), 0)
        first = lax.rem(sub, per) * span
        inside = jnp.logical_and(place >= first, place < first + span)
        least = jnp.min(jnp.where(inside, runs, 1.0), 1, keepdims=True)
        whole_out[side] = jnp.broadcast_to(least, (8, LANES))
        step = lax.broadcasted_iota(jnp.int32, (span, 8, LANES), 0)
        spread = jnp.where(step == (place - first)[None], runs[None], 0.0)
        spread = spread.reshape(span * 8, LANES).astype(bf16)
        out[...] = dot(spread, jnp.ones((LANES, LANES), bf16))
    rows8[0:count, :] = number
    first_row = rows8[pl.ds(core * used, 1), :]
    last_row = rows8[pl.ds(core * used + used - 1, 1), :]
    ids[...] = jnp.zeros_like(ids)
    ids[0:1, :] = jnp.broadcast_to(first_row[:, 0:1], (1, LANES))
    ids[1:2, :] = jnp.broadcast_to(last_row[:, LANES - 1 : LANES], (1, LANES))

    def element(start, carry):
        x = tile_order(natural, start // 8, ELEMENT_ROWS // 8, span)
        normed, inv_scale = standardise(x)
        block = pl.ds(start, ELEMENT_ROWS)
        x_out[block, :] = x
        normed_out[block, :] = normed
        inv_out[block, :] = jnp.broadcast_to(inv_scale, (ELEMENT_ROWS, LANES))
        mixed_out[block, :] = (normed * gain[0:1, :] + bias[0:1, :]).astype(bf16)
        return carry

    over_blocks(rows, element)
    scale = table[0, 2:3, :]
    drive_out[...] = dot(mixed_out[...], in_own[0, 0]) * jnp.concatenate([scale, scale], 1)


def open_second_kernel(
    row_devices,
    mixed_low,
    in_oth,
    rate,
    turn,
    table_in,
    drive_own,
    keep_own,
    keep_oth,
    whole,
    ids,
    drive_oth,
    ends_own,
    ends_oth,
    payload,
    table,
    tiles,
):
    core, _ = core_place(row_devices)
    table[...] = table_in[...]
    tiles[...] = jnp.zeros_like(tiles)
    thirds = table.shape[2] // LANES
    for layer in range(table.shape[0]):
        table_rows(table, layer, 8, rate, turn)
        for side in range(2):
            for part in range(2):
                for i in range(thirds):
                    at = 8 * side + part * thirds + i
                    tiles[layer, at : at + 1, :] = table[
                        layer, 8 * side + part : 8 * side + part + 1, i * LANES : (i + 1) * LANES
                    ]
    scale = table[0, 10:11, :]
    drive_oth[...] = dot(mixed_low[...], in_oth[0, 0]) * jnp.concatenate([scale, scale], 1)
    rows = drive_own.shape[0]
    lanes = make_lanes(table, tiles, 0, False, rows)
    first_pass(
        core == 0,
        (drive_own, drive_oth),
        (keep_own, keep_oth),
        (whole.at[0], whole.at[1]),
        lanes,
        ids,
        (ends_own, ends_oth),
        payload,
    )


def forward_states(layer, info, gathered, ends, drives, masks, whole, rows_ref, tiles_ref, ids, states, lows, places, small):
    rows = drives[0].shape[0]
    lanes = make_lanes(rows_ref, tiles_ref, layer, False, rows)
    core, place = info
    running_up = core == 0
    init = second_starts(
        running_up, place, lanes, gathered, ids, ends, (whole.at[0], whole.at[1]), places, small
    )
    width = lanes.states

    def visit(side, where, re, im, sums):
        states[side][where, :width] = re
        states[side][where, width:] = im
        return sums

    sweep(running_up, drives, masks, lanes, init, visit)
    for side in range(2):
        lows[side][...] = states[side][...].astype(bf16)


def mid_kernel(
    row_devices,
    gathered,
    ends_own,
    ends_oth,
    drive_own,
    drive_oth,
    keep_own,
    keep_oth,
    whole,
    rows_ref,
    tiles_ref,
    ids,
    out_own,
    out_oth,
    x_in,
    normed,
    gain,
    bias,
    skip,
    glu,
    glu_bias,
    in_own,
    in_oth,
    low_own,
    low_oth,
    combined_out,
    phi_out,
    sig_out,
    act_low,
    x_out,
    normed_out,
    inv_out,
    mixed_out,
    next_own,
    next_oth,
    next_ends_own,
    next_ends_oth,
    payload,
    places,
    small,
    wide,
    states_own,
    states_oth,
):
    info = core_place(row_devices)
    rows = x_in.shape[0]
    masks = (keep_own, keep_oth)
    forward_states(
        0, info, gathered, (ends_own, ends_oth), (drive_own, drive_oth), masks, whole, rows_ref, tiles_ref,
        ids, (states_own, states_oth), (low_own, low_oth), places, small,
    )
    wide[...] = dot(low_own[...], out_own[0, 0]) + dot(low_oth[...], out_oth[0, 0])

    def element(start, carry):
        block = pl.ds(start, ELEMENT_ROWS)
        mixed = normed[block, :] * gain[0:1, :] + bias[0:1, :]
        combined = wide[block, :] + skip[0:1, :] * mixed
        phi = 0.5 * (1.0 + lax.erf(combined * inv_root_two))
        combined_out[block, :] = combined
        phi_out[block, :] = phi
        act_low[block, :] = (combined * phi).astype(bf16)
        return carry

    over_blocks(rows, element)
    wide[...] = dot(act_low[...], glu[0])

    def element_two(start, carry):
        block = pl.ds(start, ELEMENT_ROWS)
        sig = jax.nn.sigmoid(wide[block, :] + glu_bias[0:1, :])
        sig_out[block, :] = sig
        x = x_in[block, :] + combined_out[block, :] * phi_out[block, :] * sig
        x_out[block, :] = x
        after, inv_scale = standardise(x)
        normed_out[block, :] = after
        inv_out[block, :] = jnp.broadcast_to(inv_scale, (ELEMENT_ROWS, LANES))
        mixed_out[block, :] = (after * gain[1:2, :] + bias[1:2, :]).astype(bf16)
        return carry

    over_blocks(rows, element_two)
    for side, (matrix, out) in enumerate(((in_own, next_own), (in_oth, next_oth))):
        scale = rows_ref[1, 8 * side + 2 : 8 * side + 3, :]
        out[...] = dot(mixed_out[...], matrix[1, 0]) * jnp.concatenate([scale, scale], 1)
    lanes = make_lanes(rows_ref, tiles_ref, 1, False, rows)
    first_pass(
        info[0] == 0,
        (next_own, next_oth),
        masks,
        (whole.at[0], whole.at[1]),
        lanes,
        ids,
        (next_ends_own, next_ends_oth),
        payload,
    )


def backward_half(
    layer, info, grad, combined, phi, sig, normed, gain, bias, skip, glu, out_own, out_oth, masks, whole,
    rows_ref, tiles_ref, ids, gate_low, combined_grad, combined_low, grad_own, grad_oth, ends, payload, sums, wide,
):
    rows = grad.shape[0]
    width = grad.shape[1]
    zero = jnp.zeros((8, width), f32)

    def element(start, carry):
        block = pl.ds(start, ELEMENT_ROWS)
        gate = sig[block, :]
        gate_grad = grad[block, :] * (combined[block, :] * phi[block, :]) * gate * (1.0 - gate)
        gate_low[block, :] = gate_grad.astype(bf16)
        return carry + fold(gate_grad)

    bias_sum = over_blocks(rows, element, zero)
    wide[...] = dot_nt(gate_low[...], glu[layer])

    def element_two(start, carry):
        block = pl.ds(start, ELEMENT_ROWS)
        value = combined[block, :]
        activation_grad = grad[block, :] * sig[block, :] + wide[block, :]
        slope = phi[block, :] + value * (jnp.exp(-0.5 * value * value) * inv_root_two_pi)
        result = activation_grad * slope
        combined_grad[block, :] = result
        combined_low[block, :] = result.astype(bf16)
        mixed = normed[block, :] * gain[layer : layer + 1, :] + bias[layer : layer + 1, :]
        return carry + fold(result * mixed)

    skip_sum = over_blocks(rows, element_two, zero)
    sums[0:1, :] = jnp.sum(bias_sum, 0, keepdims=True)
    sums[1:2, :] = jnp.sum(skip_sum, 0, keepdims=True)
    grad_own[...] = dot_nt(combined_low[...], out_own[layer, 0])
    grad_oth[...] = dot_nt(combined_low[...], out_oth[layer, 0])
    lanes = make_lanes(rows_ref, tiles_ref, layer, True, rows)
    first_pass(
        info[0] == 1,
        (grad_own, grad_oth),
        (masks[1], masks[0]),
        (whole.at[1], whole.at[0]),
        lanes,
        ids,
        ends,
        payload,
    )


def turn_kernel(
    row_devices,
    gathered,
    ends_own,
    ends_oth,
    drive_own,
    drive_oth,
    keep_own,
    keep_oth,
    whole,
    rows_ref,
    tiles_ref,
    ids,
    out_own,
    out_oth,
    x_in,
    normed,
    gain,
    bias,
    skip,
    glu,
    glu_bias,
    cotangent,
    low_own,
    low_oth,
    block_out,
    grad_out,
    act_low,
    gate_low,
    combined_grad,
    combined_low,
    grad_own,
    grad_oth,
    next_ends_own,
    next_ends_oth,
    payload,
    sums,
    places,
    small,
    wide,
    combined,
    phi_rows,
    sig_rows,
    natural,
    natural_out,
    states_own,
    states_oth,
):
    info = core_place(row_devices)
    rows = x_in.shape[0]
    span = rows // 8
    masks = (keep_own, keep_oth)
    forward_states(
        1, info, gathered, (ends_own, ends_oth), (drive_own, drive_oth), masks, whole, rows_ref, tiles_ref,
        ids, (states_own, states_oth), (low_own, low_oth), places, small,
    )
    wide[...] = dot(low_own[...], out_own[1, 0]) + dot(low_oth[...], out_oth[1, 0])

    def element(start, carry):
        block = pl.ds(start, ELEMENT_ROWS)
        mixed = normed[block, :] * gain[1:2, :] + bias[1:2, :]
        value = wide[block, :] + skip[1:2, :] * mixed
        phi = 0.5 * (1.0 + lax.erf(value * inv_root_two))
        combined[block, :] = value
        phi_rows[block, :] = phi
        act_low[block, :] = (value * phi).astype(bf16)
        return carry

    over_blocks(rows, element)
    wide[...] = dot(act_low[...], glu[1])
    base = pl.multiple_of(info[0] * rows, rows)
    fill_columns(natural, cotangent[pl.ds(base, rows), :])

    def element_two(start, carry):
        block = pl.ds(start, ELEMENT_ROWS)
        sig = jax.nn.sigmoid(wide[block, :] + glu_bias[1:2, :])
        sig_rows[block, :] = sig
        result = x_in[block, :] + combined[block, :] * phi_rows[block, :] * sig
        store_token_order(natural_out, start // 8, result, span)
        grad_out[block, :] = tile_order(natural, start // 8, ELEMENT_ROWS // 8, span)
        return carry

    over_blocks(rows, element_two)
    join_columns(block_out, natural_out)
    sums[...] = jnp.zeros_like(sums)
    backward_half(
        1, info, grad_out, combined, phi_rows, sig_rows, normed, gain, bias, skip, glu, out_own, out_oth, masks,
        whole, rows_ref, tiles_ref, ids, gate_low, combined_grad, combined_low, grad_own, grad_oth,
        (next_ends_own, next_ends_oth), payload, sums, wide,
    )


def adjoint_states(
    layer, info, gathered, ends, grads, masks, whole, rows_ref, tiles_ref, ids, states, drives, lows, decay_sums,
    adjoints, places, small,
):
    rows = grads[0].shape[0]
    lanes = make_lanes(rows_ref, tiles_ref, layer, True, rows)
    core, place = info
    running_up = core == 1
    init = second_starts(
        running_up, place, lanes, gathered, ids, ends, (whole.at[1], whole.at[0]), places, small
    )
    width = lanes.states
    zero = jnp.zeros((8, width), f32)
    for side in range(2):
        adjoints[side][...] = states[side][...].astype(f32)

    def visit(side, where, re, im, sums):
        drive_re, drive_im = drives[side][where, :width], drives[side][where, width:]
        moved_re = adjoints[side][where, :width] - drive_re
        moved_im = adjoints[side][where, width:] - drive_im
        adjoints[side][where, :width] = re
        adjoints[side][where, width:] = im
        mine = sums[side]
        mine = (
            mine[0] + (re * moved_re + im * moved_im),
            mine[1] + (im * moved_re - re * moved_im),
            mine[2] + (re * drive_re + im * drive_im),
        )
        return (mine, sums[1]) if side == 0 else (sums[0], mine)

    _, sums = sweep(
        running_up, grads, (masks[1], masks[0]), lanes, init, visit, ((zero, zero, zero), (zero, zero, zero))
    )
    decay_sums[...] = jnp.zeros_like(decay_sums)
    for side in range(2):
        for i in range(3):
            decay_sums[3 * side + i : 3 * side + i + 1, :] = jnp.sum(sums[side][i], 0, keepdims=True)
        lows[side][...] = (adjoints[side][...] * lanes.scaling(side)).astype(bf16)


def norm_backward(
    layer, low_own, low_oth, in_own, in_oth, grad, combined_grad, normed, inv_scale, gain, skip, sums, wide, finish
):
    rows, width = grad.shape
    wide[...] = dot_nt(low_own[...], in_own[layer, 0]) + dot_nt(low_oth[...], in_oth[layer, 0])
    zero = jnp.zeros((8, width), f32)

    def element(start, carry):
        block = pl.ds(start, ELEMENT_ROWS)
        mixed_grad = wide[block, :] + combined_grad[block, :] * skip[layer : layer + 1, :]
        unit = normed[block, :]
        weighted = mixed_grad * unit
        inner = mixed_grad * gain[layer : layer + 1, :]
        mean_one = jnp.sum(inner, 1, keepdims=True) * (1.0 / width)
        mean_two = jnp.sum(weighted * gain[layer : layer + 1, :], 1, keepdims=True) * (1.0 / width)
        spread = jnp.concatenate([inv_scale[block, :]] * (width // LANES), 1)
        finish(start, grad[block, :] + spread * (inner - mean_one - unit * mean_two))
        return carry[0] + fold(weighted), carry[1] + fold(mixed_grad)

    gain_sum, bias_sum = over_blocks(rows, element, (zero, zero))
    sums[2:3, :] = jnp.sum(gain_sum, 0, keepdims=True)
    sums[3:4, :] = jnp.sum(bias_sum, 0, keepdims=True)


def back_kernel(
    row_devices,
    gathered,
    ends_own,
    ends_oth,
    grad_own,
    grad_oth,
    keep_own,
    keep_oth,
    whole,
    rows_ref,
    tiles_ref,
    ids,
    states_own,
    states_oth,
    drive_own,
    drive_oth,
    in_own,
    in_oth,
    out_own,
    out_oth,
    grad_in,
    combined_grad_in,
    normed_in,
    inv_in,
    gain,
    bias,
    skip,
    glu,
    combined,
    phi,
    sig,
    normed,
    low_own,
    low_oth,
    decay_sums,
    grad_out,
    gate_low,
    combined_grad,
    combined_low,
    next_own,
    next_oth,
    next_ends_own,
    next_ends_oth,
    payload,
    sums,
    places,
    small,
    wide,
    adjoint_own,
    adjoint_oth,
):
    info = core_place(row_devices)
    masks = (keep_own, keep_oth)
    adjoint_states(
        1, info, gathered, (ends_own, ends_oth), (grad_own, grad_oth), masks, whole, rows_ref, tiles_ref, ids,
        (states_own, states_oth), (drive_own, drive_oth), (low_own, low_oth), decay_sums,
        (adjoint_own, adjoint_oth), places, small,
    )
    sums[...] = jnp.zeros_like(sums)

    def finish(start, value):
        grad_out[pl.ds(start, ELEMENT_ROWS), :] = value

    norm_backward(
        1, low_own, low_oth, in_own, in_oth, grad_in, combined_grad_in, normed_in, inv_in, gain, skip, sums, wide,
        finish,
    )
    backward_half(
        0, info, grad_out, combined, phi, sig, normed, gain, bias, skip, glu, out_own, out_oth, masks, whole,
        rows_ref, tiles_ref, ids, gate_low, combined_grad, combined_low, next_own, next_oth,
        (next_ends_own, next_ends_oth), payload, sums, wide,
    )


def last_kernel(
    row_devices,
    gathered,
    ends_own,
    ends_oth,
    grad_own,
    grad_oth,
    keep_own,
    keep_oth,
    whole,
    rows_ref,
    tiles_ref,
    ids,
    states_own,
    states_oth,
    drive_own,
    drive_oth,
    mixed_low,
    low_own,
    low_oth,
    decay_sums,
    mine,
    theirs,
    places,
    small,
    adjoint_own,
    adjoint_oth,
):
    info = core_place(row_devices)
    masks = (keep_own, keep_oth)
    adjoint_states(
        0, info, gathered, (ends_own, ends_oth), (grad_own, grad_oth), masks, whole, rows_ref, tiles_ref, ids,
        (states_own, states_oth), (drive_own, drive_oth), (low_own, low_oth), decay_sums,
        (adjoint_own, adjoint_oth), places, small,
    )
    store_columns(mine, 0, dot_tn(mixed_low[...], low_own[...]))
    store_columns(theirs, 0, dot_tn(mixed_low[...], low_oth[...]))


def final_kernel(
    low_own, low_oth, in_own, in_oth, grad_in, combined_grad, normed, inv_scale, gain, skip, out, sums, wide, natural
):
    rows = grad_in.shape[0]
    sums[...] = jnp.zeros_like(sums)

    def finish(start, value):
        store_token_order(natural, start // 8, value, rows // 8)

    norm_backward(
        0, low_own, low_oth, in_own, in_oth, grad_in, combined_grad, normed, inv_scale, gain, skip, sums, wide, finish
    )
    join_columns(out, natural)


def store_columns(out, first, values):
    rows, width = values.shape
    for i in range(width // LANES):
        out[first + i * rows : first + (i + 1) * rows, :] = values[:, i * LANES : (i + 1) * LANES].astype(out.dtype)


def half_rows(core, act_low, gate_low, mine, theirs, first, wide):
    wide[...] = dot_tn(act_low[...], gate_low[...])
    half = wide.shape[0] // 2
    width = wide.shape[1]
    for out, which in ((mine, core), (theirs, 1 - core)):
        rows = pl.ds(pl.multiple_of(which * half, half), half)
        for i in range(width // LANES):
            out[first + i * half : first + (i + 1) * half, :] = wide[rows, i * LANES : (i + 1) * LANES].astype(out.dtype)


def weights_kernel(act_low, gate_low, combined_low, low_own, low_oth, payload_in, mine, theirs, payload, wide):
    payload[...] = payload_in[...]
    core = lax.axis_index("dir")
    store_columns(theirs, 0, dot_tn(low_oth[...], combined_low[...]))
    store_columns(mine, 0, dot_tn(low_own[...], combined_low[...]))
    size = low_own.shape[1] * (combined_low.shape[1] // LANES)
    half_rows(core, act_low, gate_low, mine, theirs, size, wide)


def weights_two_kernel(
    mixed_low, in_low_own, in_low_oth, act_low, gate_low, combined_low, low_own, low_oth, payload_in, mine, theirs,
    payload, wide,
):
    payload[...] = payload_in[...]
    core = lax.axis_index("dir")
    store_columns(theirs, 0, dot_tn(mixed_low[...], in_low_oth[...]))
    store_columns(mine, 0, dot_tn(mixed_low[...], in_low_own[...]))
    size = mixed_low.shape[1] * (in_low_own.shape[1] // LANES)
    store_columns(theirs, size, dot_tn(low_oth[...], combined_low[...]))
    store_columns(mine, size, dot_tn(low_own[...], combined_low[...]))
    size = size + low_own.shape[1] * (combined_low.shape[1] // LANES)
    half_rows(core, act_low, gate_low, mine, theirs, size, wide)


def slot(low_bit, parts):
    return jnp.bitwise_and(jnp.right_shift(lax.axis_index("seq"), low_bit), parts - 1)


def sum_kernel(count, low_bit, *refs):
    sources, outs = refs[:count], refs[count:]
    parts = len(outs)
    rows = outs[0].shape[0]
    mine = slot(low_bit, parts) if parts > 1 else 0
    for k, out in enumerate(outs):
        where = pl.ds(pl.multiple_of(jnp.bitwise_xor(mine, k) * rows, rows), rows) if parts > 1 else slice(None)
        total = sources[0][where, :].astype(f32)
        for source in sources[1:]:
            total = total + source[where, :].astype(f32)
        out[...] = total.astype(out.dtype)


def gather_kernel(low_bit, *refs):
    sources, out = refs[:-1], refs[-1]
    rows = sources[0].shape[0]
    mine = slot(low_bit, len(sources))
    for k, source in enumerate(sources):
        out[pl.ds(pl.multiple_of(jnp.bitwise_xor(mine, k) * rows, rows), rows), :] = source[...]


def join_kernel(mine, theirs, out):
    core = lax.axis_index("dir")
    rows = mine.shape[0]
    out[pl.ds(pl.multiple_of(core * rows, rows), rows), :] = mine[...]
    out[pl.ds(pl.multiple_of((1 - core) * rows, rows), rows), :] = theirs[...]


def matrix_columns(source, first, out):
    rows, width = out.shape
    for i in range(width // LANES):
        out[:, i * LANES : (i + 1) * LANES] = source[first + i * rows : first + (i + 1) * rows, :].astype(f32)


def unpack_kernel(layer_of, olds, gate_rows, *refs):
    refs = list(refs)
    take = lambda n: [refs.pop(0) for _ in range(n)]
    sources = take(4)
    take(olds)
    outs = take(len(layer_of))
    gate_out = take(1 if gate_rows else 0)
    buffers = take(len(layer_of))
    whole, sems = refs
    gather_kernel(0, *sources, whole)
    first = 0
    copies = []
    for i, layer in enumerate(layer_of):
        buffer, out = buffers[i], outs[i]
        matrix_columns(whole, first, buffer)
        first = first + buffer.shape[0] * (buffer.shape[1] // LANES)
        copies.append(pltpu.make_async_copy(buffer, out.at[layer, 0], sems.at[i]))
        copies[-1].start()
    for out in gate_out:
        out[...] = whole[first : first + gate_rows, :]
    for copy in copies:
        copy.wait()


def gate_kernel(mine_early, theirs_early, mine_middle, theirs_middle, out):
    core = lax.axis_index("dir")
    half = out.shape[1] // 2
    width = out.shape[2]
    for layer, mine, theirs in ((1, mine_early, theirs_early), (0, mine_middle, theirs_middle)):
        for source, which in ((mine, core), (theirs, 1 - core)):
            rows = pl.ds(pl.multiple_of(which * half, half), half)
            for i in range(width // LANES):
                out[layer, rows, i * LANES : (i + 1) * LANES] = source[i * half : (i + 1) * half, :].astype(f32)


def small_pack_kernel(sums_turn, sums_back, sums_last, decay_late, decay_early, send, own):
    per = sums_turn.shape[1] // LANES
    thirds = decay_late.shape[1] // LANES
    send[...] = jnp.zeros_like(send)
    own[...] = jnp.zeros_like(own)
    kinds = (
        ((sums_last, 2), (sums_back, 2)),
        ((sums_last, 3), (sums_back, 3)),
        ((sums_back, 1), (sums_turn, 1)),
        ((sums_back, 0), (sums_turn, 0)),
    )
    at = 0
    for kind in kinds:
        for source, row in kind:
            for i in range(per):
                value = source[row : row + 1, i * LANES : (i + 1) * LANES]
                send[at : at + 1, :] = value
                own[at : at + 1, :] = value
                at += 1
    for source in (decay_late, decay_early):
        for term in range(3):
            for i in range(thirds):
                lanes = slice(i * LANES, (i + 1) * LANES)
                own[at : at + 1, :] = source[term : term + 1, lanes]
                send[at : at + 1, :] = source[3 + term : 4 + term, lanes]
                at += 1


def small_kernel(tokens_rows, own, got, table, out):
    layers, _, states = table.shape
    thirds = states // LANES
    out[...] = jnp.zeros_like(out)
    out[0:tokens_rows, :] = own[0:tokens_rows, :] + got[0:tokens_rows, :]
    for layer in range(layers):
        for i in range(thirds):
            lanes = slice(i * LANES, (i + 1) * LANES)
            base = tokens_rows + (layer * 3) * thirds + i
            term_re, term_im, term_scale = (
                own[base + t * thirds : base + t * thirds + 1, :] + got[base + t * thirds : base + t * thirds + 1, :]
                for t in range(3)
            )
            re, im, scale, damping, step_size, rotation, square = (
                table[layer, t : t + 1, lanes] for t in range(7)
            )
            grad_re = (term_re * re - term_im * im) / square
            grad_im = (term_re * im + term_im * re) / square
            grad_scale = term_scale / scale
            grad_damping = grad_scale * square / scale - (grad_re * re + grad_im * im)
            grad_rotation = grad_im * re - grad_re * im
            log_rate = grad_damping * damping
            at = tokens_rows + layer * thirds + i
            out[at : at + 1, :] = log_rate
            at = tokens_rows + layers * thirds + (layer * 2) * thirds + i
            out[at : at + 1, :] = grad_rotation * step_size
            out[at + thirds : at + thirds + 1, :] = log_rate + grad_rotation * rotation


def add_kernel(*refs):
    total = refs[0][...]
    for source in refs[1:-1]:
        total = total + source[...]
    refs[-1][...] = total


def small_out_kernel(*refs):
    sources, (gain, bias, rate, turn, skip, gate) = refs[:-6], refs[-6:]
    layers, width = gain.shape
    per = width // LANES
    thirds = rate.shape[1] // LANES
    total = sources[0][...]
    for source in sources[1:]:
        total = total + source[...]
    at = 0
    for out in (gain, bias, skip, gate):
        for layer in range(layers):
            for i in range(per):
                out[layer : layer + 1, i * LANES : (i + 1) * LANES] = total[at : at + 1]
                at += 1
    for layer in range(layers):
        for i in range(thirds):
            rate[layer : layer + 1, i * LANES : (i + 1) * LANES] = total[at : at + 1]
            at += 1
    for row in range(2 * layers):
        for i in range(thirds):
            turn[row : row + 1, i * LANES : (i + 1) * LANES] = total[at : at + 1]
            at += 1


class Order:
    def __init__(self):
        self.tile = None

    def run(self, kernel, outs, operands, scratch=(), flops=0, name=None, spare=8, after=(), free_outs=0, alias=None,
            semaphores=0):
        whole = pl.BlockSpec(memory_space=pltpu.VMEM)
        free = pl.BlockSpec(memory_space=pl.ANY)
        waits = list(after) + ([] if self.tile is None else [self.tile])
        inputs, results = len(operands), len(outs)
        skipped = len(waits)

        def body(*refs):
            token = refs[skipped + inputs]
            token[...] = jnp.zeros_like(token)
            kernel(*refs[skipped : skipped + inputs], *refs[skipped + inputs + 1 :])

        shapes = [jax.ShapeDtypeStruct((8, LANES), f32)]
        shapes += [jax.ShapeDtypeStruct(shape, dtype) for shape, dtype in outs]
        moved = sum(value.size * value.dtype.itemsize for value in operands)
        held = sum(jnp.dtype(dtype).itemsize * functools.reduce(lambda a, b: a * b, shape) for shape, dtype in scratch)
        specs = [free] * skipped + [whole] * inputs
        aliases = {}
        if alias is not None:
            for operand, out in alias.items():
                specs[skipped + operand] = free
                aliases[skipped + operand] = out + 1
        extra = [pltpu.SemaphoreType.DMA((semaphores,))] if semaphores else []
        results = pl.pallas_call(
            body,
            out_shape=shapes,
            in_specs=specs,
            out_specs=[whole] + [free] * free_outs + [whole] * (results - free_outs),
            scratch_shapes=[pltpu.VMEM(shape, dtype) for shape, dtype in scratch] + extra,
            input_output_aliases=aliases,
            compiler_params=pltpu.CompilerParams(vmem_limit_bytes=held + spare * 2**20),
            cost_estimate=pl.CostEstimate(flops=int(flops), bytes_accessed=int(moved), transcendentals=0),
            name=name,
        )(*waits, *operands)
        self.tile = results[0]
        return results[1:]


def swap(value):
    return lax.ppermute(value, "dir", [(0, 1), (1, 0)])


def across(value, bits):
    count = lax.axis_size("seq")
    return lax.ppermute(value, "seq", [(i, i ^ bits) for i in range(count)])


def beyond(value):
    bit = 4
    while (1 << bit) < lax.axis_size("seq"):
        value = (value.astype(f32) + across(value, 1 << bit).astype(f32)).astype(value.dtype)
        bit += 1
    return value


def exchanged(payload, row_devices):
    count = lax.axis_size("seq")
    group = 2 * row_devices
    groups = None
    if count != row_devices:
        groups = [list(range(i, i + group)) for i in range(0, 2 * count, group)]
    copies = jnp.broadcast_to(payload[None], (group,) + payload.shape)
    return lax.all_to_all(copies, ("seq", "dir"), 0, 0, tiled=True, axis_index_groups=groups)


class Pack:
    def __init__(self, order, name, mine, theirs):
        self.order, self.name = order, name
        self.mine, self.got = mine, swap(theirs)
        self.rows = mine.shape[0]

    def sum(self, sources, parts, low_bit, step, after=()):
        rows = sources[0].shape[0] // parts
        return self.order.run(
            functools.partial(sum_kernel, len(sources), low_bit), [((rows, LANES), bf16)] * parts, sources,
            name=f"{self.name}_{step}", after=after,
        )

    def first(self, after=()):
        self.parts = self.sum([self.mine, self.got], 4, 0, "sum_cores", after)
        self.parts = [self.parts[0]] + [across(self.parts[k], k) for k in (1, 2, 3)]

    def second(self, after=()):
        self.parts = self.sum(self.parts, 4, 2, "sum_plane", after)
        self.parts = [self.parts[0]] + [across(self.parts[k], k << 2) for k in (1, 2, 3)]

    def third(self, after=()):
        (share,) = self.sum(self.parts, 1, 0, "sum_planes", after)
        share = beyond(share)
        self.parts = [share] + [across(share, k << 2) for k in (1, 2, 3)]

    def fourth(self, after=()):
        (quarter,) = self.order.run(
            functools.partial(gather_kernel, 2), [((self.rows // 4, LANES), bf16)], self.parts,
            name=f"{self.name}_gather", after=after,
        )
        self.parts = [quarter] + [across(quarter, k) for k in (1, 2, 3)]


def body(
    tokens,
    segment_ids,
    norm_gain,
    norm_bias,
    input_matrix,
    output_matrix,
    rate_params,
    turn_params,
    skip_weight,
    glu_weight,
    glu_bias,
    cotangent,
):
    chip_rows, width = tokens.shape
    rows = chip_rows // 2
    layers = rate_params.shape[0]
    states = rate_params.shape[2]
    row_devices = LENGTH // chip_rows
    order = Order()
    here = functools.partial

    in_own, out_own = input_matrix, output_matrix
    in_oth = swap(input_matrix)
    rate_oth, turn_oth = swap(rate_params), swap(turn_params)
    out_oth = swap(output_matrix)
    segments = segment_ids.reshape(chip_rows // LANES, LANES)

    full = ((rows, width), f32)
    full_low = ((rows, width), bf16)
    columns = ((width // LANES, rows, LANES), f32)
    wide = ((rows, 2 * states), f32)
    wide_low = ((rows, 2 * states), bf16)
    ends = ((8, 2 * states), f32)
    payload_shape = ((16, LANES), f32)
    narrow = ((rows, LANES), f32)
    tile = ((8, LANES), f32)
    sums_shape = ((8, width), f32)
    decay_shape = ((8, states), f32)
    table_shape = ((layers, 16, states), f32)
    places = ((8, 2 * states), f32)
    one = 2.0 * rows * width * 2 * states
    gate = 2.0 * rows * width * width
    scan = 1e9

    x0, normed0, inv0, mixed0, drive_own0, keep_own, keep_oth, whole, table, ids = order.run(
        here(open_kernel, row_devices),
        [full, full, narrow, full_low, wide, narrow, narrow, ((2, 8, LANES), f32), table_shape, tile],
        [tokens, segments, norm_gain, norm_bias, rate_params, turn_params, in_own],
        [columns, tile],
        flops=one + scan,
        name="open_norm",
    )
    drive_oth0, ends_own, ends_oth, payload, table, tiles = order.run(
        here(open_second_kernel, row_devices),
        [wide, ends, ends, payload_shape, table_shape, ((layers, 16, LANES), f32)],
        [mixed0, in_oth, rate_oth, turn_oth, table, drive_own0, keep_own, keep_oth, whole, ids],
        flops=one + scan,
        name="open_scan",
    )
    gathered = exchanged(payload, row_devices)
    (
        low_own0, low_oth0, combined0, phi0, sig0, act_low0, x1, normed1, inv1, mixed1, drive_own1, drive_oth1,
        ends_own, ends_oth, payload,
    ) = order.run(
        here(mid_kernel, row_devices),
        [wide_low, wide_low, full, full, full, full_low, full, full, narrow, full_low, wide, wide, ends, ends,
         payload_shape],
        [gathered, ends_own, ends_oth, drive_own0, drive_oth0, keep_own, keep_oth, whole, table, tiles,
         ids, out_own, out_oth, x0, normed0, norm_gain, norm_bias, skip_weight, glu_weight, glu_bias, in_own, in_oth],
        [places, tile, full, wide, wide],
        flops=4 * one + gate + 3 * scan,
        name="mid",
    )
    gathered = exchanged(payload, row_devices)
    (
        low_own1, low_oth1, half_out, grad1, act_low1, gate_low1, combined_grad1, combined_low1, grad_own1, grad_oth1,
        ends_own, ends_oth, payload, sums_turn,
    ) = order.run(
        here(turn_kernel, row_devices),
        [wide_low, wide_low, full, full, full_low, full_low, full, full_low, wide, wide, ends, ends, payload_shape,
         sums_shape],
        [gathered, ends_own, ends_oth, drive_own1, drive_oth1, keep_own, keep_oth, whole, table, tiles,
         ids, out_own, out_oth, x1, normed1, norm_gain, norm_bias, skip_weight, glu_weight, glu_bias, cotangent],
        [places, tile, full, full, full, full, columns, columns, wide, wide],
        flops=4 * one + 2 * gate + 4 * scan,
        name="turn",
    )
    in_size = width * (2 * states // LANES)
    out_size = 2 * states * (width // LANES)
    glu_size = width // 2 * (width // LANES)
    pack = ((out_size + glu_size, LANES), bf16)
    mine, theirs, payload = order.run(
        weights_kernel,
        [pack, pack, payload_shape],
        [act_low1, gate_low1, combined_low1, low_own1, low_oth1, payload],
        [((width, width), f32)],
        flops=2 * one + gate,
        name="weights_early",
    )
    gathered = exchanged(payload, row_devices)
    early = Pack(order, "early", mine, theirs)
    early.first(after=[gathered])
    (
        in_low_own1, in_low_oth1, decay_sums1, grad0, gate_low0, combined_grad0, combined_low0, grad_own0, grad_oth0,
        ends_own, ends_oth, payload, sums_back,
    ) = order.run(
        here(back_kernel, row_devices),
        [wide_low, wide_low, decay_shape, full, full_low, full, full_low, wide, wide, ends, ends, payload_shape,
         sums_shape],
        [gathered, ends_own, ends_oth, grad_own1, grad_oth1, keep_own, keep_oth, whole, table, tiles,
         ids, low_own1, low_oth1, drive_own1, drive_oth1, in_own, in_oth, out_own, out_oth, grad1, combined_grad1,
         normed1, inv1, norm_gain, norm_bias, skip_weight, glu_weight, combined0, phi0, sig0, normed0],
        [places, tile, full, wide, wide],
        flops=4 * one + gate + 4 * scan,
        name="back",
    )
    early.second()
    pack = ((in_size + out_size + glu_size, LANES), bf16)
    mine, theirs, payload = order.run(
        weights_two_kernel,
        [pack, pack, payload_shape],
        [mixed1, in_low_own1, in_low_oth1, act_low0, gate_low0, combined_low0, low_own0, low_oth0, payload],
        [((width, width), f32)],
        flops=4 * one + gate,
        name="weights_middle",
    )
    gathered = exchanged(payload, row_devices)
    middle = Pack(order, "middle", mine, theirs)
    middle.first(after=[gathered])
    early.third()
    pack = ((in_size, LANES), bf16)
    in_low_own0, in_low_oth0, decay_sums0, mine, theirs = order.run(
        here(last_kernel, row_devices),
        [wide_low, wide_low, decay_shape, pack, pack],
        [gathered, ends_own, ends_oth, grad_own0, grad_oth0, keep_own, keep_oth, whole, table, tiles,
         ids, low_own0, low_oth0, drive_own0, drive_oth0, mixed0],
        [places, tile, wide, wide],
        flops=2 * one + 2 * scan,
        name="last_scan",
    )
    late = Pack(order, "late", mine, theirs)
    early.fourth()
    half_grad, sums_last = order.run(
        final_kernel,
        [full, sums_shape],
        [in_low_own0, in_low_oth0, in_own, in_oth, grad0, combined_grad0, normed0, inv0, norm_gain, skip_weight],
        [full, columns],
        flops=2 * one + scan,
        name="final_norm",
    )
    late.first()
    token_rows = 4 * layers * (width // LANES)
    small_rows = -(-(token_rows + 3 * layers * (states // LANES)) // 8) * 8
    small = ((small_rows, LANES), f32)
    send, own = order.run(
        small_pack_kernel, [small, small], [sums_turn, sums_back, sums_last, decay_sums0, decay_sums1],
        name="small_pack",
    )
    got = swap(send)
    whole_rows = ((chip_rows, width), f32)
    (block_output,) = order.run(join_kernel, [whole_rows], [half_out, swap(half_out)], name="join_out")
    (tiny,) = order.run(here(small_kernel, token_rows), [small], [own, got, table], name="small_map")
    tiny = [tiny] + [across(tiny, k) for k in (1, 2, 3)]
    middle.second()
    (tokens_grad,) = order.run(join_kernel, [whole_rows], [half_grad, swap(half_grad)], name="join_grad")
    (tiny,) = order.run(add_kernel, [small], tiny, name="small_plane")
    tiny = beyond(tiny)
    tiny = [tiny] + [across(tiny, k << 2) for k in (1, 2, 3)]
    late.second()
    middle.third()
    gain_grad, bias_grad, rate_grad, turn_grad, skip_grad, gate_grad = order.run(
        small_out_kernel,
        [((layers, width), f32), ((layers, width), f32), ((layers, states), f32), ((2 * layers, states), f32),
         ((layers, width), f32), ((layers, width), f32)],
        tiny,
        name="small_out",
    )

    def unpack(pack, shapes, layer_of, old, gate_rows, name):
        held = [value for value in old if value is not None]
        alias = {4 + i: j for i, j in enumerate(j for j, value in enumerate(old) if value is not None)}
        gate_out = [((gate_rows, LANES), bf16)] if gate_rows else []
        return order.run(
            here(unpack_kernel, layer_of, len(held), gate_rows),
            [(shape, f32) for shape in shapes] + gate_out,
            list(pack.parts) + held,
            [(shape[2:], f32) for shape in shapes] + [((pack.rows, LANES), bf16)],
            name=name,
            free_outs=len(shapes),
            alias=alias,
            semaphores=len(shapes),
        )

    in_shape, out_shape = input_matrix.shape, output_matrix.shape
    out_all, gate_early = unpack(early, [out_shape], (1,), [None], glu_size, "unpack_early")
    got_early = swap(gate_early)
    late.third()
    middle.fourth()
    late.fourth()
    in_all, out_all, gate_middle = unpack(
        middle, [in_shape, out_shape], (1, 0), [None, out_all], glu_size, "unpack_middle"
    )
    got_middle = swap(gate_middle)
    (in_all,) = unpack(late, [in_shape], (0,), [in_all], 0, "unpack_late")
    (glu_all,) = order.run(
        gate_kernel, [(glu_weight.shape, f32)], [gate_early, got_early, gate_middle, got_middle], name="unpack_gate"
    )
    return (
        block_output,
        tokens_grad,
        gain_grad,
        bias_grad,
        in_all,
        out_all,
        rate_grad.reshape(rate_params.shape),
        turn_grad.reshape(turn_params.shape),
        skip_grad,
        glu_all,
        gate_grad,
    )


def solution(mesh):
    return jax.shard_map(
        body,
        mesh=mesh,
        in_specs=(
            P("seq", None),
            P("seq"),
            P(),
            P(),
            P(None, "dir", None, None),
            P(None, "dir", None, None),
            P(None, "dir", None),
            P(None, "dir", None, None),
            P(),
            P(),
            P(),
            P("seq", None),
        ),
        out_specs=(
            P("seq", None),
            P("seq", None),
            P(),
            P(),
            P(None, "dir", None, None),
            P(None, "dir", None, None),
            P(None, "dir", None),
            P(None, "dir", None, None),
            P(),
            P(),
            P(),
        ),
        check_vma=False,
    )
```

```python
import functools

import jax
import jax.numpy as jnp
from jax import lax
from jax.experimental import pallas as pl
from jax.experimental.pallas import tpu as pltpu
from jax.sharding import PartitionSpec as P

LENGTH = 16384
LONGEST_RUN = 8192

eps = 1e-05
inv_root_two = 0.7071067811865476
inv_root_two_pi = 0.3989422804014327

f32 = jnp.float32
bf16 = jnp.bfloat16


LANES = 128
ELEMENT_ROWS = 32
UNROLL = 4
RELAY = 50


def core_place(row_devices):
    core = lax.axis_index("dir")
    return core, lax.rem(lax.axis_index("seq"), row_devices) * 2 + core


def dot(a, b):
    return jnp.dot(a, b, preferred_element_type=f32)


def dot_nt(a, b):
    return lax.dot_general(a, b, (((1,), (1,)), ((), ())), preferred_element_type=f32)


def dot_tn(a, b):
    return lax.dot_general(a, b, (((0,), (0,)), ((), ())), preferred_element_type=f32)


def squared(re, im, times):
    for _ in range(times):
        re, im = re * re - im * im, 2.0 * re * im
    return re, im


def over_blocks(rows, step, init=()):
    def one(i, carry):
        return step(pl.multiple_of(i * ELEMENT_ROWS, ELEMENT_ROWS), carry)

    return lax.fori_loop(0, rows // ELEMENT_ROWS, one, init)


def fold(values):
    total = values[0:8]
    for start in range(8, values.shape[0], 8):
        total = total + values[start : start + 8]
    return total


class Lanes:
    def __init__(self, rows_ref, tiles_ref, layer, adjoint, spans, rows):
        states = rows_ref.shape[2]
        self.states = states
        self.rows_ref, self.layer = rows_ref, layer
        flip = -1.0 if adjoint else 1.0
        self.step = []
        self.run = []
        self.block = []
        for side in range(2):
            row = 8 * side
            re = rows_ref[layer, row : row + 1, :]
            im = rows_ref[layer, row + 1 : row + 2, :] * flip
            self.step.append((jnp.broadcast_to(re, (8, states)), jnp.broadcast_to(im, (8, states))))
            self.run.append(squared(re, im, (spans - 1).bit_length()))
            thirds = states // LANES
            tile_re = tiles_ref[layer, 8 * side : 8 * side + thirds, :]
            tile_im = tiles_ref[layer, 8 * side + thirds : 8 * side + 2 * thirds, :] * flip
            self.block.append(squared(tile_re, tile_im, (rows - 1).bit_length()))

    def scaling(self, side):
        row = self.rows_ref[self.layer, 8 * side + 2 : 8 * side + 3, :]
        return jnp.concatenate([row, row], 1)


def sweep(first_forward, drives, masks, lanes, init, visit=None, totals=()):
    states = lanes.states
    span = drives[0].shape[0] // 8

    def step(i, carry):
        values, sums = carry
        up = pl.multiple_of(i * 8, 8)
        down = pl.multiple_of((span - 1 - i) * 8, 8)
        places = (jnp.where(first_forward, up, down), jnp.where(first_forward, down, up))
        new = []
        for side in range(2):
            rows = pl.ds(pl.multiple_of(places[side], 8), 8)
            keep = masks[side][rows, :]
            keep = jnp.concatenate([keep] * (states // LANES), 1)
            step_re, step_im = lanes.step[side]
            step_re, step_im = step_re * keep, step_im * keep
            re, im = values[side]
            drive_re = drives[side][rows, :states]
            drive_im = drives[side][rows, states:]
            re, im = (
                step_re * re - step_im * im + drive_re,
                step_re * im + step_im * re + drive_im,
            )
            new.append((re, im))
            if visit is not None:
                sums = visit(side, rows, re, im, sums)
        return tuple(new), sums

    return lax.fori_loop(0, span, step, (init, totals), unroll=UNROLL)


def run_chain(first_up, lanes, side, ends, whole, start, places):
    states = lanes.states
    power_re, power_im = lanes.run[side]
    re, im = start
    for i in range(8):
        s = jnp.where(first_up, i, 7 - i)
        row = pl.ds(s, 1)
        if places is not None:
            places[row, :states] = re
            places[row, states:] = im
        passes = whole[row, :]
        passes = jnp.concatenate([passes] * (states // LANES), 1)
        pass_re, pass_im = power_re * passes, power_im * passes
        end_re, end_im = ends[row, :states], ends[row, states:]
        re, im = (end_re + pass_re * re - pass_im * im, end_im + pass_re * im + pass_im * re)
    return re, im


def first_pass(running_up, drives, masks, wholes, lanes, ids_ref, ends, payload):
    states = lanes.states
    thirds = states // LANES
    nothing = jnp.zeros((8, states), f32)
    zero = (nothing, nothing)
    values, _ = sweep(running_up, drives, masks, lanes, (zero, zero))
    one = jnp.zeros((16, LANES), f32)
    payload[0] = one
    for side in range(2):
        ends[side][:, :states] = values[side][0]
        ends[side][:, states:] = values[side][1]
        upward = running_up if side == 0 else jnp.logical_not(running_up)
        start = jnp.zeros((1, states), f32)
        re, im = run_chain(upward, lanes, side, ends[side], wholes[side], (start, start), None)
        base = jnp.where(upward, 0, 8)
        for i in range(thirds):
            payload[0, pl.ds(base + i, 1), :] = re[:, LANES * i : LANES * (i + 1)]
            payload[0, pl.ds(base + thirds + i, 1), :] = im[:, LANES * i : LANES * (i + 1)]
        payload[0, 8 * side + 6 : 8 * side + 8, :] = ids_ref[0:2, :]
    one = payload[0]
    for i in range(1, payload.shape[0]):
        payload[i] = one


def entering(upward, place, lanes, side, gathered, ids_ref, small):
    states = lanes.states
    thirds = states // LANES
    count = gathered.shape[0]
    rows = lanes.token_rows
    block_re, block_im = lanes.block[side]
    re = jnp.zeros((thirds, LANES), f32)
    im = jnp.zeros((thirds, LANES), f32)
    base = jnp.where(upward, 0, 8)
    key = jnp.where(upward, ids_ref[0:1, :], ids_ref[1:2, :])
    for distance in range(min(count - 1, LONGEST_RUN // rows), 0, -1):
        source = jnp.where(upward, place - distance, place + distance)
        inside = jnp.logical_and(source >= 0, source < count)
        source = jnp.clip(source, 0, count - 1)
        sent_re = gathered[source, pl.ds(base, thirds), :]
        sent_im = gathered[source, pl.ds(base + thirds, thirds), :]
        sent_key = gathered[source, pl.ds(jnp.where(upward, base + 7, base + 6), 1), :]
        joined = jnp.where(jnp.logical_and(sent_key == key, inside), 1.0, 0.0)
        re, im = (
            joined * sent_re + block_re * re - block_im * im,
            joined * sent_im + block_re * im + block_im * re,
        )
    small[0:thirds, :] = re
    small[thirds : 2 * thirds, :] = im
    wide_re = jnp.concatenate([small[i : i + 1, :] for i in range(thirds)], 1)
    wide_im = jnp.concatenate([small[thirds + i : thirds + i + 1, :] for i in range(thirds)], 1)
    return wide_re, wide_im


def second_starts(running_up, place, lanes, gathered, ids_ref, ends, wholes, places, small):
    init = []
    states = lanes.states
    for side in range(2):
        upward = running_up if side == 0 else jnp.logical_not(running_up)
        start = entering(upward, place, lanes, side, gathered, ids_ref, small)
        run_chain(upward, lanes, side, ends[side], wholes[side], start, places)
        init.append((places[:, :states], places[:, states:]))
    return tuple(init)


def make_lanes(rows_ref, tiles_ref, layer, adjoint, token_rows):
    lanes = Lanes(rows_ref, tiles_ref, layer, adjoint, token_rows // 8, token_rows)
    lanes.token_rows = token_rows
    return lanes


def standardise(x):
    width = x.shape[1]
    average = jnp.sum(x, 1, keepdims=True) * (1.0 / width)
    centred = x - average
    inv_scale = lax.rsqrt(jnp.sum(centred * centred, 1, keepdims=True) * (1.0 / width) + eps)
    return centred * inv_scale, inv_scale


def fill_columns(columns, values):
    for i in range(columns.shape[0]):
        columns[i] = values[:, i * LANES : (i + 1) * LANES].astype(columns.dtype)


def tile_order(columns, first, count, span):
    tiles = [
        jnp.concatenate([columns[i, pl.ds(first + j, 8, stride=span), :] for i in range(columns.shape[0])], 1)
        for j in range(count)
    ]
    return jnp.concatenate(tiles, 0)


def store_token_order(columns, first, values, span):
    for j in range(values.shape[0] // 8):
        for i in range(columns.shape[0]):
            columns[i, pl.ds(first + j, 8, stride=span), :] = values[8 * j : 8 * j + 8, i * LANES : (i + 1) * LANES]


def join_columns(out, columns):
    for i in range(columns.shape[0]):
        out[:, i * LANES : (i + 1) * LANES] = columns[i]


def one_minus_exp(x):
    series = jnp.ones_like(x)
    for term in range(12, 1, -1):
        series = 1.0 - x * (1.0 / term) * series
    return jnp.where(x < 0.5, x * series, 1.0 - jnp.exp(-x))


def table_rows(table, layer, base, rate, turn):
    frequency = turn[layer, 0, 0:1, :]
    log_step = turn[layer, 0, 1:2, :]
    step_size = jnp.exp(log_step)
    damping = jnp.exp(rate[layer, 0:1, :] + log_step)
    magnitude = jnp.exp(-damping)
    rotation = frequency * step_size
    square = magnitude * magnitude
    rows = (
        magnitude * jnp.cos(rotation), magnitude * jnp.sin(rotation), jnp.sqrt(one_minus_exp(2.0 * damping)), damping,
        step_size, rotation, square,
    )
    for i, row in enumerate(rows):
        table[layer, base + i : base + i + 1, :] = row


def open_kernel(
    row_devices,
    tokens,
    segments,
    gain,
    bias,
    rate,
    turn,
    in_own,
    x_out,
    normed_out,
    inv_out,
    mixed_out,
    drive_out,
    keep_own,
    keep_oth,
    whole_out,
    table,
    ids,
    natural,
    rows8,
):
    core, _ = core_place(row_devices)
    rows = x_out.shape[0]
    span = rows // 8
    base = pl.multiple_of(core * rows, rows)
    fill_columns(natural, tokens[pl.ds(base, rows), :].astype(f32))
    table[...] = jnp.zeros_like(table)
    for layer in range(table.shape[0]):
        table_rows(table, layer, 0, rate, turn)

    number = segments[...].astype(f32)
    count = number.shape[0]
    lane = lax.broadcasted_iota(jnp.int32, number.shape, 1)
    row = lax.broadcasted_iota(jnp.int32, number.shape, 0)
    back = pltpu.roll(number, 1, 1)
    back = jnp.where(lane == 0, pltpu.roll(back, 1, 0), back)
    ahead = pltpu.roll(number, LANES - 1, 1)
    ahead = jnp.where(lane == LANES - 1, pltpu.roll(ahead, count - 1, 0), ahead)
    edge_first = jnp.logical_and(lane == 0, row == 0)
    edge_last = jnp.logical_and(lane == LANES - 1, row == count - 1)
    up_keep = jnp.where(jnp.logical_or(number == back, edge_first), 1.0, 0.0)
    down_keep = jnp.where(jnp.logical_or(number == ahead, edge_last), 1.0, 0.0)
    per = LANES // span
    used = 8 // per
    for side, out in ((0, keep_own), (1, keep_oth)):
        rows8[0:count, :] = jnp.where(core == side, up_keep, down_keep)
        half = rows8[pl.ds(core * used, used), :]
        runs = jnp.concatenate([half[s // per : s // per + 1] for s in range(8)], 0)
        place = lax.broadcasted_iota(jnp.int32, (8, LANES), 1)
        sub = lax.broadcasted_iota(jnp.int32, (8, LANES), 0)
        first = lax.rem(sub, per) * span
        inside = jnp.logical_and(place >= first, place < first + span)
        least = jnp.min(jnp.where(inside, runs, 1.0), 1, keepdims=True)
        whole_out[side] = jnp.broadcast_to(least, (8, LANES))
        step = lax.broadcasted_iota(jnp.int32, (span, 8, LANES), 0)
        spread = jnp.where(step == (place - first)[None], runs[None], 0.0)
        spread = spread.reshape(span * 8, LANES).astype(bf16)
        out[...] = dot(spread, jnp.ones((LANES, LANES), bf16))
    rows8[0:count, :] = number
    first_row = rows8[pl.ds(core * used, 1), :]
    last_row = rows8[pl.ds(core * used + used - 1, 1), :]
    ids[...] = jnp.zeros_like(ids)
    ids[0:1, :] = jnp.broadcast_to(first_row[:, 0:1], (1, LANES))
    ids[1:2, :] = jnp.broadcast_to(last_row[:, LANES - 1 : LANES], (1, LANES))

    def element(start, carry):
        x = tile_order(natural, start // 8, ELEMENT_ROWS // 8, span)
        normed, inv_scale = standardise(x)
        block = pl.ds(start, ELEMENT_ROWS)
        x_out[block, :] = x
        normed_out[block, :] = normed
        inv_out[block, :] = jnp.broadcast_to(inv_scale, (ELEMENT_ROWS, LANES))
        mixed_out[block, :] = (normed * gain[0:1, :] + bias[0:1, :]).astype(bf16)
        return carry

    over_blocks(rows, element)
    scale = table[0, 2:3, :]
    drive_out[...] = dot(mixed_out[...], in_own[0, 0]) * jnp.concatenate([scale, scale], 1)


def open_second_kernel(
    row_devices,
    mixed_low,
    in_oth,
    rate,
    turn,
    table_in,
    drive_own,
    keep_own,
    keep_oth,
    whole,
    ids,
    drive_oth,
    ends_own,
    ends_oth,
    payload,
    table,
    tiles,
):
    core, _ = core_place(row_devices)
    table[...] = table_in[...]
    tiles[...] = jnp.zeros_like(tiles)
    thirds = table.shape[2] // LANES
    for layer in range(table.shape[0]):
        table_rows(table, layer, 8, rate, turn)
        for side in range(2):
            for part in range(2):
                for i in range(thirds):
                    at = 8 * side + part * thirds + i
                    tiles[layer, at : at + 1, :] = table[
                        layer, 8 * side + part : 8 * side + part + 1, i * LANES : (i + 1) * LANES
                    ]
    scale = table[0, 10:11, :]
    drive_oth[...] = dot(mixed_low[...], in_oth[0, 0]) * jnp.concatenate([scale, scale], 1)
    rows = drive_own.shape[0]
    lanes = make_lanes(table, tiles, 0, False, rows)
    first_pass(
        core == 0,
        (drive_own, drive_oth),
        (keep_own, keep_oth),
        (whole.at[0], whole.at[1]),
        lanes,
        ids,
        (ends_own, ends_oth),
        payload,
    )


def forward_states(layer, info, gathered, ends, drives, masks, whole, rows_ref, tiles_ref, ids, states, lows, places, small):
    rows = drives[0].shape[0]
    lanes = make_lanes(rows_ref, tiles_ref, layer, False, rows)
    core, place = info
    running_up = core == 0
    init = second_starts(
        running_up, place, lanes, gathered, ids, ends, (whole.at[0], whole.at[1]), places, small
    )
    width = lanes.states

    def visit(side, where, re, im, sums):
        states[side][where, :width] = re
        states[side][where, width:] = im
        return sums

    sweep(running_up, drives, masks, lanes, init, visit)
    for side in range(2):
        lows[side][...] = states[side][...].astype(bf16)


def mid_kernel(
    row_devices,
    gathered,
    ends_own,
    ends_oth,
    drive_own,
    drive_oth,
    keep_own,
    keep_oth,
    whole,
    rows_ref,
    tiles_ref,
    ids,
    out_own,
    out_oth,
    x_in,
    normed,
    gain,
    bias,
    skip,
    glu,
    glu_bias,
    in_own,
    in_oth,
    low_own,
    low_oth,
    combined_out,
    phi_out,
    sig_out,
    act_low,
    x_out,
    normed_out,
    inv_out,
    mixed_out,
    next_own,
    next_oth,
    next_ends_own,
    next_ends_oth,
    payload,
    places,
    small,
    wide,
    states_own,
    states_oth,
):
    info = core_place(row_devices)
    rows = x_in.shape[0]
    masks = (keep_own, keep_oth)
    forward_states(
        0, info, gathered, (ends_own, ends_oth), (drive_own, drive_oth), masks, whole, rows_ref, tiles_ref,
        ids, (states_own, states_oth), (low_own, low_oth), places, small,
    )
    wide[...] = dot(low_own[...], out_own[0, 0]) + dot(low_oth[...], out_oth[0, 0])

    def element(start, carry):
        block = pl.ds(start, ELEMENT_ROWS)
        mixed = normed[block, :] * gain[0:1, :] + bias[0:1, :]
        combined = wide[block, :] + skip[0:1, :] * mixed
        phi = 0.5 * (1.0 + lax.erf(combined * inv_root_two))
        combined_out[block, :] = combined
        phi_out[block, :] = phi
        act_low[block, :] = (combined * phi).astype(bf16)
        return carry

    over_blocks(rows, element)
    wide[...] = dot(act_low[...], glu[0])

    def element_two(start, carry):
        block = pl.ds(start, ELEMENT_ROWS)
        sig = jax.nn.sigmoid(wide[block, :] + glu_bias[0:1, :])
        sig_out[block, :] = sig
        x = x_in[block, :] + combined_out[block, :] * phi_out[block, :] * sig
        x_out[block, :] = x
        after, inv_scale = standardise(x)
        normed_out[block, :] = after
        inv_out[block, :] = jnp.broadcast_to(inv_scale, (ELEMENT_ROWS, LANES))
        mixed_out[block, :] = (after * gain[1:2, :] + bias[1:2, :]).astype(bf16)
        return carry

    over_blocks(rows, element_two)
    for side, (matrix, out) in enumerate(((in_own, next_own), (in_oth, next_oth))):
        scale = rows_ref[1, 8 * side + 2 : 8 * side + 3, :]
        out[...] = dot(mixed_out[...], matrix[1, 0]) * jnp.concatenate([scale, scale], 1)
    lanes = make_lanes(rows_ref, tiles_ref, 1, False, rows)
    first_pass(
        info[0] == 0,
        (next_own, next_oth),
        masks,
        (whole.at[0], whole.at[1]),
        lanes,
        ids,
        (next_ends_own, next_ends_oth),
        payload,
    )


def backward_half(
    layer, info, grad, combined, phi, sig, normed, gain, bias, skip, glu, out_own, out_oth, masks, whole,
    rows_ref, tiles_ref, ids, gate_low, combined_grad, combined_low, grad_own, grad_oth, ends, payload, sums, wide,
):
    rows = grad.shape[0]
    width = grad.shape[1]
    zero = jnp.zeros((8, width), f32)

    def element(start, carry):
        block = pl.ds(start, ELEMENT_ROWS)
        gate = sig[block, :]
        gate_grad = grad[block, :] * (combined[block, :] * phi[block, :]) * gate * (1.0 - gate)
        gate_low[block, :] = gate_grad.astype(bf16)
        return carry + fold(gate_grad)

    bias_sum = over_blocks(rows, element, zero)
    wide[...] = dot_nt(gate_low[...], glu[layer])

    def element_two(start, carry):
        block = pl.ds(start, ELEMENT_ROWS)
        value = combined[block, :]
        activation_grad = grad[block, :] * sig[block, :] + wide[block, :]
        slope = phi[block, :] + value * (jnp.exp(-0.5 * value * value) * inv_root_two_pi)
        result = activation_grad * slope
        combined_grad[block, :] = result
        combined_low[block, :] = result.astype(bf16)
        mixed = normed[block, :] * gain[layer : layer + 1, :] + bias[layer : layer + 1, :]
        return carry + fold(result * mixed)

    skip_sum = over_blocks(rows, element_two, zero)
    sums[0:1, :] = jnp.sum(bias_sum, 0, keepdims=True)
    sums[1:2, :] = jnp.sum(skip_sum, 0, keepdims=True)
    grad_own[...] = dot_nt(combined_low[...], out_own[layer, 0])
    grad_oth[...] = dot_nt(combined_low[...], out_oth[layer, 0])
    lanes = make_lanes(rows_ref, tiles_ref, layer, True, rows)
    first_pass(
        info[0] == 1,
        (grad_own, grad_oth),
        (masks[1], masks[0]),
        (whole.at[1], whole.at[0]),
        lanes,
        ids,
        ends,
        payload,
    )


def turn_kernel(
    row_devices,
    gathered,
    ends_own,
    ends_oth,
    drive_own,
    drive_oth,
    keep_own,
    keep_oth,
    whole,
    rows_ref,
    tiles_ref,
    ids,
    out_own,
    out_oth,
    x_in,
    normed,
    gain,
    bias,
    skip,
    glu,
    glu_bias,
    cotangent,
    low_own,
    low_oth,
    block_out,
    grad_out,
    combined_grad,
    grad_own,
    grad_oth,
    next_ends_own,
    next_ends_oth,
    payload,
    sums,
    mine,
    theirs,
    places,
    small,
    wide,
    combined,
    phi_rows,
    sig_rows,
    natural,
    natural_out,
    states_own,
    states_oth,
    act_low,
    gate_low,
    combined_low,
):
    info = core_place(row_devices)
    rows = x_in.shape[0]
    span = rows // 8
    masks = (keep_own, keep_oth)
    forward_states(
        1, info, gathered, (ends_own, ends_oth), (drive_own, drive_oth), masks, whole, rows_ref, tiles_ref,
        ids, (states_own, states_oth), (low_own, low_oth), places, small,
    )
    wide[...] = dot(low_own[...], out_own[1, 0]) + dot(low_oth[...], out_oth[1, 0])

    def element(start, carry):
        block = pl.ds(start, ELEMENT_ROWS)
        mixed = normed[block, :] * gain[1:2, :] + bias[1:2, :]
        value = wide[block, :] + skip[1:2, :] * mixed
        phi = 0.5 * (1.0 + lax.erf(value * inv_root_two))
        combined[block, :] = value
        phi_rows[block, :] = phi
        act_low[block, :] = (value * phi).astype(bf16)
        return carry

    over_blocks(rows, element)
    wide[...] = dot(act_low[...], glu[1])
    base = pl.multiple_of(info[0] * rows, rows)
    fill_columns(natural, cotangent[pl.ds(base, rows), :])

    def element_two(start, carry):
        block = pl.ds(start, ELEMENT_ROWS)
        sig = jax.nn.sigmoid(wide[block, :] + glu_bias[1:2, :])
        sig_rows[block, :] = sig
        result = x_in[block, :] + combined[block, :] * phi_rows[block, :] * sig
        store_token_order(natural_out, start // 8, result, span)
        grad_out[block, :] = tile_order(natural, start // 8, ELEMENT_ROWS // 8, span)
        return carry

    over_blocks(rows, element_two)
    join_columns(block_out, natural_out)
    sums[...] = jnp.zeros_like(sums)
    backward_half(
        1, info, grad_out, combined, phi_rows, sig_rows, normed, gain, bias, skip, glu, out_own, out_oth, masks,
        whole, rows_ref, tiles_ref, ids, gate_low, combined_grad, combined_low, grad_own, grad_oth,
        (next_ends_own, next_ends_oth), payload, sums, wide,
    )
    gradient_pack(act_low, gate_low, combined_low, low_own, low_oth, mine, theirs, wide)


def adjoint_states(
    layer, info, gathered, ends, grads, masks, whole, rows_ref, tiles_ref, ids, states, drives, lows, decay_sums,
    adjoints, places, small,
):
    rows = grads[0].shape[0]
    lanes = make_lanes(rows_ref, tiles_ref, layer, True, rows)
    core, place = info
    running_up = core == 1
    init = second_starts(
        running_up, place, lanes, gathered, ids, ends, (whole.at[1], whole.at[0]), places, small
    )
    width = lanes.states
    zero = jnp.zeros((8, width), f32)
    for side in range(2):
        adjoints[side][...] = states[side][...].astype(f32)

    def visit(side, where, re, im, sums):
        drive_re, drive_im = drives[side][where, :width], drives[side][where, width:]
        moved_re = adjoints[side][where, :width] - drive_re
        moved_im = adjoints[side][where, width:] - drive_im
        adjoints[side][where, :width] = re
        adjoints[side][where, width:] = im
        mine = sums[side]
        mine = (
            mine[0] + (re * moved_re + im * moved_im),
            mine[1] + (im * moved_re - re * moved_im),
            mine[2] + (re * drive_re + im * drive_im),
        )
        return (mine, sums[1]) if side == 0 else (sums[0], mine)

    _, sums = sweep(
        running_up, grads, (masks[1], masks[0]), lanes, init, visit, ((zero, zero, zero), (zero, zero, zero))
    )
    decay_sums[...] = jnp.zeros_like(decay_sums)
    for side in range(2):
        for i in range(3):
            decay_sums[3 * side + i : 3 * side + i + 1, :] = jnp.sum(sums[side][i], 0, keepdims=True)
        lows[side][...] = (adjoints[side][...] * lanes.scaling(side)).astype(bf16)


def norm_backward(
    layer, low_own, low_oth, in_own, in_oth, grad, combined_grad, normed, inv_scale, gain, skip, sums, wide, finish
):
    rows, width = grad.shape
    wide[...] = dot_nt(low_own[...], in_own[layer, 0]) + dot_nt(low_oth[...], in_oth[layer, 0])
    zero = jnp.zeros((8, width), f32)

    def element(start, carry):
        block = pl.ds(start, ELEMENT_ROWS)
        mixed_grad = wide[block, :] + combined_grad[block, :] * skip[layer : layer + 1, :]
        unit = normed[block, :]
        weighted = mixed_grad * unit
        inner = mixed_grad * gain[layer : layer + 1, :]
        mean_one = jnp.sum(inner, 1, keepdims=True) * (1.0 / width)
        mean_two = jnp.sum(weighted * gain[layer : layer + 1, :], 1, keepdims=True) * (1.0 / width)
        spread = jnp.concatenate([inv_scale[block, :]] * (width // LANES), 1)
        finish(start, grad[block, :] + spread * (inner - mean_one - unit * mean_two))
        return carry[0] + fold(weighted), carry[1] + fold(mixed_grad)

    gain_sum, bias_sum = over_blocks(rows, element, (zero, zero))
    sums[2:3, :] = jnp.sum(gain_sum, 0, keepdims=True)
    sums[3:4, :] = jnp.sum(bias_sum, 0, keepdims=True)


def back_kernel(
    row_devices,
    in_low_own,
    in_low_oth,
    keep_own,
    keep_oth,
    whole,
    rows_ref,
    tiles_ref,
    ids,
    in_own,
    in_oth,
    out_own,
    out_oth,
    grad_in,
    combined_grad_in,
    normed_in,
    inv_in,
    gain,
    bias,
    skip,
    glu,
    combined,
    phi,
    sig,
    normed,
    act_low,
    low_own,
    low_oth,
    grad_out,
    combined_grad,
    next_own,
    next_oth,
    next_ends_own,
    next_ends_oth,
    payload,
    sums,
    mine,
    theirs,
    wide,
    gate_low,
    combined_low,
):
    info = core_place(row_devices)
    masks = (keep_own, keep_oth)
    sums[...] = jnp.zeros_like(sums)

    def finish(start, value):
        grad_out[pl.ds(start, ELEMENT_ROWS), :] = value

    norm_backward(
        1, in_low_own, in_low_oth, in_own, in_oth, grad_in, combined_grad_in, normed_in, inv_in, gain, skip, sums, wide,
        finish,
    )
    backward_half(
        0, info, grad_out, combined, phi, sig, normed, gain, bias, skip, glu, out_own, out_oth, masks, whole,
        rows_ref, tiles_ref, ids, gate_low, combined_grad, combined_low, next_own, next_oth,
        (next_ends_own, next_ends_oth), payload, sums, wide,
    )
    gradient_pack(act_low, gate_low, combined_low, low_own, low_oth, mine, theirs, wide)


def scan_kernel(
    layer,
    row_devices,
    gathered,
    ends_own,
    ends_oth,
    grad_own,
    grad_oth,
    keep_own,
    keep_oth,
    whole,
    rows_ref,
    tiles_ref,
    ids,
    states_own,
    states_oth,
    drive_own,
    drive_oth,
    mixed_low,
    low_own,
    low_oth,
    decay_sums,
    mine,
    theirs,
    places,
    small,
    adjoint_own,
    adjoint_oth,
):
    info = core_place(row_devices)
    masks = (keep_own, keep_oth)
    adjoint_states(
        layer, info, gathered, (ends_own, ends_oth), (grad_own, grad_oth), masks, whole, rows_ref, tiles_ref, ids,
        (states_own, states_oth), (drive_own, drive_oth), (low_own, low_oth), decay_sums,
        (adjoint_own, adjoint_oth), places, small,
    )
    store_columns(mine, 0, dot_tn(mixed_low[...], low_own[...]))
    store_columns(theirs, 0, dot_tn(mixed_low[...], low_oth[...]))


def final_kernel(
    low_own, low_oth, in_own, in_oth, grad_in, combined_grad, normed, inv_scale, gain, skip, out, sums, wide, natural
):
    rows = grad_in.shape[0]
    sums[...] = jnp.zeros_like(sums)

    def finish(start, value):
        store_token_order(natural, start // 8, value, rows // 8)

    norm_backward(
        0, low_own, low_oth, in_own, in_oth, grad_in, combined_grad, normed, inv_scale, gain, skip, sums, wide, finish
    )
    join_columns(out, natural)


def store_columns(out, first, values):
    rows, width = values.shape
    for i in range(width // LANES):
        out[first + i * rows : first + (i + 1) * rows, :] = values[:, i * LANES : (i + 1) * LANES].astype(out.dtype)


def half_rows(core, act_low, gate_low, mine, theirs, first, wide):
    wide[...] = dot_tn(act_low[...], gate_low[...])
    half = wide.shape[0] // 2
    width = wide.shape[1]
    for out, which in ((mine, core), (theirs, 1 - core)):
        rows = pl.ds(pl.multiple_of(which * half, half), half)
        for i in range(width // LANES):
            out[first + i * half : first + (i + 1) * half, :] = wide[rows, i * LANES : (i + 1) * LANES].astype(out.dtype)


def gradient_pack(act_low, gate_low, combined_low, low_own, low_oth, mine, theirs, wide):
    store_columns(theirs, 0, dot_tn(low_oth[...], combined_low[...]))
    store_columns(mine, 0, dot_tn(low_own[...], combined_low[...]))
    size = low_own.shape[1] * (combined_low.shape[1] // LANES)
    half_rows(lax.axis_index("dir"), act_low, gate_low, mine, theirs, size, wide)


def slot(low_bit, parts):
    return jnp.bitwise_and(jnp.right_shift(lax.axis_index("seq"), low_bit), parts - 1)


def paired(values):
    while len(values) > 1:
        values = [a + b for a, b in zip(values[::2], values[1::2])]
    return values[0]


def part_rows(index, rows):
    return pl.ds(pl.multiple_of(index * rows, rows), rows)


def sum_parts(groups, outs, low_bit):
    parts = len(outs)
    mine = slot(low_bit, parts)
    for k, out in enumerate(outs):
        first = 0
        for rows, sources in groups:
            share = rows // parts
            where = part_rows(jnp.bitwise_xor(mine, k), share)
            total = paired([source[where, :].astype(f32) for source in sources])
            out[first : first + share, :] = total.astype(out.dtype)
            first += share


def gather_parts(sizes, sources, low_bit, outs):
    mine = slot(low_bit, len(sources))
    for k, source in enumerate(sources):
        first = 0
        for rows, out in zip(sizes, outs):
            out[part_rows(jnp.bitwise_xor(mine, k), rows), :] = source[first : first + rows, :]
            first += rows


def encode_small(value, outs, first):
    high = value.astype(bf16)
    low = (value - high.astype(f32)).astype(bf16)
    rows = value.shape[0]
    for out in outs:
        out[first : first + rows, :] = high
        out[first + rows : first + 2 * rows, :] = low


def decode_small(sources, first, rows):
    return paired(
        [
            source[first : first + rows, :].astype(f32) + source[first + rows : first + 2 * rows, :].astype(f32)
            for source in sources
        ]
    )


def early_cores_kernel(mine, got, *outs):
    sum_parts([(mine.shape[0], [mine, got])], outs, 0)


def relay_kernel(payload_in, payload):
    payload[...] = payload_in[...]


def first_plane_kernel(*refs):
    early, inner, (mine, got), outs = refs[:4], refs[4:8], refs[8:10], refs[10:]
    sum_parts([(early[0].shape[0], early), (inner[0].shape[0], inner)], outs[:4], 2)
    sum_parts([(mine.shape[0], [mine, got])], outs[4:], 0)


def late_cores_kernel(small_rows, mine, got, sums_turn, sums_back, sums_last, decay_late, decay_early, *outs):
    pack = outs[:4]
    small = outs[4]
    small_pack(sums_turn, sums_back, sums_last, decay_late, decay_early, small)
    sum_parts([(mine.shape[0], [mine, got])], pack, 0)
    encode_small(small[...], pack, mine.shape[0] // 4)


def planes_kernel(*refs):
    refs[-1][...] = paired([source[...].astype(f32) for source in refs[:-1]]).astype(bf16)


def gather_kernel(sizes, *refs):
    out = refs[-1]
    outs = []
    first = 0
    for rows in sizes:
        outs.append(out.at[first : first + 4 * rows])
        first += 4 * rows
    gather_parts(sizes, refs[:-1], 2, outs)


def second_plane_kernel(small_rows, *refs):
    outer, late, outs, small = refs[:4], refs[4:8], refs[8:12], refs[12]
    late_rows = late[0].shape[0] - 2 * small_rows
    sum_parts([(outer[0].shape[0], outer), (late_rows, late)], outs, 2)
    small[...] = decode_small(late, late_rows, small_rows)
    encode_small(small[...], outs, (outer[0].shape[0] + late_rows) // 4)


def second_planes_kernel(small_rows, *refs):
    sources, out, small = refs[:-2], refs[-2], refs[-1]
    rows = out.shape[0]
    out[...] = paired([source[0:rows, :].astype(f32) for source in sources]).astype(bf16)
    small[...] = decode_small(sources, rows, small_rows)


def join_kernel(mine, theirs, out):
    core = lax.axis_index("dir")
    rows = mine.shape[0]
    out[pl.ds(pl.multiple_of(core * rows, rows), rows), :] = mine[...]
    out[pl.ds(pl.multiple_of((1 - core) * rows, rows), rows), :] = theirs[...]


def matrix_columns(source, first, out):
    rows, width = out.shape
    for i in range(width // LANES):
        out[:, i * LANES : (i + 1) * LANES] = source[first + i * rows : first + (i + 1) * rows, :].astype(f32)


def gate_part_kernel(quarter_rows, first, *refs):
    sources, out, whole = refs[:-2], refs[-2], refs[-1]
    gather_parts((quarter_rows,), sources, 0, (whole,))
    out[...] = whole[first : first + out.shape[0], :]


def unpack_kernel(layer, olds, sizes, *refs):
    refs = list(refs)
    take = lambda n: [refs.pop(0) for _ in range(n)]
    sources = take(4)
    take(olds)
    outs = take(2)
    buffers = take(2)
    whole = take(2)
    (sems,) = refs
    gather_parts(sizes, sources, 0, whole)
    copies = []
    for i in range(2):
        matrix_columns(whole[i], 0, buffers[i])
        copies.append(pltpu.make_async_copy(buffers[i], outs[i].at[layer, 0], sems.at[i]))
        copies[-1].start()
    for copy in copies:
        copy.wait()


def gate_kernel(mine_early, theirs_early, mine_middle, theirs_middle, out):
    core = lax.axis_index("dir")
    half = out.shape[1] // 2
    width = out.shape[2]
    for layer, mine, theirs in ((1, mine_early, theirs_early), (0, mine_middle, theirs_middle)):
        for source, which in ((mine, core), (theirs, 1 - core)):
            rows = pl.ds(pl.multiple_of(which * half, half), half)
            for i in range(width // LANES):
                out[layer, rows, i * LANES : (i + 1) * LANES] = source[i * half : (i + 1) * half, :].astype(f32)


def small_pack(sums_turn, sums_back, sums_last, decay_late, decay_early, out):
    per = sums_turn.shape[1] // LANES
    thirds = decay_late.shape[1] // LANES
    out[...] = jnp.zeros_like(out)
    kinds = (
        ((sums_last, 2), (sums_back, 2)),
        ((sums_last, 3), (sums_back, 3)),
        ((sums_back, 1), (sums_turn, 1)),
        ((sums_back, 0), (sums_turn, 0)),
    )
    at = 0
    for kind in kinds:
        for source, row in kind:
            for i in range(per):
                out[at : at + 1, :] = source[row : row + 1, i * LANES : (i + 1) * LANES]
                at += 1
    for side in range(2):
        for source in (decay_late, decay_early):
            for term in range(3):
                for i in range(thirds):
                    row = 3 * side + term
                    out[at : at + 1, :] = source[row : row + 1, i * LANES : (i + 1) * LANES]
                    at += 1


def small_out_kernel(own, got, table, gain, bias, rate, turn, skip, gate):
    layers, _, states = table.shape
    thirds = states // LANES
    width = gain.shape[1]
    per = width // LANES
    at = 0
    for out in (gain, bias, skip, gate):
        for layer in range(layers):
            for i in range(per):
                out[layer : layer + 1, i * LANES : (i + 1) * LANES] = own[at : at + 1, :] + got[at : at + 1, :]
                at += 1
    other = at + layers * 3 * thirds
    for layer in range(layers):
        for i in range(thirds):
            lanes = slice(i * LANES, (i + 1) * LANES)
            rows = [(layer * 3 + t) * thirds + i for t in range(3)]
            term_re, term_im, term_scale = (
                own[at + row : at + row + 1, :] + got[other + row : other + row + 1, :] for row in rows
            )
            re, im, scale, damping, step_size, rotation, square = (
                table[layer, t : t + 1, lanes] for t in range(7)
            )
            grad_re = (term_re * re - term_im * im) / square
            grad_im = (term_re * im + term_im * re) / square
            grad_scale = term_scale / scale
            grad_damping = grad_scale * square / scale - (grad_re * re + grad_im * im)
            grad_rotation = grad_im * re - grad_re * im
            log_rate = grad_damping * damping
            rate[layer : layer + 1, lanes] = log_rate
            turn[2 * layer : 2 * layer + 1, lanes] = grad_rotation * step_size
            turn[2 * layer + 1 : 2 * layer + 2, lanes] = log_rate + grad_rotation * rotation


class Order:
    def __init__(self):
        self.tile = None

    def run(self, kernel, outs, operands, scratch=(), flops=0, name=None, spare=8, after=(), free_outs=0, alias=None,
            semaphores=0, cost=0):
        whole = pl.BlockSpec(memory_space=pltpu.VMEM)
        free = pl.BlockSpec(memory_space=pl.ANY)
        waits = list(after) + ([] if self.tile is None else [self.tile])
        inputs, results = len(operands), len(outs)
        skipped = len(waits)

        def body(*refs):
            token = refs[skipped + inputs]
            token[...] = jnp.zeros_like(token)
            kernel(*refs[skipped : skipped + inputs], *refs[skipped + inputs + 1 :])

        shapes = [jax.ShapeDtypeStruct((8, LANES), f32)]
        shapes += [jax.ShapeDtypeStruct(shape, dtype) for shape, dtype in outs]
        held = sum(jnp.dtype(dtype).itemsize * functools.reduce(lambda a, b: a * b, shape) for shape, dtype in scratch)
        specs = [free] * skipped + [whole] * inputs
        aliases = {}
        if alias is not None:
            for operand, out in alias.items():
                specs[skipped + operand] = free
                aliases[skipped + operand] = out + 1
        extra = [pltpu.SemaphoreType.DMA((semaphores,))] if semaphores else []
        results = pl.pallas_call(
            body,
            out_shape=shapes,
            in_specs=specs,
            out_specs=[whole] + [free] * free_outs + [whole] * (results - free_outs),
            scratch_shapes=[pltpu.VMEM(shape, dtype) for shape, dtype in scratch] + extra,
            input_output_aliases=aliases,
            compiler_params=pltpu.CompilerParams(vmem_limit_bytes=held + spare * 2**20),
            cost_estimate=pl.CostEstimate(flops=int(1 + cost * 1e9), bytes_accessed=int(1 + cost * 3e6), transcendentals=0),
            name=name,
        )(*waits, *operands)
        self.tile = results[0]
        return results[1:]


def swap(value):
    return lax.ppermute(value, "dir", [(0, 1), (1, 0)])


def across(value, bits):
    count = lax.axis_size("seq")
    return lax.ppermute(value, "seq", [(i, i ^ bits) for i in range(count)])


def beyond(value):
    bit = 4
    while (1 << bit) < lax.axis_size("seq"):
        value = (value.astype(f32) + across(value, 1 << bit).astype(f32)).astype(value.dtype)
        bit += 1
    return value


def exchanged(payload, row_devices):
    count = lax.axis_size("seq")
    group = 2 * row_devices
    groups = None
    if count != row_devices:
        groups = [list(range(i, i + group)) for i in range(0, 2 * count, group)]
    return lax.all_to_all(payload, ("seq", "dir"), 0, 0, tiled=True, axis_index_groups=groups)


def sent(parts, low_bit):
    return [parts[0]] + [across(parts[k], k << low_bit) for k in (1, 2, 3)]


def shared(value, low_bit):
    return [value] + [across(value, k << low_bit) for k in (1, 2, 3)]


def body(
    tokens,
    segment_ids,
    norm_gain,
    norm_bias,
    input_matrix,
    output_matrix,
    rate_params,
    turn_params,
    skip_weight,
    glu_weight,
    glu_bias,
    cotangent,
):
    chip_rows, width = tokens.shape
    rows = chip_rows // 2
    layers = rate_params.shape[0]
    states = rate_params.shape[2]
    row_devices = LENGTH // chip_rows
    order = Order()
    here = functools.partial

    in_own, out_own = input_matrix, output_matrix
    in_oth = swap(input_matrix)
    rate_oth, turn_oth = swap(rate_params), swap(turn_params)
    out_oth = swap(output_matrix)
    segments = segment_ids.reshape(chip_rows // LANES, LANES)

    full = ((rows, width), f32)
    full_low = ((rows, width), bf16)
    columns = ((width // LANES, rows, LANES), f32)
    wide = ((rows, 2 * states), f32)
    wide_low = ((rows, 2 * states), bf16)
    ends = ((8, 2 * states), f32)
    payload_shape = ((2 * row_devices, 16, LANES), f32)
    narrow = ((rows, LANES), f32)
    tile = ((8, LANES), f32)
    sums_shape = ((8, width), f32)
    decay_shape = ((8, states), f32)
    table_shape = ((layers, 16, states), f32)
    places = ((8, 2 * states), f32)
    in_size = width * (2 * states // LANES)
    out_size = 2 * states * (width // LANES)
    glu_size = width // 2 * (width // LANES)
    outer_size = out_size + glu_size
    outer_pack = ((outer_size, LANES), bf16)
    inner_pack = ((in_size, LANES), bf16)
    one = 2.0 * rows * width * 2 * states
    gate = 2.0 * rows * width * width
    scan = 1e9

    x0, normed0, inv0, mixed0, drive_own0, keep_own, keep_oth, whole, table, ids = order.run(
        here(open_kernel, row_devices),
        [full, full, narrow, full_low, wide, narrow, narrow, ((2, 8, LANES), f32), table_shape, tile],
        [tokens, segments, norm_gain, norm_bias, rate_params, turn_params, in_own],
        [columns, tile],
        flops=one + scan,
        name="open_norm",
    )
    drive_oth0, ends_own, ends_oth, payload, table, tiles = order.run(
        here(open_second_kernel, row_devices),
        [wide, ends, ends, payload_shape, table_shape, ((layers, 16, LANES), f32)],
        [mixed0, in_oth, rate_oth, turn_oth, table, drive_own0, keep_own, keep_oth, whole, ids],
        flops=one + scan,
        name="open_scan",
        after=[out_oth],
    )
    gathered = exchanged(payload, row_devices)
    (
        low_own0, low_oth0, combined0, phi0, sig0, act_low0, x1, normed1, inv1, mixed1, drive_own1, drive_oth1,
        ends_own, ends_oth, payload,
    ) = order.run(
        here(mid_kernel, row_devices),
        [wide_low, wide_low, full, full, full, full_low, full, full, narrow, full_low, wide, wide, ends, ends,
         payload_shape],
        [gathered, ends_own, ends_oth, drive_own0, drive_oth0, keep_own, keep_oth, whole, table, tiles,
         ids, out_own, out_oth, x0, normed0, norm_gain, norm_bias, skip_weight, glu_weight, glu_bias, in_own, in_oth],
        [places, tile, full, wide, wide],
        flops=4 * one + gate + 3 * scan,
        name="mid",
    )
    gathered = exchanged(payload, row_devices)
    (
        low_own1, low_oth1, half_out, grad1, combined_grad1, grad_own1, grad_oth1, ends_own, ends_oth, payload,
        sums_turn, mine, theirs,
    ) = order.run(
        here(turn_kernel, row_devices),
        [wide_low, wide_low, full, full, full, wide, wide, ends, ends, payload_shape, sums_shape, outer_pack, outer_pack],
        [gathered, ends_own, ends_oth, drive_own1, drive_oth1, keep_own, keep_oth, whole, table, tiles,
         ids, out_own, out_oth, x1, normed1, norm_gain, norm_bias, skip_weight, glu_weight, glu_bias, cotangent],
        [places, tile, full, full, full, full, columns, columns, wide, wide, full_low, full_low, full_low],
        flops=4 * one + 2 * gate + 4 * scan,
        name="turn",
    )
    got = swap(theirs)
    got_half = swap(half_out)
    gathered = exchanged(payload, row_devices)
    early = order.run(
        early_cores_kernel, [((outer_size // 4, LANES), bf16)] * 4, [mine, got], name="early_cores", after=[gathered]
    )
    early = sent(early, 0)
    in_low_own1, in_low_oth1, decay_sums1, mine, theirs = order.run(
        here(scan_kernel, 1, row_devices),
        [wide_low, wide_low, decay_shape, inner_pack, inner_pack],
        [gathered, ends_own, ends_oth, grad_own1, grad_oth1, keep_own, keep_oth, whole, table, tiles,
         ids, low_own1, low_oth1, drive_own1, drive_oth1, mixed1],
        [places, tile, wide, wide],
        name="scan_one",
    )
    got = swap(theirs)
    (
        grad0, combined_grad0, grad_own0, grad_oth0, ends_own, ends_oth, payload, sums_back, mine_outer, theirs_outer,
    ) = order.run(
        here(back_kernel, row_devices),
        [full, full, wide, wide, ends, ends, payload_shape, sums_shape, outer_pack, outer_pack],
        [in_low_own1, in_low_oth1, keep_own, keep_oth, whole, table, tiles, ids, in_own, in_oth, out_own, out_oth, grad1,
         combined_grad1, normed1, inv1, norm_gain, norm_bias, skip_weight, glu_weight, combined0, phi0, sig0, normed0,
         act_low0, low_own0, low_oth0],
        [full, full_low, full_low],
        name="back",
    )
    got_outer = swap(theirs_outer)
    (payload,) = order.run(relay_kernel, [payload_shape], [payload], name="relay", after=early[1:] + [got_half], cost=RELAY)
    gathered = exchanged(payload, row_devices)
    inner = order.run(
        early_cores_kernel, [((in_size // 4, LANES), bf16)] * 4, [mine, got], name="inner_cores", after=[gathered]
    )
    inner = sent(inner, 0)
    in_low_own0, in_low_oth0, decay_sums0, mine, theirs = order.run(
        here(scan_kernel, 0, row_devices),
        [wide_low, wide_low, decay_shape, inner_pack, inner_pack],
        [gathered, ends_own, ends_oth, grad_own0, grad_oth0, keep_own, keep_oth, whole, table, tiles,
         ids, low_own0, low_oth0, drive_own0, drive_oth0, mixed0],
        [places, tile, wide, wide],
        name="scan_zero",
    )
    got = swap(theirs)
    quarter = (outer_size + in_size) // 4
    parts = order.run(
        first_plane_kernel,
        [((quarter // 4, LANES), bf16)] * 4 + [((outer_size // 4, LANES), bf16)] * 4,
        early + inner + [mine_outer, got_outer],
        name="first_plane",
    )
    first = sent(parts[:4], 2)
    outer = sent(parts[4:], 0)
    half_grad, sums_last = order.run(
        final_kernel,
        [full, sums_shape],
        [in_low_own0, in_low_oth0, in_own, in_oth, grad0, combined_grad0, normed0, inv0, norm_gain, skip_weight],
        [full, columns],
        name="final_norm",
    )
    small_rows = -(-(4 * layers * (width // LANES) + 6 * layers * (states // LANES)) // 16) * 16
    *late, _ = order.run(
        here(late_cores_kernel, small_rows),
        [((in_size // 4 + 2 * small_rows, LANES), bf16)] * 4 + [((small_rows, LANES), f32)],
        [mine, got, sums_turn, sums_back, sums_last, decay_sums0, decay_sums1],
        name="late_cores",
    )
    late = sent(late, 0)
    (share,) = order.run(planes_kernel, [((quarter // 4, LANES), bf16)], first, name="first_planes", after=outer[1:])
    first = shared(beyond(share), 2)
    whole_rows = ((chip_rows, width), f32)
    (block_output,) = order.run(join_kernel, [whole_rows], [half_out, got_half], name="join_out")
    sizes = (outer_size // 16, in_size // 16)
    (full_quarter,) = order.run(
        here(gather_kernel, sizes), [((quarter, LANES), bf16)], first, name="first_gather"
    )
    first = shared(full_quarter, 0)
    (tokens_grad,) = order.run(join_kernel, [whole_rows], [half_grad, swap(half_grad)], name="join_grad")
    *second, _ = order.run(
        here(second_plane_kernel, small_rows),
        [((quarter // 4 + 2 * small_rows, LANES), bf16)] * 4 + [((small_rows, LANES), f32)],
        outer + late,
        name="second_plane",
    )
    second = sent(second, 2)
    share, small = order.run(
        here(second_planes_kernel, small_rows), [((quarter // 4, LANES), bf16), ((small_rows, LANES), f32)], second,
        name="second_planes",
    )
    second = shared(beyond(share), 2)
    small = beyond(small)
    got_small = swap(small)
    in_shape, out_shape = input_matrix.shape, output_matrix.shape

    def gate_part(quarters, name):
        (value,) = order.run(
            here(gate_part_kernel, outer_size // 4, out_size), [((glu_size, LANES), bf16)], quarters,
            [((outer_size, LANES), bf16)], name=name,
        )
        return value

    def unpack(quarters, layer, old, name):
        return order.run(
            here(unpack_kernel, layer, len(old), (outer_size // 4, in_size // 4)),
            [(out_shape, f32), (in_shape, f32)],
            quarters + old,
            [(out_shape[2:], f32), (in_shape[2:], f32), outer_pack, inner_pack],
            name=name,
            free_outs=2,
            alias={4 + i: i for i in range(len(old))},
            semaphores=2,
        )

    gate_one = gate_part(first, "gate_one")
    got_one = swap(gate_one)
    results = unpack(first, 1, [], "unpack_one")
    gain_grad, bias_grad, rate_grad, turn_grad, skip_grad, gate_grad = order.run(
        small_out_kernel,
        [((layers, width), f32), ((layers, width), f32), ((layers, states), f32), ((2 * layers, states), f32),
         ((layers, width), f32), ((layers, width), f32)],
        [small, got_small, table],
        name="small_out",
    )
    (full_quarter,) = order.run(
        here(gather_kernel, sizes), [((quarter, LANES), bf16)], second, name="second_gather"
    )
    second = shared(full_quarter, 0)
    gate_zero = gate_part(second, "gate_zero")
    got_zero = swap(gate_zero)
    out_all, in_all = unpack(second, 0, list(results), "unpack_zero")
    (glu_all,) = order.run(
        gate_kernel, [(glu_weight.shape, f32)], [gate_one, got_one, gate_zero, got_zero], name="unpack_gate"
    )
    return (
        block_output,
        tokens_grad,
        gain_grad,
        bias_grad,
        in_all,
        out_all,
        rate_grad.reshape(rate_params.shape),
        turn_grad.reshape(turn_params.shape),
        skip_grad,
        glu_all,
        gate_grad,
    )


def solution(mesh):
    return jax.shard_map(
        body,
        mesh=mesh,
        in_specs=(
            P("seq", None),
            P("seq"),
            P(),
            P(),
            P(None, "dir", None, None),
            P(None, "dir", None, None),
            P(None, "dir", None),
            P(None, "dir", None, None),
            P(),
            P(),
            P(),
            P("seq", None),
        ),
        out_specs=(
            P("seq", None),
            P("seq", None),
            P(),
            P(),
            P(None, "dir", None, None),
            P(None, "dir", None, None),
            P(None, "dir", None),
            P(None, "dir", None, None),
            P(),
            P(),
            P(),
        ),
        check_vma=False,
    )
```

```python
import functools

import jax
import jax.numpy as jnp
from jax import lax
from jax.experimental import pallas as pl
from jax.experimental.pallas import tpu as pltpu
from jax.sharding import PartitionSpec as P

LENGTH = 16384
LONGEST_RUN = 8192

eps = 1e-05
inv_root_two = 0.7071067811865476
inv_root_two_pi = 0.3989422804014327

f32 = jnp.float32
bf16 = jnp.bfloat16


LANES = 128
ELEMENT_ROWS = 512
UNROLL = 8
RELAY = 50


def core_place(row_devices):
    core = lax.axis_index("dir")
    return core, lax.rem(lax.axis_index("seq"), row_devices) * 2 + core


def dot(a, b):
    return jnp.dot(a, b, preferred_element_type=f32)


def dot_nt(a, b):
    return lax.dot_general(a, b, (((1,), (1,)), ((), ())), preferred_element_type=f32)


def dot_tn(a, b):
    return lax.dot_general(a, b, (((0,), (0,)), ((), ())), preferred_element_type=f32)


def squared(re, im, times):
    for _ in range(times):
        re, im = re * re - im * im, 2.0 * re * im
    return re, im


def over_blocks(rows, step, init=()):
    def one(i, carry):
        return step(pl.multiple_of(i * ELEMENT_ROWS, ELEMENT_ROWS), carry)

    return lax.fori_loop(0, rows // ELEMENT_ROWS, one, init)


def fold(values):
    total = values[0:8]
    for start in range(8, values.shape[0], 8):
        total = total + values[start : start + 8]
    return total


class Lanes:
    def __init__(self, rows_ref, tiles_ref, layer, adjoint, spans, rows):
        states = rows_ref.shape[2]
        self.states = states
        self.rows_ref, self.layer = rows_ref, layer
        flip = -1.0 if adjoint else 1.0
        self.step = []
        self.run = []
        self.block = []
        for side in range(2):
            row = 8 * side
            re = rows_ref[layer, row : row + 1, :]
            im = rows_ref[layer, row + 1 : row + 2, :] * flip
            self.step.append((jnp.broadcast_to(re, (8, states)), jnp.broadcast_to(im, (8, states))))
            self.run.append(squared(re, im, (spans - 1).bit_length()))
            thirds = states // LANES
            tile_re = tiles_ref[layer, 8 * side : 8 * side + thirds, :]
            tile_im = tiles_ref[layer, 8 * side + thirds : 8 * side + 2 * thirds, :] * flip
            self.block.append(squared(tile_re, tile_im, (rows - 1).bit_length()))

    def scaling(self, side):
        row = self.rows_ref[self.layer, 8 * side + 2 : 8 * side + 3, :]
        return jnp.concatenate([row, row], 1)


def sweep(first_forward, drives, masks, lanes, init, visit=None, totals=()):
    states = lanes.states
    span = drives[0].shape[0] // 8

    def step(i, carry):
        values, sums = carry
        up = pl.multiple_of(i * 8, 8)
        down = pl.multiple_of((span - 1 - i) * 8, 8)
        places = (jnp.where(first_forward, up, down), jnp.where(first_forward, down, up))
        new = []
        for side in range(2):
            rows = pl.ds(pl.multiple_of(places[side], 8), 8)
            keep = masks[side][rows, :]
            keep = jnp.concatenate([keep] * (states // LANES), 1)
            step_re, step_im = lanes.step[side]
            step_re, step_im = step_re * keep, step_im * keep
            re, im = values[side]
            drive_re = drives[side][rows, :states]
            drive_im = drives[side][rows, states:]
            re, im = (
                step_re * re - step_im * im + drive_re,
                step_re * im + step_im * re + drive_im,
            )
            new.append((re, im))
            if visit is not None:
                sums = visit(side, rows, re, im, sums)
        return tuple(new), sums

    return lax.fori_loop(0, span, step, (init, totals), unroll=UNROLL)


def run_chain(first_up, lanes, side, ends, whole, start, places):
    states = lanes.states
    power_re, power_im = lanes.run[side]
    re, im = start
    for i in range(8):
        s = jnp.where(first_up, i, 7 - i)
        row = pl.ds(s, 1)
        if places is not None:
            places[row, :states] = re
            places[row, states:] = im
        passes = whole[row, :]
        passes = jnp.concatenate([passes] * (states // LANES), 1)
        pass_re, pass_im = power_re * passes, power_im * passes
        end_re, end_im = ends[row, :states], ends[row, states:]
        re, im = (end_re + pass_re * re - pass_im * im, end_im + pass_re * im + pass_im * re)
    return re, im


def first_pass(running_up, drives, masks, wholes, lanes, ids_ref, ends, payload):
    states = lanes.states
    thirds = states // LANES
    nothing = jnp.zeros((8, states), f32)
    zero = (nothing, nothing)
    values, _ = sweep(running_up, drives, masks, lanes, (zero, zero))
    one = jnp.zeros((16, LANES), f32)
    payload[0] = one
    for side in range(2):
        ends[side][:, :states] = values[side][0]
        ends[side][:, states:] = values[side][1]
        upward = running_up if side == 0 else jnp.logical_not(running_up)
        start = jnp.zeros((1, states), f32)
        re, im = run_chain(upward, lanes, side, ends[side], wholes[side], (start, start), None)
        base = jnp.where(upward, 0, 8)
        for i in range(thirds):
            payload[0, pl.ds(base + i, 1), :] = re[:, LANES * i : LANES * (i + 1)]
            payload[0, pl.ds(base + thirds + i, 1), :] = im[:, LANES * i : LANES * (i + 1)]
        payload[0, 8 * side + 6 : 8 * side + 8, :] = ids_ref[0:2, :]
    one = payload[0]
    for i in range(1, payload.shape[0]):
        payload[i] = one


def entering(upward, place, lanes, side, gathered, ids_ref, small):
    states = lanes.states
    thirds = states // LANES
    count = gathered.shape[0]
    rows = lanes.token_rows
    block_re, block_im = lanes.block[side]
    re = jnp.zeros((thirds, LANES), f32)
    im = jnp.zeros((thirds, LANES), f32)
    base = jnp.where(upward, 0, 8)
    key = jnp.where(upward, ids_ref[0:1, :], ids_ref[1:2, :])
    for distance in range(min(count - 1, LONGEST_RUN // rows), 0, -1):
        source = jnp.where(upward, place - distance, place + distance)
        inside = jnp.logical_and(source >= 0, source < count)
        source = jnp.clip(source, 0, count - 1)
        sent_re = gathered[source, pl.ds(base, thirds), :]
        sent_im = gathered[source, pl.ds(base + thirds, thirds), :]
        sent_key = gathered[source, pl.ds(jnp.where(upward, base + 7, base + 6), 1), :]
        joined = jnp.where(jnp.logical_and(sent_key == key, inside), 1.0, 0.0)
        re, im = (
            joined * sent_re + block_re * re - block_im * im,
            joined * sent_im + block_re * im + block_im * re,
        )
    small[0:thirds, :] = re
    small[thirds : 2 * thirds, :] = im
    wide_re = jnp.concatenate([small[i : i + 1, :] for i in range(thirds)], 1)
    wide_im = jnp.concatenate([small[thirds + i : thirds + i + 1, :] for i in range(thirds)], 1)
    return wide_re, wide_im


def second_starts(running_up, place, lanes, gathered, ids_ref, ends, wholes, places, small):
    init = []
    states = lanes.states
    for side in range(2):
        upward = running_up if side == 0 else jnp.logical_not(running_up)
        start = entering(upward, place, lanes, side, gathered, ids_ref, small)
        run_chain(upward, lanes, side, ends[side], wholes[side], start, places)
        init.append((places[:, :states], places[:, states:]))
    return tuple(init)


def make_lanes(rows_ref, tiles_ref, layer, adjoint, token_rows):
    lanes = Lanes(rows_ref, tiles_ref, layer, adjoint, token_rows // 8, token_rows)
    lanes.token_rows = token_rows
    return lanes


def standardise(x):
    width = x.shape[1]
    average = jnp.sum(x, 1, keepdims=True) * (1.0 / width)
    centred = x - average
    inv_scale = lax.rsqrt(jnp.sum(centred * centred, 1, keepdims=True) * (1.0 / width) + eps)
    return centred * inv_scale, inv_scale


def fill_columns(columns, values):
    for i in range(columns.shape[0]):
        columns[i] = values[:, i * LANES : (i + 1) * LANES].astype(columns.dtype)


def tile_order(columns, first, count, span):
    tiles = [
        jnp.concatenate([columns[i, pl.ds(first + j, 8, stride=span), :] for i in range(columns.shape[0])], 1)
        for j in range(count)
    ]
    return jnp.concatenate(tiles, 0)


def store_token_order(columns, first, values, span):
    for j in range(values.shape[0] // 8):
        for i in range(columns.shape[0]):
            columns[i, pl.ds(first + j, 8, stride=span), :] = values[8 * j : 8 * j + 8, i * LANES : (i + 1) * LANES]


def join_columns(out, columns):
    for i in range(columns.shape[0]):
        out[:, i * LANES : (i + 1) * LANES] = columns[i]


def one_minus_exp(x):
    series = jnp.ones_like(x)
    for term in range(12, 1, -1):
        series = 1.0 - x * (1.0 / term) * series
    return jnp.where(x < 0.5, x * series, 1.0 - jnp.exp(-x))


def table_rows(table, layer, base, rate, turn):
    frequency = turn[layer, 0, 0:1, :]
    log_step = turn[layer, 0, 1:2, :]
    step_size = jnp.exp(log_step)
    damping = jnp.exp(rate[layer, 0:1, :] + log_step)
    magnitude = jnp.exp(-damping)
    rotation = frequency * step_size
    square = magnitude * magnitude
    rows = (
        magnitude * jnp.cos(rotation), magnitude * jnp.sin(rotation), jnp.sqrt(one_minus_exp(2.0 * damping)), damping,
        step_size, rotation, square,
    )
    for i, row in enumerate(rows):
        table[layer, base + i : base + i + 1, :] = row


def open_kernel(row_devices, tokens_from, x_out, normed_out, inv_out, tokens, natural, sems):
    copy = pltpu.make_async_copy(
        tokens_from.at[part_rows(lax.axis_index("dir"), tokens.shape[0])], tokens, sems.at[0]
    )
    copy.start()
    copy.wait()
    rows = x_out.shape[0]
    span = rows // 8
    fill_columns(natural, tokens[...].astype(f32))

    def element(start, carry):
        x = tile_order(natural, start // 8, ELEMENT_ROWS // 8, span)
        normed, inv_scale = standardise(x)
        block = pl.ds(start, ELEMENT_ROWS)
        x_out[block, :] = x
        normed_out[block, :] = normed
        inv_out[block, :] = jnp.broadcast_to(inv_scale, (ELEMENT_ROWS, LANES))
        return carry

    over_blocks(rows, element)


def open_second_kernel(
    row_devices,
    normed,
    segments,
    gain,
    bias,
    rate,
    turn,
    rate_oth,
    turn_oth,
    in_own,
    in_oth,
    mixed_low,
    drive_own,
    drive_oth,
    keep_own,
    keep_oth,
    whole_out,
    ends_own,
    ends_oth,
    payload,
    table,
    tiles,
    ids,
    rows8,
):
    core, _ = core_place(row_devices)
    rows = normed.shape[0]
    span = rows // 8

    def element(start, carry):
        block = pl.ds(start, ELEMENT_ROWS)
        mixed_low[block, :] = (normed[block, :] * gain[0:1, :] + bias[0:1, :]).astype(bf16)
        return carry

    over_blocks(rows, element)
    table[...] = jnp.zeros_like(table)
    tiles[...] = jnp.zeros_like(tiles)
    thirds = table.shape[2] // LANES
    for layer in range(table.shape[0]):
        table_rows(table, layer, 0, rate, turn)
        table_rows(table, layer, 8, rate_oth, turn_oth)
        for side in range(2):
            for part in range(2):
                for i in range(thirds):
                    at = 8 * side + part * thirds + i
                    tiles[layer, at : at + 1, :] = table[
                        layer, 8 * side + part : 8 * side + part + 1, i * LANES : (i + 1) * LANES
                    ]

    number = segments[...].astype(f32)
    count = number.shape[0]
    lane = lax.broadcasted_iota(jnp.int32, number.shape, 1)
    row = lax.broadcasted_iota(jnp.int32, number.shape, 0)
    back = pltpu.roll(number, 1, 1)
    back = jnp.where(lane == 0, pltpu.roll(back, 1, 0), back)
    ahead = pltpu.roll(number, LANES - 1, 1)
    ahead = jnp.where(lane == LANES - 1, pltpu.roll(ahead, count - 1, 0), ahead)
    edge_first = jnp.logical_and(lane == 0, row == 0)
    edge_last = jnp.logical_and(lane == LANES - 1, row == count - 1)
    up_keep = jnp.where(jnp.logical_or(number == back, edge_first), 1.0, 0.0)
    down_keep = jnp.where(jnp.logical_or(number == ahead, edge_last), 1.0, 0.0)
    per = LANES // span
    used = 8 // per
    for side, out in ((0, keep_own), (1, keep_oth)):
        rows8[0:count, :] = jnp.where(core == side, up_keep, down_keep)
        half = rows8[pl.ds(core * used, used), :]
        runs = jnp.concatenate([half[s // per : s // per + 1] for s in range(8)], 0)
        place = lax.broadcasted_iota(jnp.int32, (8, LANES), 1)
        sub = lax.broadcasted_iota(jnp.int32, (8, LANES), 0)
        first = lax.rem(sub, per) * span
        inside = jnp.logical_and(place >= first, place < first + span)
        least = jnp.min(jnp.where(inside, runs, 1.0), 1, keepdims=True)
        whole_out[side] = jnp.broadcast_to(least, (8, LANES))
        step = lax.broadcasted_iota(jnp.int32, (span, 8, LANES), 0)
        spread = jnp.where(step == (place - first)[None], runs[None], 0.0)
        spread = spread.reshape(span * 8, LANES).astype(bf16)
        out[...] = dot(spread, jnp.ones((LANES, LANES), bf16))
    rows8[0:count, :] = number
    first_row = rows8[pl.ds(core * used, 1), :]
    last_row = rows8[pl.ds(core * used + used - 1, 1), :]
    ids[...] = jnp.zeros_like(ids)
    ids[0:1, :] = jnp.broadcast_to(first_row[:, 0:1], (1, LANES))
    ids[1:2, :] = jnp.broadcast_to(last_row[:, LANES - 1 : LANES], (1, LANES))
    for side, (matrix, drive) in enumerate(((in_own, drive_own), (in_oth, drive_oth))):
        scale = table[0, 8 * side + 2 : 8 * side + 3, :]
        drive[...] = dot(mixed_low[...], matrix[0, 0]) * jnp.concatenate([scale, scale], 1)
    lanes = make_lanes(table, tiles, 0, False, rows)
    first_pass(
        core == 0,
        (drive_own, drive_oth),
        (keep_own, keep_oth),
        (whole_out.at[0], whole_out.at[1]),
        lanes,
        ids,
        (ends_own, ends_oth),
        payload,
    )


def forward_states(layer, info, gathered, ends, drives, masks, whole, rows_ref, tiles_ref, ids, states, lows, places, small):
    rows = drives[0].shape[0]
    lanes = make_lanes(rows_ref, tiles_ref, layer, False, rows)
    core, place = info
    running_up = core == 0
    init = second_starts(
        running_up, place, lanes, gathered, ids, ends, (whole.at[0], whole.at[1]), places, small
    )
    width = lanes.states

    def visit(side, where, re, im, sums):
        states[side][where, :width] = re
        states[side][where, width:] = im
        return sums

    sweep(running_up, drives, masks, lanes, init, visit)
    for side in range(2):
        lows[side][...] = states[side][...].astype(bf16)


def mid_kernel(
    row_devices,
    gathered,
    ends_own,
    ends_oth,
    drive_own,
    drive_oth,
    keep_own,
    keep_oth,
    whole,
    rows_ref,
    tiles_ref,
    ids,
    out_own,
    out_oth,
    x_in,
    normed,
    gain,
    bias,
    skip,
    glu,
    glu_bias,
    in_own,
    in_oth,
    low_own,
    low_oth,
    combined_out,
    phi_out,
    sig_out,
    act_low,
    x_out,
    normed_out,
    inv_out,
    mixed_out,
    next_own,
    next_oth,
    next_ends_own,
    next_ends_oth,
    payload,
    places,
    small,
    wide,
    states_own,
    states_oth,
):
    info = core_place(row_devices)
    rows = x_in.shape[0]
    masks = (keep_own, keep_oth)
    forward_states(
        0, info, gathered, (ends_own, ends_oth), (drive_own, drive_oth), masks, whole, rows_ref, tiles_ref,
        ids, (states_own, states_oth), (low_own, low_oth), places, small,
    )
    wide[...] = dot(low_own[...], out_own[0, 0]) + dot(low_oth[...], out_oth[0, 0])

    def element(start, carry):
        block = pl.ds(start, ELEMENT_ROWS)
        mixed = normed[block, :] * gain[0:1, :] + bias[0:1, :]
        combined = wide[block, :] + skip[0:1, :] * mixed
        phi = 0.5 * (1.0 + lax.erf(combined * inv_root_two))
        combined_out[block, :] = combined
        phi_out[block, :] = phi
        act_low[block, :] = (combined * phi).astype(bf16)
        return carry

    over_blocks(rows, element)
    wide[...] = dot(act_low[...], glu[0])

    def element_two(start, carry):
        block = pl.ds(start, ELEMENT_ROWS)
        sig = jax.nn.sigmoid(wide[block, :] + glu_bias[0:1, :])
        sig_out[block, :] = sig
        x = x_in[block, :] + combined_out[block, :] * phi_out[block, :] * sig
        x_out[block, :] = x
        after, inv_scale = standardise(x)
        normed_out[block, :] = after
        inv_out[block, :] = jnp.broadcast_to(inv_scale, (ELEMENT_ROWS, LANES))
        mixed_out[block, :] = (after * gain[1:2, :] + bias[1:2, :]).astype(bf16)
        return carry

    over_blocks(rows, element_two)
    for side, (matrix, out) in enumerate(((in_own, next_own), (in_oth, next_oth))):
        scale = rows_ref[1, 8 * side + 2 : 8 * side + 3, :]
        out[...] = dot(mixed_out[...], matrix[1, 0]) * jnp.concatenate([scale, scale], 1)
    lanes = make_lanes(rows_ref, tiles_ref, 1, False, rows)
    first_pass(
        info[0] == 0,
        (next_own, next_oth),
        masks,
        (whole.at[0], whole.at[1]),
        lanes,
        ids,
        (next_ends_own, next_ends_oth),
        payload,
    )


def backward_half(
    layer, info, grad, combined, phi, sig, normed, gain, bias, skip, glu, out_own, out_oth, masks, whole,
    rows_ref, tiles_ref, ids, gate_low, combined_grad, combined_low, grad_own, grad_oth, ends, payload, sums, wide,
):
    rows = grad.shape[0]
    width = grad.shape[1]
    zero = jnp.zeros((8, width), f32)

    def element(start, carry):
        block = pl.ds(start, ELEMENT_ROWS)
        gate = sig[block, :]
        gate_grad = grad[block, :] * (combined[block, :] * phi[block, :]) * gate * (1.0 - gate)
        gate_low[block, :] = gate_grad.astype(bf16)
        return carry + fold(gate_grad)

    bias_sum = over_blocks(rows, element, zero)
    wide[...] = dot_nt(gate_low[...], glu[layer])

    def element_two(start, carry):
        block = pl.ds(start, ELEMENT_ROWS)
        value = combined[block, :]
        activation_grad = grad[block, :] * sig[block, :] + wide[block, :]
        slope = phi[block, :] + value * (jnp.exp(-0.5 * value * value) * inv_root_two_pi)
        result = activation_grad * slope
        combined_grad[block, :] = result
        combined_low[block, :] = result.astype(bf16)
        mixed = normed[block, :] * gain[layer : layer + 1, :] + bias[layer : layer + 1, :]
        return carry + fold(result * mixed)

    skip_sum = over_blocks(rows, element_two, zero)
    sums[0:1, :] = jnp.sum(bias_sum, 0, keepdims=True)
    sums[1:2, :] = jnp.sum(skip_sum, 0, keepdims=True)
    grad_own[...] = dot_nt(combined_low[...], out_own[layer, 0])
    grad_oth[...] = dot_nt(combined_low[...], out_oth[layer, 0])
    lanes = make_lanes(rows_ref, tiles_ref, layer, True, rows)
    first_pass(
        info[0] == 1,
        (grad_own, grad_oth),
        (masks[1], masks[0]),
        (whole.at[1], whole.at[0]),
        lanes,
        ids,
        ends,
        payload,
    )


def turn_kernel(
    row_devices,
    gathered,
    ends_own,
    ends_oth,
    drive_own,
    drive_oth,
    keep_own,
    keep_oth,
    whole,
    rows_ref,
    tiles_ref,
    ids,
    out_own,
    out_oth,
    x_in,
    normed,
    gain,
    bias,
    skip,
    glu,
    glu_bias,
    cotangent,
    low_own,
    low_oth,
    block_out,
    grad_out,
    combined_grad,
    grad_own,
    grad_oth,
    next_ends_own,
    next_ends_oth,
    payload,
    sums,
    mine,
    theirs,
    places,
    small,
    wide,
    combined,
    phi_rows,
    sig_rows,
    natural,
    states_own,
    states_oth,
    act_low,
    gate_low,
    combined_low,
):
    info = core_place(row_devices)
    rows = x_in.shape[0]
    span = rows // 8
    masks = (keep_own, keep_oth)
    forward_states(
        1, info, gathered, (ends_own, ends_oth), (drive_own, drive_oth), masks, whole, rows_ref, tiles_ref,
        ids, (states_own, states_oth), (low_own, low_oth), places, small,
    )
    wide[...] = dot(low_own[...], out_own[1, 0]) + dot(low_oth[...], out_oth[1, 0])

    def element(start, carry):
        block = pl.ds(start, ELEMENT_ROWS)
        mixed = normed[block, :] * gain[1:2, :] + bias[1:2, :]
        value = wide[block, :] + skip[1:2, :] * mixed
        phi = 0.5 * (1.0 + lax.erf(value * inv_root_two))
        combined[block, :] = value
        phi_rows[block, :] = phi
        act_low[block, :] = (value * phi).astype(bf16)
        return carry

    over_blocks(rows, element)
    wide[...] = dot(act_low[...], glu[1])
    base = pl.multiple_of(info[0] * rows, rows)
    fill_columns(natural, cotangent[pl.ds(base, rows), :])

    def element_two(start, carry):
        block = pl.ds(start, ELEMENT_ROWS)
        sig = jax.nn.sigmoid(wide[block, :] + glu_bias[1:2, :])
        sig_rows[block, :] = sig
        block_out[block, :] = x_in[block, :] + combined[block, :] * phi_rows[block, :] * sig
        grad_out[block, :] = tile_order(natural, start // 8, ELEMENT_ROWS // 8, span)
        return carry

    over_blocks(rows, element_two)
    sums[...] = jnp.zeros_like(sums)
    backward_half(
        1, info, grad_out, combined, phi_rows, sig_rows, normed, gain, bias, skip, glu, out_own, out_oth, masks,
        whole, rows_ref, tiles_ref, ids, gate_low, combined_grad, combined_low, grad_own, grad_oth,
        (next_ends_own, next_ends_oth), payload, sums, wide,
    )
    gradient_pack(act_low, gate_low, combined_low, low_own, low_oth, mine, theirs, wide)


def adjoint_states(
    layer, info, gathered, ends, grads, masks, whole, rows_ref, tiles_ref, ids, states, drives, lows, decay_sums,
    adjoints, places, small,
):
    rows = grads[0].shape[0]
    lanes = make_lanes(rows_ref, tiles_ref, layer, True, rows)
    core, place = info
    running_up = core == 1
    init = second_starts(
        running_up, place, lanes, gathered, ids, ends, (whole.at[1], whole.at[0]), places, small
    )
    width = lanes.states
    zero = jnp.zeros((8, width), f32)
    for side in range(2):
        adjoints[side][...] = states[side][...].astype(f32)

    def visit(side, where, re, im, sums):
        drive_re, drive_im = drives[side][where, :width], drives[side][where, width:]
        moved_re = adjoints[side][where, :width] - drive_re
        moved_im = adjoints[side][where, width:] - drive_im
        adjoints[side][where, :width] = re
        adjoints[side][where, width:] = im
        mine = sums[side]
        mine = (
            mine[0] + (re * moved_re + im * moved_im),
            mine[1] + (im * moved_re - re * moved_im),
            mine[2] + (re * drive_re + im * drive_im),
        )
        return (mine, sums[1]) if side == 0 else (sums[0], mine)

    _, sums = sweep(
        running_up, grads, (masks[1], masks[0]), lanes, init, visit, ((zero, zero, zero), (zero, zero, zero))
    )
    decay_sums[...] = jnp.zeros_like(decay_sums)
    for side in range(2):
        for i in range(3):
            decay_sums[3 * side + i : 3 * side + i + 1, :] = jnp.sum(sums[side][i], 0, keepdims=True)
        lows[side][...] = (adjoints[side][...] * lanes.scaling(side)).astype(bf16)


def norm_backward(
    layer, low_own, low_oth, in_own, in_oth, grad, combined_grad, normed, inv_scale, gain, skip, sums, wide, finish
):
    rows, width = grad.shape
    wide[...] = dot_nt(low_own[...], in_own[layer, 0]) + dot_nt(low_oth[...], in_oth[layer, 0])
    zero = jnp.zeros((8, width), f32)

    def element(start, carry):
        block = pl.ds(start, ELEMENT_ROWS)
        mixed_grad = wide[block, :] + combined_grad[block, :] * skip[layer : layer + 1, :]
        unit = normed[block, :]
        weighted = mixed_grad * unit
        inner = mixed_grad * gain[layer : layer + 1, :]
        mean_one = jnp.sum(inner, 1, keepdims=True) * (1.0 / width)
        mean_two = jnp.sum(weighted * gain[layer : layer + 1, :], 1, keepdims=True) * (1.0 / width)
        spread = jnp.concatenate([inv_scale[block, :]] * (width // LANES), 1)
        finish(start, grad[block, :] + spread * (inner - mean_one - unit * mean_two))
        return carry[0] + fold(weighted), carry[1] + fold(mixed_grad)

    gain_sum, bias_sum = over_blocks(rows, element, (zero, zero))
    sums[2:3, :] = jnp.sum(gain_sum, 0, keepdims=True)
    sums[3:4, :] = jnp.sum(bias_sum, 0, keepdims=True)


def back_kernel(
    row_devices,
    in_low_own,
    in_low_oth,
    keep_own,
    keep_oth,
    whole,
    rows_ref,
    tiles_ref,
    ids,
    in_own,
    in_oth,
    out_own,
    out_oth,
    grad_in,
    combined_grad_in,
    normed_in,
    inv_in,
    gain,
    bias,
    skip,
    glu,
    combined,
    phi,
    sig,
    normed,
    act_low,
    low_own,
    low_oth,
    grad_out,
    combined_grad,
    next_own,
    next_oth,
    next_ends_own,
    next_ends_oth,
    payload,
    sums,
    mine,
    theirs,
    wide,
    gate_low,
    combined_low,
):
    info = core_place(row_devices)
    masks = (keep_own, keep_oth)
    sums[...] = jnp.zeros_like(sums)

    def finish(start, value):
        grad_out[pl.ds(start, ELEMENT_ROWS), :] = value

    norm_backward(
        1, in_low_own, in_low_oth, in_own, in_oth, grad_in, combined_grad_in, normed_in, inv_in, gain, skip, sums, wide,
        finish,
    )
    backward_half(
        0, info, grad_out, combined, phi, sig, normed, gain, bias, skip, glu, out_own, out_oth, masks, whole,
        rows_ref, tiles_ref, ids, gate_low, combined_grad, combined_low, next_own, next_oth,
        (next_ends_own, next_ends_oth), payload, sums, wide,
    )
    gradient_pack(act_low, gate_low, combined_low, low_own, low_oth, mine, theirs, wide)


def scan_kernel(
    layer,
    row_devices,
    gathered,
    ends_own,
    ends_oth,
    grad_own,
    grad_oth,
    keep_own,
    keep_oth,
    whole,
    rows_ref,
    tiles_ref,
    ids,
    states_own,
    states_oth,
    drive_own,
    drive_oth,
    mixed_low,
    low_own,
    low_oth,
    decay_sums,
    mine,
    theirs,
    places,
    small,
    adjoint_own,
    adjoint_oth,
):
    info = core_place(row_devices)
    masks = (keep_own, keep_oth)
    adjoint_states(
        layer, info, gathered, (ends_own, ends_oth), (grad_own, grad_oth), masks, whole, rows_ref, tiles_ref, ids,
        (states_own, states_oth), (drive_own, drive_oth), (low_own, low_oth), decay_sums,
        (adjoint_own, adjoint_oth), places, small,
    )
    store_columns(mine, 0, dot_tn(mixed_low[...], low_own[...]))
    store_columns(theirs, 0, dot_tn(mixed_low[...], low_oth[...]))


def final_kernel(
    low_own, low_oth, in_own, in_oth, grad_in, combined_grad, normed, inv_scale, gain, skip, block_out, out, sums, wide, natural, natural_out
):
    rows = grad_in.shape[0]
    sums[...] = jnp.zeros_like(sums)

    def finish(start, value):
        store_token_order(natural, start // 8, value, rows // 8)
        store_token_order(natural_out, start // 8, block_out[pl.ds(start, ELEMENT_ROWS), :], rows // 8)

    norm_backward(
        0, low_own, low_oth, in_own, in_oth, grad_in, combined_grad, normed, inv_scale, gain, skip, sums, wide, finish
    )
    join_columns(out.at[0], natural_out)
    join_columns(out.at[1], natural)


def store_columns(out, first, values):
    rows, width = values.shape
    for i in range(width // LANES):
        out[first + i * rows : first + (i + 1) * rows, :] = values[:, i * LANES : (i + 1) * LANES].astype(out.dtype)


def half_rows(core, act_low, gate_low, mine, theirs, first, wide):
    wide[...] = dot_tn(act_low[...], gate_low[...])
    half = wide.shape[0] // 2
    width = wide.shape[1]
    for out, which in ((mine, core), (theirs, 1 - core)):
        rows = pl.ds(pl.multiple_of(which * half, half), half)
        for i in range(width // LANES):
            out[first + i * half : first + (i + 1) * half, :] = wide[rows, i * LANES : (i + 1) * LANES].astype(out.dtype)


def gradient_pack(act_low, gate_low, combined_low, low_own, low_oth, mine, theirs, wide):
    store_columns(theirs, 0, dot_tn(low_oth[...], combined_low[...]))
    store_columns(mine, 0, dot_tn(low_own[...], combined_low[...]))
    size = low_own.shape[1] * (combined_low.shape[1] // LANES)
    half_rows(lax.axis_index("dir"), act_low, gate_low, mine, theirs, size, wide)


def slot(low_bit, parts):
    return jnp.bitwise_and(jnp.right_shift(lax.axis_index("seq"), low_bit), parts - 1)


def paired(values):
    while len(values) > 1:
        values = [a + b for a, b in zip(values[::2], values[1::2])]
    return values[0]


def part_rows(index, rows):
    return pl.ds(pl.multiple_of(index * rows, rows), rows)


def sum_parts(groups, outs, low_bit):
    parts = len(outs)
    mine = slot(low_bit, parts)
    for k, out in enumerate(outs):
        first = 0
        for rows, sources in groups:
            share = rows // parts
            where = part_rows(jnp.bitwise_xor(mine, k), share)
            total = paired([source[where, :].astype(f32) for source in sources])
            out[first : first + share, :] = total.astype(out.dtype)
            first += share


def gather_parts(sizes, sources, low_bit, outs):
    mine = slot(low_bit, len(sources))
    for k, source in enumerate(sources):
        first = 0
        for rows, out in zip(sizes, outs):
            out[part_rows(jnp.bitwise_xor(mine, k), rows), :] = source[first : first + rows, :]
            first += rows


def encode_small(value, outs, first):
    high = value.astype(bf16)
    low = (value - high.astype(f32)).astype(bf16)
    rows = value.shape[0]
    for out in outs:
        out[first : first + rows, :] = high
        out[first + rows : first + 2 * rows, :] = low


def decode_small(sources, first, rows):
    return paired(
        [
            source[first : first + rows, :].astype(f32) + source[first + rows : first + 2 * rows, :].astype(f32)
            for source in sources
        ]
    )


def early_cores_kernel(mine, got, *outs):
    sum_parts([(mine.shape[0], [mine, got])], outs, 0)


def relay_kernel(payload_in, payload):
    payload[...] = payload_in[...]


def first_plane_kernel(small_rows, *refs):
    early, inner, (outer, got_outer, late, got_late), small_sums = refs[:4], refs[4:8], refs[8:12], refs[12:17]
    first, second, small = refs[17:21], refs[21:25], refs[25]
    sum_parts([(early[0].shape[0], early), (inner[0].shape[0], inner)], first, 2)
    sum_parts([(outer.shape[0], [outer, got_outer]), (late.shape[0], [late, got_late])], second, 0)
    small_pack(*small_sums, small)
    encode_small(small[...], second, (outer.shape[0] + late.shape[0]) // 4)


def planes_kernel(*refs):
    refs[-1][...] = paired([source[...].astype(f32) for source in refs[:-1]]).astype(bf16)


def gather_kernel(sizes, *refs):
    out = refs[-1]
    outs = []
    first = 0
    for rows in sizes:
        outs.append(out.at[first : first + 4 * rows])
        first += 4 * rows
    gather_parts(sizes, refs[:-1], 2, outs)


def second_plane_kernel(small_rows, outer_rows, *refs):
    sources, outs, small = refs[:4], refs[4:8], refs[8]
    late_end = sources[0].shape[0] - 2 * small_rows
    groups = [
        (outer_rows, [source.at[0:outer_rows] for source in sources]),
        (late_end - outer_rows, [source.at[outer_rows:late_end] for source in sources]),
    ]
    sum_parts(groups, outs, 2)
    small[...] = decode_small(sources, late_end, small_rows)
    encode_small(small[...], outs, late_end // 4)


def second_planes_kernel(small_rows, *refs):
    sources, out, small = refs[:-2], refs[-2], refs[-1]
    rows = out.shape[0]
    out[...] = paired([source[0:rows, :].astype(f32) for source in sources]).astype(bf16)
    small[...] = decode_small(sources, rows, small_rows)


def join_kernel(mine, theirs, *outs):
    core = lax.axis_index("dir")
    rows = mine.shape[1]
    for i, out in enumerate(outs):
        out[part_rows(core, rows), :] = mine[i]
        out[part_rows(1 - core, rows), :] = theirs[i]


def matrix_columns(source, first, out):
    rows, width = out.shape
    for i in range(width // LANES):
        out[:, i * LANES : (i + 1) * LANES] = source[first + i * rows : first + (i + 1) * rows, :].astype(f32)


def gate_part_kernel(quarter_rows, first, *refs):
    sources, out, whole = refs[:-2], refs[-2], refs[-1]
    gather_parts((quarter_rows,), sources, 0, (whole,))
    out[...] = whole[first : first + out.shape[0], :]


def unpack_kernel(layer, olds, sizes, *refs):
    refs = list(refs)
    take = lambda n: [refs.pop(0) for _ in range(n)]
    sources = take(4)
    take(olds)
    outs = take(2)
    buffers = take(2)
    whole = take(2)
    (sems,) = refs
    gather_parts(sizes, sources, 0, whole)
    copies = []
    for i in range(2):
        matrix_columns(whole[i], 0, buffers[i])
        copies.append(pltpu.make_async_copy(buffers[i], outs[i].at[layer, 0], sems.at[i]))
        copies[-1].start()
    for copy in copies:
        copy.wait()


def gate_kernel(mine_early, theirs_early, mine_middle, theirs_middle, out):
    core = lax.axis_index("dir")
    half = out.shape[1] // 2
    width = out.shape[2]
    for layer, mine, theirs in ((1, mine_early, theirs_early), (0, mine_middle, theirs_middle)):
        for source, which in ((mine, core), (theirs, 1 - core)):
            rows = pl.ds(pl.multiple_of(which * half, half), half)
            for i in range(width // LANES):
                out[layer, rows, i * LANES : (i + 1) * LANES] = source[i * half : (i + 1) * half, :].astype(f32)


def small_pack(sums_turn, sums_back, sums_last, decay_late, decay_early, out):
    per = sums_turn.shape[1] // LANES
    thirds = decay_late.shape[1] // LANES
    out[...] = jnp.zeros_like(out)
    kinds = (
        ((sums_last, 2), (sums_back, 2)),
        ((sums_last, 3), (sums_back, 3)),
        ((sums_back, 1), (sums_turn, 1)),
        ((sums_back, 0), (sums_turn, 0)),
    )
    at = 0
    for kind in kinds:
        for source, row in kind:
            for i in range(per):
                out[at : at + 1, :] = source[row : row + 1, i * LANES : (i + 1) * LANES]
                at += 1
    for side in range(2):
        for source in (decay_late, decay_early):
            for term in range(3):
                for i in range(thirds):
                    row = 3 * side + term
                    out[at : at + 1, :] = source[row : row + 1, i * LANES : (i + 1) * LANES]
                    at += 1


def small_out_kernel(own, got, table, gain, bias, rate, turn, skip, gate):
    layers, _, states = table.shape
    thirds = states // LANES
    width = gain.shape[1]
    per = width // LANES
    at = 0
    for out in (gain, bias, skip, gate):
        for layer in range(layers):
            for i in range(per):
                out[layer : layer + 1, i * LANES : (i + 1) * LANES] = own[at : at + 1, :] + got[at : at + 1, :]
                at += 1
    other = at + layers * 3 * thirds
    for layer in range(layers):
        for i in range(thirds):
            lanes = slice(i * LANES, (i + 1) * LANES)
            rows = [(layer * 3 + t) * thirds + i for t in range(3)]
            term_re, term_im, term_scale = (
                own[at + row : at + row + 1, :] + got[other + row : other + row + 1, :] for row in rows
            )
            re, im, scale, damping, step_size, rotation, square = (
                table[layer, t : t + 1, lanes] for t in range(7)
            )
            grad_re = (term_re * re - term_im * im) / square
            grad_im = (term_re * im + term_im * re) / square
            grad_scale = term_scale / scale
            grad_damping = grad_scale * square / scale - (grad_re * re + grad_im * im)
            grad_rotation = grad_im * re - grad_re * im
            log_rate = grad_damping * damping
            rate[layer : layer + 1, lanes] = log_rate
            turn[2 * layer : 2 * layer + 1, lanes] = grad_rotation * step_size
            turn[2 * layer + 1 : 2 * layer + 2, lanes] = log_rate + grad_rotation * rotation


class Order:
    def __init__(self):
        self.tile = None

    def run(self, kernel, outs, operands, scratch=(), flops=0, name=None, spare=8, after=(), free_outs=0, alias=None,
            semaphores=0, cost=0, far=False):
        whole = pl.BlockSpec(memory_space=pltpu.VMEM)
        free = pl.BlockSpec(memory_space=pl.ANY)
        waits = list(after) + ([] if self.tile is None else [self.tile])
        inputs, results = len(operands), len(outs)
        skipped = len(waits)

        def body(*refs):
            token = refs[skipped + inputs]
            token[...] = jnp.zeros_like(token)
            kernel(*refs[skipped : skipped + inputs], *refs[skipped + inputs + 1 :])

        shapes = [jax.ShapeDtypeStruct((8, LANES), f32)]
        shapes += [jax.ShapeDtypeStruct(shape, dtype) for shape, dtype in outs]
        held = sum(jnp.dtype(dtype).itemsize * functools.reduce(lambda a, b: a * b, shape) for shape, dtype in scratch)
        specs = [free] * skipped + [pl.BlockSpec(memory_space=pltpu.HBM) if far else whole] * inputs
        aliases = {}
        if alias is not None:
            for operand, out in alias.items():
                specs[skipped + operand] = free
                aliases[skipped + operand] = out + 1
        extra = [pltpu.SemaphoreType.DMA((semaphores,))] if semaphores else []
        results = pl.pallas_call(
            body,
            out_shape=shapes,
            in_specs=specs,
            out_specs=[whole] + [free] * free_outs + [whole] * (results - free_outs),
            scratch_shapes=[pltpu.VMEM(shape, dtype) for shape, dtype in scratch] + extra,
            input_output_aliases=aliases,
            compiler_params=pltpu.CompilerParams(vmem_limit_bytes=held + spare * 2**20),
            cost_estimate=pl.CostEstimate(flops=int(1 + cost * 1e9), bytes_accessed=int(1 + cost * 3e6), transcendentals=0),
            name=name,
        )(*waits, *operands)
        self.tile = results[0]
        return results[1:]


def swap(value):
    return lax.ppermute(value, "dir", [(0, 1), (1, 0)])


def across(value, bits):
    count = lax.axis_size("seq")
    return lax.ppermute(value, "seq", [(i, i ^ bits) for i in range(count)])


def beyond(value):
    bit = 4
    while (1 << bit) < lax.axis_size("seq"):
        value = (value.astype(f32) + across(value, 1 << bit).astype(f32)).astype(value.dtype)
        bit += 1
    return value


def exchanged(payload, row_devices):
    count = lax.axis_size("seq")
    group = 2 * row_devices
    groups = None
    if count != row_devices:
        groups = [list(range(i, i + group)) for i in range(0, 2 * count, group)]
    return lax.all_to_all(payload, ("seq", "dir"), 0, 0, tiled=True, axis_index_groups=groups)


def sent(parts, low_bit):
    return [parts[0]] + [across(parts[k], k << low_bit) for k in (1, 2, 3)]


def shared(value, low_bit):
    return [value] + [across(value, k << low_bit) for k in (1, 2, 3)]


def body(
    tokens,
    segment_ids,
    norm_gain,
    norm_bias,
    input_matrix,
    output_matrix,
    rate_params,
    turn_params,
    skip_weight,
    glu_weight,
    glu_bias,
    cotangent,
):
    chip_rows, width = tokens.shape
    rows = chip_rows // 2
    layers = rate_params.shape[0]
    states = rate_params.shape[2]
    row_devices = LENGTH // chip_rows
    order = Order()
    here = functools.partial

    in_own, out_own = input_matrix, output_matrix
    in_oth = swap(input_matrix)
    rate_oth, turn_oth = swap(rate_params), swap(turn_params)
    out_oth = swap(output_matrix)
    segments = segment_ids.reshape(chip_rows // LANES, LANES)

    full = ((rows, width), f32)
    full_low = ((rows, width), bf16)
    columns = ((width // LANES, rows, LANES), f32)
    wide = ((rows, 2 * states), f32)
    wide_low = ((rows, 2 * states), bf16)
    ends = ((8, 2 * states), f32)
    payload_shape = ((2 * row_devices, 16, LANES), f32)
    narrow = ((rows, LANES), f32)
    tile = ((8, LANES), f32)
    sums_shape = ((8, width), f32)
    decay_shape = ((8, states), f32)
    table_shape = ((layers, 16, states), f32)
    places = ((8, 2 * states), f32)
    in_size = width * (2 * states // LANES)
    out_size = 2 * states * (width // LANES)
    glu_size = width // 2 * (width // LANES)
    outer_size = out_size + glu_size
    outer_pack = ((outer_size, LANES), bf16)
    inner_pack = ((in_size, LANES), bf16)
    one = 2.0 * rows * width * 2 * states
    gate = 2.0 * rows * width * width
    scan = 1e9

    x0, normed0, inv0 = order.run(
        here(open_kernel, row_devices),
        [full, full, narrow],
        [tokens],
        [full_low, columns],
        far=True,
        semaphores=1,
        name="open_norm",
        cost=10,
    )
    (
        mixed0, drive_own0, drive_oth0, keep_own, keep_oth, whole, ends_own, ends_oth, payload, table, tiles, ids,
    ) = order.run(
        here(open_second_kernel, row_devices),
        [full_low, wide, wide, narrow, narrow, ((2, 8, LANES), f32), ends, ends, payload_shape, table_shape,
         ((layers, 16, LANES), f32), tile],
        [normed0, segments, norm_gain, norm_bias, rate_params, turn_params, rate_oth, turn_oth, in_own, in_oth],
        [tile],
        name="open_scan",
        after=[out_oth],
    )
    gathered = exchanged(payload, row_devices)
    (
        low_own0, low_oth0, combined0, phi0, sig0, act_low0, x1, normed1, inv1, mixed1, drive_own1, drive_oth1,
        ends_own, ends_oth, payload,
    ) = order.run(
        here(mid_kernel, row_devices),
        [wide_low, wide_low, full, full, full, full_low, full, full, narrow, full_low, wide, wide, ends, ends,
         payload_shape],
        [gathered, ends_own, ends_oth, drive_own0, drive_oth0, keep_own, keep_oth, whole, table, tiles,
         ids, out_own, out_oth, x0, normed0, norm_gain, norm_bias, skip_weight, glu_weight, glu_bias, in_own, in_oth],
        [places, tile, full, wide, wide],
        flops=4 * one + gate + 3 * scan,
        name="mid",
    )
    gathered = exchanged(payload, row_devices)
    (
        low_own1, low_oth1, out1, grad1, combined_grad1, grad_own1, grad_oth1, ends_own, ends_oth, payload,
        sums_turn, mine, theirs,
    ) = order.run(
        here(turn_kernel, row_devices),
        [wide_low, wide_low, full, full, full, wide, wide, ends, ends, payload_shape, sums_shape, outer_pack, outer_pack],
        [gathered, ends_own, ends_oth, drive_own1, drive_oth1, keep_own, keep_oth, whole, table, tiles,
         ids, out_own, out_oth, x1, normed1, norm_gain, norm_bias, skip_weight, glu_weight, glu_bias, cotangent],
        [places, tile, full, full, full, full, columns, wide, wide, full_low, full_low, full_low],
        flops=4 * one + 2 * gate + 4 * scan,
        name="turn",
    )
    got = swap(theirs)
    gathered = exchanged(payload, row_devices)
    early = order.run(
        early_cores_kernel, [((outer_size // 4, LANES), bf16)] * 4, [mine, got], name="early_cores", after=[gathered]
    )
    early = sent(early, 0)
    in_low_own1, in_low_oth1, decay_sums1, mine, theirs = order.run(
        here(scan_kernel, 1, row_devices),
        [wide_low, wide_low, decay_shape, inner_pack, inner_pack],
        [gathered, ends_own, ends_oth, grad_own1, grad_oth1, keep_own, keep_oth, whole, table, tiles,
         ids, low_own1, low_oth1, drive_own1, drive_oth1, mixed1],
        [places, tile, wide, wide],
        name="scan_one",
    )
    got = swap(theirs)
    (
        grad0, combined_grad0, grad_own0, grad_oth0, ends_own, ends_oth, payload, sums_back, mine_outer, theirs_outer,
    ) = order.run(
        here(back_kernel, row_devices),
        [full, full, wide, wide, ends, ends, payload_shape, sums_shape, outer_pack, outer_pack],
        [in_low_own1, in_low_oth1, keep_own, keep_oth, whole, table, tiles, ids, in_own, in_oth, out_own, out_oth, grad1,
         combined_grad1, normed1, inv1, norm_gain, norm_bias, skip_weight, glu_weight, combined0, phi0, sig0, normed0,
         act_low0, low_own0, low_oth0],
        [full, full_low, full_low],
        name="back",
    )
    got_outer = swap(theirs_outer)
    (payload,) = order.run(relay_kernel, [payload_shape], [payload], name="relay", after=early[1:], cost=RELAY)
    gathered = exchanged(payload, row_devices)
    inner = order.run(
        early_cores_kernel, [((in_size // 4, LANES), bf16)] * 4, [mine, got], name="inner_cores", after=[gathered, got_outer]
    )
    inner = sent(inner, 0)
    in_low_own0, in_low_oth0, decay_sums0, mine, theirs = order.run(
        here(scan_kernel, 0, row_devices),
        [wide_low, wide_low, decay_shape, inner_pack, inner_pack],
        [gathered, ends_own, ends_oth, grad_own0, grad_oth0, keep_own, keep_oth, whole, table, tiles,
         ids, low_own0, low_oth0, drive_own0, drive_oth0, mixed0],
        [places, tile, wide, wide],
        name="scan_zero",
    )
    got = swap(theirs)
    quarter = (outer_size + in_size) // 4
    halves, sums_last = order.run(
        final_kernel,
        [((2, rows, width), f32), sums_shape],
        [in_low_own0, in_low_oth0, in_own, in_oth, grad0, combined_grad0, normed0, inv0, norm_gain, skip_weight, out1],
        [full, columns, columns],
        name="final_norm",
    )
    quarter = (outer_size + in_size) // 4
    small_rows = -(-(4 * layers * (width // LANES) + 6 * layers * (states // LANES)) // 16) * 16
    small_shape = ((small_rows, LANES), f32)
    parts = order.run(
        here(first_plane_kernel, small_rows),
        [((quarter // 4, LANES), bf16)] * 4 + [((quarter + 2 * small_rows, LANES), bf16)] * 4 + [small_shape],
        early + inner + [mine_outer, got_outer, mine, got, sums_turn, sums_back, sums_last, decay_sums0, decay_sums1],
        name="first_plane",
        cost=RELAY,
    )
    first = sent(parts[:4], 2)
    second = sent(parts[4:8], 0)
    whole_rows = ((chip_rows, width), f32)
    block_output, tokens_grad = order.run(
        join_kernel, [whole_rows, whole_rows], [halves, swap(halves)], name="join"
    )
    (share,) = order.run(planes_kernel, [((quarter // 4, LANES), bf16)], first, name="first_planes")
    first = shared(beyond(share), 2)
    sizes = (outer_size // 16, in_size // 16)
    (full_quarter,) = order.run(
        here(gather_kernel, sizes), [((quarter, LANES), bf16)], first, name="first_gather"
    )
    first = shared(full_quarter, 0)
    *second, _ = order.run(
        here(second_plane_kernel, small_rows, outer_size // 4),
        [((quarter // 4 + 2 * small_rows, LANES), bf16)] * 4 + [((small_rows, LANES), f32)],
        second,
        name="second_plane",
    )
    second = sent(second, 2)
    share, small = order.run(
        here(second_planes_kernel, small_rows), [((quarter // 4, LANES), bf16), ((small_rows, LANES), f32)], second,
        name="second_planes",
    )
    second = shared(beyond(share), 2)
    small = beyond(small)
    got_small = swap(small)
    in_shape, out_shape = input_matrix.shape, output_matrix.shape

    def gate_part(quarters, name):
        (value,) = order.run(
            here(gate_part_kernel, outer_size // 4, out_size), [((glu_size, LANES), bf16)], quarters,
            [((outer_size, LANES), bf16)], name=name,
        )
        return value

    def unpack(quarters, layer, old, name):
        return order.run(
            here(unpack_kernel, layer, len(old), (outer_size // 4, in_size // 4)),
            [(out_shape, f32), (in_shape, f32)],
            quarters + old,
            [(out_shape[2:], f32), (in_shape[2:], f32), outer_pack, inner_pack],
            name=name,
            free_outs=2,
            alias={4 + i: i for i in range(len(old))},
            semaphores=2,
        )

    gate_one = gate_part(first, "gate_one")
    got_one = swap(gate_one)
    results = unpack(first, 1, [], "unpack_one")
    gain_grad, bias_grad, rate_grad, turn_grad, skip_grad, gate_grad = order.run(
        small_out_kernel,
        [((layers, width), f32), ((layers, width), f32), ((layers, states), f32), ((2 * layers, states), f32),
         ((layers, width), f32), ((layers, width), f32)],
        [small, got_small, table],
        name="small_out",
    )
    (full_quarter,) = order.run(
        here(gather_kernel, sizes), [((quarter, LANES), bf16)], second, name="second_gather"
    )
    second = shared(full_quarter, 0)
    gate_zero = gate_part(second, "gate_zero")
    got_zero = swap(gate_zero)
    out_all, in_all = unpack(second, 0, list(results), "unpack_zero")
    (glu_all,) = order.run(
        gate_kernel, [(glu_weight.shape, f32)], [gate_one, got_one, gate_zero, got_zero], name="unpack_gate"
    )
    return (
        block_output,
        tokens_grad,
        gain_grad,
        bias_grad,
        in_all,
        out_all,
        rate_grad.reshape(rate_params.shape),
        turn_grad.reshape(turn_params.shape),
        skip_grad,
        glu_all,
        gate_grad,
    )


def solution(mesh):
    return jax.shard_map(
        body,
        mesh=mesh,
        in_specs=(
            P("seq", None),
            P("seq"),
            P(),
            P(),
            P(None, "dir", None, None),
            P(None, "dir", None, None),
            P(None, "dir", None),
            P(None, "dir", None, None),
            P(),
            P(),
            P(),
            P("seq", None),
        ),
        out_specs=(
            P("seq", None),
            P("seq", None),
            P(),
            P(),
            P(None, "dir", None, None),
            P(None, "dir", None, None),
            P(None, "dir", None),
            P(None, "dir", None, None),
            P(),
            P(),
            P(),
        ),
        check_vma=False,
    )
```

```python
import functools

import jax
import jax.numpy as jnp
from jax import lax
from jax.experimental import pallas as pl
from jax.experimental.pallas import tpu as pltpu
from jax.sharding import PartitionSpec as P

LENGTH = 16384
LONGEST_RUN = 8192

eps = 1e-05
inv_root_two = 0.7071067811865476
inv_root_two_pi = 0.3989422804014327

f32 = jnp.float32
bf16 = jnp.bfloat16


LANES = 128
ELEMENT_ROWS = 512
UNROLL = 8
CORES_COST = 0


def core_place(row_devices):
    core = lax.axis_index("dir")
    return core, lax.rem(lax.axis_index("seq"), row_devices) * 2 + core


def dot(a, b):
    return jnp.dot(a, b, preferred_element_type=f32)


def dot_nt(a, b):
    return lax.dot_general(a, b, (((1,), (1,)), ((), ())), preferred_element_type=f32)


def dot_tn(a, b):
    return lax.dot_general(a, b, (((0,), (0,)), ((), ())), preferred_element_type=f32)


def squared(re, im, times):
    for _ in range(times):
        re, im = re * re - im * im, 2.0 * re * im
    return re, im


def over_blocks(rows, step, init=()):
    def one(i, carry):
        return step(pl.multiple_of(i * ELEMENT_ROWS, ELEMENT_ROWS), carry)

    return lax.fori_loop(0, rows // ELEMENT_ROWS, one, init)


def fold(values):
    total = values[0:8]
    for start in range(8, values.shape[0], 8):
        total = total + values[start : start + 8]
    return total


class Lanes:
    def __init__(self, rows_ref, tiles_ref, layer, adjoint, spans, rows):
        states = rows_ref.shape[2]
        self.states = states
        self.rows_ref, self.layer = rows_ref, layer
        flip = -1.0 if adjoint else 1.0
        self.step = []
        self.run = []
        self.block = []
        for side in range(2):
            row = 8 * side
            re = rows_ref[layer, row : row + 1, :]
            im = rows_ref[layer, row + 1 : row + 2, :] * flip
            self.step.append((jnp.broadcast_to(re, (8, states)), jnp.broadcast_to(im, (8, states))))
            self.run.append(squared(re, im, (spans - 1).bit_length()))
            thirds = states // LANES
            tile_re = tiles_ref[layer, 8 * side : 8 * side + thirds, :]
            tile_im = tiles_ref[layer, 8 * side + thirds : 8 * side + 2 * thirds, :] * flip
            self.block.append(squared(tile_re, tile_im, (rows - 1).bit_length()))

    def scaling(self, side):
        row = self.rows_ref[self.layer, 8 * side + 2 : 8 * side + 3, :]
        return jnp.concatenate([row, row], 1)


def sweep(first_forward, drives, masks, lanes, init, visit=None, totals=()):
    states = lanes.states
    span = drives[0].shape[0] // 8

    def step(i, carry):
        values, sums = carry
        up = pl.multiple_of(i * 8, 8)
        down = pl.multiple_of((span - 1 - i) * 8, 8)
        places = (jnp.where(first_forward, up, down), jnp.where(first_forward, down, up))
        new = []
        for side in range(2):
            rows = pl.ds(pl.multiple_of(places[side], 8), 8)
            keep = masks[side][rows, :]
            keep = jnp.concatenate([keep] * (states // LANES), 1)
            step_re, step_im = lanes.step[side]
            step_re, step_im = step_re * keep, step_im * keep
            re, im = values[side]
            drive_re = drives[side][rows, :states]
            drive_im = drives[side][rows, states:]
            re, im = (
                step_re * re - step_im * im + drive_re,
                step_re * im + step_im * re + drive_im,
            )
            new.append((re, im))
            if visit is not None:
                sums = visit(side, rows, re, im, sums)
        return tuple(new), sums

    return lax.fori_loop(0, span, step, (init, totals), unroll=UNROLL)


def run_chain(first_up, lanes, side, ends, whole, start, places):
    states = lanes.states
    power_re, power_im = lanes.run[side]
    re, im = start
    for i in range(8):
        s = jnp.where(first_up, i, 7 - i)
        row = pl.ds(s, 1)
        if places is not None:
            places[row, :states] = re
            places[row, states:] = im
        passes = whole[row, :]
        passes = jnp.concatenate([passes] * (states // LANES), 1)
        pass_re, pass_im = power_re * passes, power_im * passes
        end_re, end_im = ends[row, :states], ends[row, states:]
        re, im = (end_re + pass_re * re - pass_im * im, end_im + pass_re * im + pass_im * re)
    return re, im


def first_pass(running_up, place, drives, masks, wholes, lanes, ids_ref, ends, payload):
    states = lanes.states
    thirds = states // LANES
    nothing = jnp.zeros((8, states), f32)
    zero = (nothing, nothing)
    values, _ = sweep(running_up, drives, masks, lanes, (zero, zero))
    tiles = []
    for side in range(2):
        ends[side][:, :states] = values[side][0]
        ends[side][:, states:] = values[side][1]
        upward = running_up if side == 0 else jnp.logical_not(running_up)
        start = jnp.zeros((1, states), f32)
        re, im = run_chain(upward, lanes, side, ends[side], wholes[side], (start, start), None)
        for i in range(thirds):
            payload[side, i : i + 1, :] = re[:, LANES * i : LANES * (i + 1)]
            payload[side, thirds + i : thirds + i + 1, :] = im[:, LANES * i : LANES * (i + 1)]
        payload[side, 6:8, :] = ids_ref[0:2, :]
    first, second = payload[0], payload[1]
    for i in range(payload.shape[0]):
        to_later = jnp.logical_xor(running_up, i < place)
        payload[i] = jnp.where(to_later, first, second)


def entering(upward, place, lanes, side, gathered, ids_ref, small):
    states = lanes.states
    thirds = states // LANES
    count = gathered.shape[0]
    rows = lanes.token_rows
    block_re, block_im = lanes.block[side]
    re = jnp.zeros((thirds, LANES), f32)
    im = jnp.zeros((thirds, LANES), f32)
    key = jnp.where(upward, ids_ref[0:1, :], ids_ref[1:2, :])
    for distance in range(min(count - 1, LONGEST_RUN // rows), 0, -1):
        source = jnp.where(upward, place - distance, place + distance)
        inside = jnp.logical_and(source >= 0, source < count)
        source = jnp.clip(source, 0, count - 1)
        sent_re = gathered[source, 0:thirds, :]
        sent_im = gathered[source, thirds : 2 * thirds, :]
        sent_key = gathered[source, pl.ds(jnp.where(upward, 7, 6), 1), :]
        joined = jnp.where(jnp.logical_and(sent_key == key, inside), 1.0, 0.0)
        re, im = (
            joined * sent_re + block_re * re - block_im * im,
            joined * sent_im + block_re * im + block_im * re,
        )
    small[0:thirds, :] = re
    small[thirds : 2 * thirds, :] = im
    wide_re = jnp.concatenate([small[i : i + 1, :] for i in range(thirds)], 1)
    wide_im = jnp.concatenate([small[thirds + i : thirds + i + 1, :] for i in range(thirds)], 1)
    return wide_re, wide_im


def second_starts(running_up, place, lanes, gathered, ids_ref, ends, wholes, places, small):
    init = []
    states = lanes.states
    for side in range(2):
        upward = running_up if side == 0 else jnp.logical_not(running_up)
        start = entering(upward, place, lanes, side, gathered, ids_ref, small)
        run_chain(upward, lanes, side, ends[side], wholes[side], start, places)
        init.append((places[:, :states], places[:, states:]))
    return tuple(init)


def make_lanes(rows_ref, tiles_ref, layer, adjoint, token_rows):
    lanes = Lanes(rows_ref, tiles_ref, layer, adjoint, token_rows // 8, token_rows)
    lanes.token_rows = token_rows
    return lanes


def standardise(x):
    width = x.shape[1]
    average = jnp.sum(x, 1, keepdims=True) * (1.0 / width)
    centred = x - average
    inv_scale = lax.rsqrt(jnp.sum(centred * centred, 1, keepdims=True) * (1.0 / width) + eps)
    return centred * inv_scale, inv_scale


def fill_columns(columns, values):
    for i in range(columns.shape[0]):
        columns[i] = values[:, i * LANES : (i + 1) * LANES].astype(columns.dtype)


def tile_order(columns, first, count, span):
    tiles = [
        jnp.concatenate([columns[i, pl.ds(first + j, 8, stride=span), :] for i in range(columns.shape[0])], 1)
        for j in range(count)
    ]
    return jnp.concatenate(tiles, 0)


def store_token_order(columns, first, values, span):
    for j in range(values.shape[0] // 8):
        for i in range(columns.shape[0]):
            columns[i, pl.ds(first + j, 8, stride=span), :] = values[8 * j : 8 * j + 8, i * LANES : (i + 1) * LANES]


def join_columns(out, columns):
    for i in range(columns.shape[0]):
        out[:, i * LANES : (i + 1) * LANES] = columns[i]


def one_minus_exp(x):
    series = jnp.ones_like(x)
    for term in range(12, 1, -1):
        series = 1.0 - x * (1.0 / term) * series
    return jnp.where(x < 0.5, x * series, 1.0 - jnp.exp(-x))


def table_rows(table, layer, base, rate, turn):
    frequency = turn[layer, 0, 0:1, :]
    log_step = turn[layer, 0, 1:2, :]
    step_size = jnp.exp(log_step)
    damping = jnp.exp(rate[layer, 0:1, :] + log_step)
    magnitude = jnp.exp(-damping)
    rotation = frequency * step_size
    square = magnitude * magnitude
    rows = (
        magnitude * jnp.cos(rotation), magnitude * jnp.sin(rotation), jnp.sqrt(one_minus_exp(2.0 * damping)), damping,
        step_size, rotation, square,
    )
    for i, row in enumerate(rows):
        table[layer, base + i : base + i + 1, :] = row


def open_kernel(row_devices, tokens_from, x_out, normed_out, inv_out, tokens, natural, sems):
    copy = pltpu.make_async_copy(
        tokens_from.at[part_rows(lax.axis_index("dir"), tokens.shape[0])], tokens, sems.at[0]
    )
    copy.start()
    copy.wait()
    rows = x_out.shape[0]
    span = rows // 8
    fill_columns(natural, tokens[...].astype(f32))

    def element(start, carry):
        x = tile_order(natural, start // 8, ELEMENT_ROWS // 8, span)
        normed, inv_scale = standardise(x)
        block = pl.ds(start, ELEMENT_ROWS)
        x_out[block, :] = x
        normed_out[block, :] = normed
        inv_out[block, :] = jnp.broadcast_to(inv_scale, (ELEMENT_ROWS, LANES))
        return carry

    over_blocks(rows, element)


def open_second_kernel(
    row_devices,
    normed,
    segments,
    gain,
    bias,
    rate,
    turn,
    rate_oth,
    turn_oth,
    in_own,
    in_oth,
    mixed_low,
    drive_own,
    drive_oth,
    keep_own,
    keep_oth,
    whole_out,
    ends_own,
    ends_oth,
    payload,
    table,
    tiles,
    ids,
    rows8,
):
    core, place = core_place(row_devices)
    rows = normed.shape[0]
    span = rows // 8

    def element(start, carry):
        block = pl.ds(start, ELEMENT_ROWS)
        mixed_low[block, :] = (normed[block, :] * gain[0:1, :] + bias[0:1, :]).astype(bf16)
        return carry

    over_blocks(rows, element)
    table[...] = jnp.zeros_like(table)
    tiles[...] = jnp.zeros_like(tiles)
    thirds = table.shape[2] // LANES
    for layer in range(table.shape[0]):
        table_rows(table, layer, 0, rate, turn)
        table_rows(table, layer, 8, rate_oth, turn_oth)
        for side in range(2):
            for part in range(2):
                for i in range(thirds):
                    at = 8 * side + part * thirds + i
                    tiles[layer, at : at + 1, :] = table[
                        layer, 8 * side + part : 8 * side + part + 1, i * LANES : (i + 1) * LANES
                    ]

    number = segments[...].astype(f32)
    count = number.shape[0]
    lane = lax.broadcasted_iota(jnp.int32, number.shape, 1)
    row = lax.broadcasted_iota(jnp.int32, number.shape, 0)
    back = pltpu.roll(number, 1, 1)
    back = jnp.where(lane == 0, pltpu.roll(back, 1, 0), back)
    ahead = pltpu.roll(number, LANES - 1, 1)
    ahead = jnp.where(lane == LANES - 1, pltpu.roll(ahead, count - 1, 0), ahead)
    edge_first = jnp.logical_and(lane == 0, row == 0)
    edge_last = jnp.logical_and(lane == LANES - 1, row == count - 1)
    up_keep = jnp.where(jnp.logical_or(number == back, edge_first), 1.0, 0.0)
    down_keep = jnp.where(jnp.logical_or(number == ahead, edge_last), 1.0, 0.0)
    per = LANES // span
    used = 8 // per
    for side, out in ((0, keep_own), (1, keep_oth)):
        rows8[0:count, :] = jnp.where(core == side, up_keep, down_keep)
        half = rows8[pl.ds(core * used, used), :]
        runs = jnp.concatenate([half[s // per : s // per + 1] for s in range(8)], 0)
        place = lax.broadcasted_iota(jnp.int32, (8, LANES), 1)
        sub = lax.broadcasted_iota(jnp.int32, (8, LANES), 0)
        first = lax.rem(sub, per) * span
        inside = jnp.logical_and(place >= first, place < first + span)
        least = jnp.min(jnp.where(inside, runs, 1.0), 1, keepdims=True)
        whole_out[side] = jnp.broadcast_to(least, (8, LANES))
        step = lax.broadcasted_iota(jnp.int32, (span, 8, LANES), 0)
        spread = jnp.where(step == (place - first)[None], runs[None], 0.0)
        spread = spread.reshape(span * 8, LANES).astype(bf16)
        out[...] = dot(spread, jnp.ones((LANES, LANES), bf16))
    rows8[0:count, :] = number
    first_row = rows8[pl.ds(core * used, 1), :]
    last_row = rows8[pl.ds(core * used + used - 1, 1), :]
    ids[...] = jnp.zeros_like(ids)
    ids[0:1, :] = jnp.broadcast_to(first_row[:, 0:1], (1, LANES))
    ids[1:2, :] = jnp.broadcast_to(last_row[:, LANES - 1 : LANES], (1, LANES))
    for side, (matrix, drive) in enumerate(((in_own, drive_own), (in_oth, drive_oth))):
        scale = table[0, 8 * side + 2 : 8 * side + 3, :]
        drive[...] = dot(mixed_low[...], matrix[0, 0]) * jnp.concatenate([scale, scale], 1)
    lanes = make_lanes(table, tiles, 0, False, rows)
    first_pass(
        core == 0,
        core_place(row_devices)[1],
        (drive_own, drive_oth),
        (keep_own, keep_oth),
        (whole_out.at[0], whole_out.at[1]),
        lanes,
        ids,
        (ends_own, ends_oth),
        payload,
    )


def forward_states(layer, info, gathered, ends, drives, masks, whole, rows_ref, tiles_ref, ids, states, lows, places, small):
    rows = drives[0].shape[0]
    lanes = make_lanes(rows_ref, tiles_ref, layer, False, rows)
    core, place = info
    running_up = core == 0
    init = second_starts(
        running_up, place, lanes, gathered, ids, ends, (whole.at[0], whole.at[1]), places, small
    )
    width = lanes.states

    def visit(side, where, re, im, sums):
        states[side][where, :width] = re
        states[side][where, width:] = im
        return sums

    sweep(running_up, drives, masks, lanes, init, visit)
    for side in range(2):
        lows[side][...] = states[side][...].astype(bf16)


def mid_kernel(
    row_devices,
    gathered,
    ends_own,
    ends_oth,
    drive_own,
    drive_oth,
    keep_own,
    keep_oth,
    whole,
    rows_ref,
    tiles_ref,
    ids,
    out_own,
    out_oth,
    x_in,
    normed,
    gain,
    bias,
    skip,
    glu,
    glu_bias,
    in_own,
    in_oth,
    low_own,
    low_oth,
    combined_out,
    phi_out,
    sig_out,
    act_low,
    x_out,
    normed_out,
    inv_out,
    mixed_out,
    next_own,
    next_oth,
    next_ends_own,
    next_ends_oth,
    payload,
    places,
    small,
    wide,
    states_own,
    states_oth,
):
    info = core_place(row_devices)
    rows = x_in.shape[0]
    masks = (keep_own, keep_oth)
    forward_states(
        0, info, gathered, (ends_own, ends_oth), (drive_own, drive_oth), masks, whole, rows_ref, tiles_ref,
        ids, (states_own, states_oth), (low_own, low_oth), places, small,
    )
    wide[...] = dot(low_own[...], out_own[0, 0]) + dot(low_oth[...], out_oth[0, 0])

    def element(start, carry):
        block = pl.ds(start, ELEMENT_ROWS)
        mixed = normed[block, :] * gain[0:1, :] + bias[0:1, :]
        combined = wide[block, :] + skip[0:1, :] * mixed
        phi = 0.5 * (1.0 + lax.erf(combined * inv_root_two))
        combined_out[block, :] = combined
        phi_out[block, :] = phi
        act_low[block, :] = (combined * phi).astype(bf16)
        return carry

    over_blocks(rows, element)
    wide[...] = dot(act_low[...], glu[0])

    def element_two(start, carry):
        block = pl.ds(start, ELEMENT_ROWS)
        sig = jax.nn.sigmoid(wide[block, :] + glu_bias[0:1, :])
        sig_out[block, :] = sig
        x = x_in[block, :] + combined_out[block, :] * phi_out[block, :] * sig
        x_out[block, :] = x
        after, inv_scale = standardise(x)
        normed_out[block, :] = after
        inv_out[block, :] = jnp.broadcast_to(inv_scale, (ELEMENT_ROWS, LANES))
        mixed_out[block, :] = (after * gain[1:2, :] + bias[1:2, :]).astype(bf16)
        return carry

    over_blocks(rows, element_two)
    for side, (matrix, out) in enumerate(((in_own, next_own), (in_oth, next_oth))):
        scale = rows_ref[1, 8 * side + 2 : 8 * side + 3, :]
        out[...] = dot(mixed_out[...], matrix[1, 0]) * jnp.concatenate([scale, scale], 1)
    lanes = make_lanes(rows_ref, tiles_ref, 1, False, rows)
    first_pass(
        info[0] == 0,
        info[1],
        (next_own, next_oth),
        masks,
        (whole.at[0], whole.at[1]),
        lanes,
        ids,
        (next_ends_own, next_ends_oth),
        payload,
    )


def backward_half(
    layer, info, grad, combined, phi, sig, normed, gain, bias, skip, glu, out_own, out_oth, masks, whole,
    rows_ref, tiles_ref, ids, gate_low, combined_grad, combined_low, grad_own, grad_oth, ends, payload, sums, wide,
):
    rows = grad.shape[0]
    width = grad.shape[1]
    zero = jnp.zeros((8, width), f32)

    def element(start, carry):
        block = pl.ds(start, ELEMENT_ROWS)
        gate = sig[block, :]
        gate_grad = grad[block, :] * (combined[block, :] * phi[block, :]) * gate * (1.0 - gate)
        gate_low[block, :] = gate_grad.astype(bf16)
        return carry + fold(gate_grad)

    bias_sum = over_blocks(rows, element, zero)
    wide[...] = dot_nt(gate_low[...], glu[layer])

    def element_two(start, carry):
        block = pl.ds(start, ELEMENT_ROWS)
        value = combined[block, :]
        activation_grad = grad[block, :] * sig[block, :] + wide[block, :]
        slope = phi[block, :] + value * (jnp.exp(-0.5 * value * value) * inv_root_two_pi)
        result = activation_grad * slope
        combined_grad[block, :] = result
        combined_low[block, :] = result.astype(bf16)
        mixed = normed[block, :] * gain[layer : layer + 1, :] + bias[layer : layer + 1, :]
        return carry + fold(result * mixed)

    skip_sum = over_blocks(rows, element_two, zero)
    sums[0:1, :] = jnp.sum(bias_sum, 0, keepdims=True)
    sums[1:2, :] = jnp.sum(skip_sum, 0, keepdims=True)
    grad_own[...] = dot_nt(combined_low[...], out_own[layer, 0])
    grad_oth[...] = dot_nt(combined_low[...], out_oth[layer, 0])
    lanes = make_lanes(rows_ref, tiles_ref, layer, True, rows)
    first_pass(
        info[0] == 1,
        info[1],
        (grad_own, grad_oth),
        (masks[1], masks[0]),
        (whole.at[1], whole.at[0]),
        lanes,
        ids,
        ends,
        payload,
    )


def turn_kernel(
    row_devices,
    gathered,
    ends_own,
    ends_oth,
    drive_own,
    drive_oth,
    keep_own,
    keep_oth,
    whole,
    rows_ref,
    tiles_ref,
    ids,
    out_own,
    out_oth,
    x_in,
    normed,
    gain,
    bias,
    skip,
    glu,
    glu_bias,
    cotangent,
    low_own,
    low_oth,
    block_out,
    grad_out,
    combined_grad,
    grad_own,
    grad_oth,
    next_ends_own,
    next_ends_oth,
    payload,
    sums,
    mine,
    theirs,
    places,
    small,
    wide,
    combined,
    phi_rows,
    sig_rows,
    natural,
    states_own,
    states_oth,
    act_low,
    gate_low,
    combined_low,
):
    info = core_place(row_devices)
    rows = x_in.shape[0]
    span = rows // 8
    masks = (keep_own, keep_oth)
    forward_states(
        1, info, gathered, (ends_own, ends_oth), (drive_own, drive_oth), masks, whole, rows_ref, tiles_ref,
        ids, (states_own, states_oth), (low_own, low_oth), places, small,
    )
    wide[...] = dot(low_own[...], out_own[1, 0]) + dot(low_oth[...], out_oth[1, 0])

    def element(start, carry):
        block = pl.ds(start, ELEMENT_ROWS)
        mixed = normed[block, :] * gain[1:2, :] + bias[1:2, :]
        value = wide[block, :] + skip[1:2, :] * mixed
        phi = 0.5 * (1.0 + lax.erf(value * inv_root_two))
        combined[block, :] = value
        phi_rows[block, :] = phi
        act_low[block, :] = (value * phi).astype(bf16)
        return carry

    over_blocks(rows, element)
    wide[...] = dot(act_low[...], glu[1])
    base = pl.multiple_of(info[0] * rows, rows)
    fill_columns(natural, cotangent[pl.ds(base, rows), :])

    def element_two(start, carry):
        block = pl.ds(start, ELEMENT_ROWS)
        sig = jax.nn.sigmoid(wide[block, :] + glu_bias[1:2, :])
        sig_rows[block, :] = sig
        block_out[block, :] = x_in[block, :] + combined[block, :] * phi_rows[block, :] * sig
        grad_out[block, :] = tile_order(natural, start // 8, ELEMENT_ROWS // 8, span)
        return carry

    over_blocks(rows, element_two)
    sums[...] = jnp.zeros_like(sums)
    backward_half(
        1, info, grad_out, combined, phi_rows, sig_rows, normed, gain, bias, skip, glu, out_own, out_oth, masks,
        whole, rows_ref, tiles_ref, ids, gate_low, combined_grad, combined_low, grad_own, grad_oth,
        (next_ends_own, next_ends_oth), payload, sums, wide,
    )
    gradient_pack(act_low, gate_low, combined_low, low_own, low_oth, mine, theirs, wide)


def adjoint_states(
    layer, info, gathered, ends, grads, masks, whole, rows_ref, tiles_ref, ids, states, drives, lows, decay_sums,
    adjoints, places, small,
):
    rows = grads[0].shape[0]
    lanes = make_lanes(rows_ref, tiles_ref, layer, True, rows)
    core, place = info
    running_up = core == 1
    init = second_starts(
        running_up, place, lanes, gathered, ids, ends, (whole.at[1], whole.at[0]), places, small
    )
    width = lanes.states
    zero = jnp.zeros((8, width), f32)
    for side in range(2):
        adjoints[side][...] = states[side][...].astype(f32)

    def visit(side, where, re, im, sums):
        drive_re, drive_im = drives[side][where, :width], drives[side][where, width:]
        moved_re = adjoints[side][where, :width] - drive_re
        moved_im = adjoints[side][where, width:] - drive_im
        adjoints[side][where, :width] = re
        adjoints[side][where, width:] = im
        mine = sums[side]
        mine = (
            mine[0] + (re * moved_re + im * moved_im),
            mine[1] + (im * moved_re - re * moved_im),
            mine[2] + (re * drive_re + im * drive_im),
        )
        return (mine, sums[1]) if side == 0 else (sums[0], mine)

    _, sums = sweep(
        running_up, grads, (masks[1], masks[0]), lanes, init, visit, ((zero, zero, zero), (zero, zero, zero))
    )
    decay_sums[...] = jnp.zeros_like(decay_sums)
    for side in range(2):
        for i in range(3):
            decay_sums[3 * side + i : 3 * side + i + 1, :] = jnp.sum(sums[side][i], 0, keepdims=True)
        lows[side][...] = (adjoints[side][...] * lanes.scaling(side)).astype(bf16)


def norm_backward(
    layer, low_own, low_oth, in_own, in_oth, grad, combined_grad, normed, inv_scale, gain, skip, sums, wide, finish
):
    rows, width = grad.shape
    wide[...] = dot_nt(low_own[...], in_own[layer, 0]) + dot_nt(low_oth[...], in_oth[layer, 0])
    zero = jnp.zeros((8, width), f32)

    def element(start, carry):
        block = pl.ds(start, ELEMENT_ROWS)
        mixed_grad = wide[block, :] + combined_grad[block, :] * skip[layer : layer + 1, :]
        unit = normed[block, :]
        weighted = mixed_grad * unit
        inner = mixed_grad * gain[layer : layer + 1, :]
        mean_one = jnp.sum(inner, 1, keepdims=True) * (1.0 / width)
        mean_two = jnp.sum(weighted * gain[layer : layer + 1, :], 1, keepdims=True) * (1.0 / width)
        spread = jnp.concatenate([inv_scale[block, :]] * (width // LANES), 1)
        finish(start, grad[block, :] + spread * (inner - mean_one - unit * mean_two))
        return carry[0] + fold(weighted), carry[1] + fold(mixed_grad)

    gain_sum, bias_sum = over_blocks(rows, element, (zero, zero))
    sums[2:3, :] = jnp.sum(gain_sum, 0, keepdims=True)
    sums[3:4, :] = jnp.sum(bias_sum, 0, keepdims=True)


def back_kernel(
    row_devices,
    in_low_own,
    in_low_oth,
    keep_own,
    keep_oth,
    whole,
    rows_ref,
    tiles_ref,
    ids,
    in_own,
    in_oth,
    out_own,
    out_oth,
    grad_in,
    combined_grad_in,
    normed_in,
    inv_in,
    gain,
    bias,
    skip,
    glu,
    combined,
    phi,
    sig,
    normed,
    act_low,
    low_own,
    low_oth,
    grad_out,
    combined_grad,
    next_own,
    next_oth,
    next_ends_own,
    next_ends_oth,
    payload,
    sums,
    mine,
    theirs,
    wide,
    gate_low,
    combined_low,
):
    info = core_place(row_devices)
    masks = (keep_own, keep_oth)
    sums[...] = jnp.zeros_like(sums)

    def finish(start, value):
        grad_out[pl.ds(start, ELEMENT_ROWS), :] = value

    norm_backward(
        1, in_low_own, in_low_oth, in_own, in_oth, grad_in, combined_grad_in, normed_in, inv_in, gain, skip, sums, wide,
        finish,
    )
    backward_half(
        0, info, grad_out, combined, phi, sig, normed, gain, bias, skip, glu, out_own, out_oth, masks, whole,
        rows_ref, tiles_ref, ids, gate_low, combined_grad, combined_low, next_own, next_oth,
        (next_ends_own, next_ends_oth), payload, sums, wide,
    )
    gradient_pack(act_low, gate_low, combined_low, low_own, low_oth, mine, theirs, wide)


def scan_kernel(
    layer,
    row_devices,
    gathered,
    ends_own,
    ends_oth,
    grad_own,
    grad_oth,
    keep_own,
    keep_oth,
    whole,
    rows_ref,
    tiles_ref,
    ids,
    states_own,
    states_oth,
    drive_own,
    drive_oth,
    mixed_low,
    low_own,
    low_oth,
    decay_sums,
    mine,
    theirs,
    places,
    small,
    adjoint_own,
    adjoint_oth,
):
    info = core_place(row_devices)
    masks = (keep_own, keep_oth)
    adjoint_states(
        layer, info, gathered, (ends_own, ends_oth), (grad_own, grad_oth), masks, whole, rows_ref, tiles_ref, ids,
        (states_own, states_oth), (drive_own, drive_oth), (low_own, low_oth), decay_sums,
        (adjoint_own, adjoint_oth), places, small,
    )
    store_columns(mine, 0, dot_tn(mixed_low[...], low_own[...]))
    store_columns(theirs, 0, dot_tn(mixed_low[...], low_oth[...]))


def final_kernel(
    low_own, low_oth, in_own, in_oth, grad_in, combined_grad, normed, inv_scale, gain, skip, block_out, halves, sums, wide,
    *columns,
):
    rows = grad_in.shape[0]
    sums[...] = jnp.zeros_like(sums)

    def finish(start, value):
        store_token_order(columns[1], start // 8, value, rows // 8)

    norm_backward(
        0, low_own, low_oth, in_own, in_oth, grad_in, combined_grad, normed, inv_scale, gain, skip, sums, wide, finish
    )
    store_token_order(columns[0], 0, block_out[...], rows // 8)
    for i in range(2):
        join_columns(halves.at[i], columns[i])


def store_columns(out, first, values):
    rows, width = values.shape
    for i in range(width // LANES):
        out[first + i * rows : first + (i + 1) * rows, :] = values[:, i * LANES : (i + 1) * LANES].astype(out.dtype)


def half_rows(core, act_low, gate_low, mine, theirs, first, wide):
    wide[...] = dot_tn(act_low[...], gate_low[...])
    half = wide.shape[0] // 2
    width = wide.shape[1]
    for out, which in ((mine, core), (theirs, 1 - core)):
        rows = pl.ds(pl.multiple_of(which * half, half), half)
        for i in range(width // LANES):
            out[first + i * half : first + (i + 1) * half, :] = wide[rows, i * LANES : (i + 1) * LANES].astype(out.dtype)


def gradient_pack(act_low, gate_low, combined_low, low_own, low_oth, mine, theirs, wide):
    store_columns(theirs, 0, dot_tn(low_oth[...], combined_low[...]))
    store_columns(mine, 0, dot_tn(low_own[...], combined_low[...]))
    size = low_own.shape[1] * (combined_low.shape[1] // LANES)
    half_rows(lax.axis_index("dir"), act_low, gate_low, mine, theirs, size, wide)


def slot(low_bit, parts):
    return jnp.bitwise_and(jnp.right_shift(lax.axis_index("seq"), low_bit), parts - 1)


def paired(values):
    while len(values) > 1:
        values = [a + b for a, b in zip(values[::2], values[1::2])]
    return values[0]


def part_rows(index, rows):
    return pl.ds(pl.multiple_of(index * rows, rows), rows)


def sum_parts(groups, outs, low_bit):
    parts = len(outs)
    mine = slot(low_bit, parts)
    for k, out in enumerate(outs):
        first = 0
        for rows, sources in groups:
            share = rows // parts
            where = part_rows(jnp.bitwise_xor(mine, k), share)
            total = paired([source[where, :].astype(f32) for source in sources])
            out[first : first + share, :] = total.astype(out.dtype)
            first += share


def gather_parts(sizes, sources, low_bit, outs):
    mine = slot(low_bit, len(sources))
    for k, source in enumerate(sources):
        first = 0
        for rows, out in zip(sizes, outs):
            out[part_rows(jnp.bitwise_xor(mine, k), rows), :] = source[first : first + rows, :]
            first += rows


def relay_kernel(payload_in, payload):
    payload[...] = payload_in[...]


def add_rows(out, at, sources, start, rows):
    where = pl.ds(pl.multiple_of(start, rows), rows)
    out[at : at + rows, :] = paired([source[where, :].astype(f32) for source in sources]).astype(out.dtype)


def put_small(outs, first, value):
    for out in outs:
        out[first : first + value.shape[0], :] = value.astype(out.dtype)


def half_groups(outer, inner, side):
    return ((outer // 2, side * (outer // 2)), (inner // 2, side * (inner // 2)))


def cores_kernel(outer_half, half, outer, got_outer, inner, got_inner, *refs):
    small_sums, (a_keep, a_send, b_keep, b_send), small = refs[:-5], refs[-5:-1], refs[-1]
    outer_rows, inner_rows = 2 * outer_half, 2 * (half - outer_half)
    mine = slot(0, 4)
    for side, out, parts in ((0, a_keep, (0, 2)), (0, a_send, (1, 3)), (1, b_keep, (0, 1)), (1, b_send, (2, 3))):
        (rows_one, at_one), (rows_two, at_two) = half_groups(outer_rows, inner_rows, side)
        for place, k in enumerate(parts):
            which = jnp.bitwise_xor(mine, k)
            add_rows(out, place * half, [outer, got_outer], which * outer_rows + at_one, rows_one)
            add_rows(out, place * half + rows_one, [inner, got_inner], which * inner_rows + at_two, rows_two)
    if small_sums:
        small_pack(*small_sums, small)
        put_small((a_keep, a_send), 2 * half, small[...])


def half_kernel(half, a_own, a_got, b_own, b_got, a_keep, a_send, b_keep, b_send):
    for own, got, outs in ((a_own, a_got, (a_keep, a_send)), (b_own, b_got, (b_keep, b_send))):
        for i, out in enumerate(outs):
            add_rows(out, 0, [own, got], i * half, half)
    if a_own.shape[0] > 2 * half:
        put_small((a_keep, a_send), half, a_own[2 * half :, :].astype(f32) + a_got[2 * half :, :].astype(f32))


def plane_kernel(half, outer_half, a_own, a_got, b_own, b_got, *outs):
    groups = []
    for own, got in ((a_own, a_got), (b_own, b_got)):
        groups.append((outer_half, [own.at[0:outer_half], got.at[0:outer_half]]))
        groups.append((half - outer_half, [own.at[outer_half:half], got.at[outer_half:half]]))
    sum_parts(groups, outs, 2)
    if a_own.shape[0] > half:
        put_small(outs, half // 2, a_own[half:, :].astype(f32) + a_got[half:, :].astype(f32))


def planes_kernel(*refs):
    refs[-1][...] = paired([source[...].astype(f32) for source in refs[:-1]]).astype(bf16)


def second_planes_kernel(*refs):
    sources, out, small = refs[:-2], refs[-2], refs[-1]
    rows = out.shape[0]
    out[...] = paired([source[0:rows, :].astype(f32) for source in sources]).astype(bf16)
    small[...] = paired([source[rows:, :].astype(f32) for source in sources])


def gather_kernel(outer_half, *refs):
    sources, outs = refs[:4], refs[4:]
    half = outs[0].shape[0]
    sizes, places = [], []
    for out in outs:
        sizes += [outer_half // 4, (half - outer_half) // 4]
        places += [out.at[0:outer_half], out.at[outer_half:half]]
    gather_parts(sizes, sources, 2, places)


def pair_kernel(a_own, a_got, b_own, b_got, a_out, b_out):
    half = a_own.shape[0]
    for own, got, out in ((a_own, a_got, a_out), (b_own, b_got, b_out)):
        out[0:half, :] = own[...]
        out[half : 2 * half, :] = got[...]


def last_pair_kernel(a_own, a_got, b_own, b_got, through, through_out, a_out, b_out):
    pair_kernel(a_own, a_got, b_own, b_got, a_out, b_out)


def assemble(outer_half, a_own, a_got, b_own, b_got, outer, inner):
    half = a_own.shape[0] // 2
    mine = slot(0, 4)
    for side, sources in ((0, (a_own, a_got, a_own, a_got)), (1, (b_own, b_own, b_got, b_got))):
        second = (0, 0, 1, 1) if side == 0 else (0, 1, 0, 1)
        for k, source in enumerate(sources):
            which = jnp.bitwise_xor(mine, k)
            first = second[k] * half
            rows = outer_half
            outer[part_rows(2 * which + side, rows), :] = source[first : first + rows, :]
            if inner is not None:
                rows = half - outer_half
                inner[part_rows(2 * which + side, rows), :] = source[first + outer_half : first + half, :]


def join_kernel(mine, theirs, *outs):
    core = lax.axis_index("dir")
    rows = mine.shape[1]
    for i, out in enumerate(outs):
        out[part_rows(core, rows), :] = mine[i]
        out[part_rows(1 - core, rows), :] = theirs[i]


def matrix_columns(source, first, out):
    rows, width = out.shape
    for i in range(width // LANES):
        out[:, i * LANES : (i + 1) * LANES] = source[first + i * rows : first + (i + 1) * rows, :].astype(f32)


def gate_part_kernel(outer_half, first, *refs):
    sources, out, whole = refs[:-2], refs[-2], refs[-1]
    assemble(outer_half, *sources, whole, None)
    out[...] = whole[first : first + out.shape[0], :]


def unpack_kernel(layer, olds, outer_half, *refs):
    refs = list(refs)
    take = lambda n: [refs.pop(0) for _ in range(n)]
    sources = take(4)
    take(olds)
    outs = take(2)
    buffers = take(2)
    whole = take(2)
    (sems,) = refs
    assemble(outer_half, *sources, *whole)
    copies = []
    for i in range(2):
        matrix_columns(whole[i], 0, buffers[i])
        copies.append(pltpu.make_async_copy(buffers[i], outs[i].at[layer, 0], sems.at[i]))
        copies[-1].start()
    for copy in copies:
        copy.wait()


def gate_kernel(layer, *refs):
    mine, theirs, (out, buffer, sems) = refs[0], refs[1], refs[-3:]
    core = lax.axis_index("dir")
    half = buffer.shape[0] // 2
    width = buffer.shape[1]
    for source, which in ((mine, core), (theirs, 1 - core)):
        rows = part_rows(which, half)
        for i in range(width // LANES):
            buffer[rows, i * LANES : (i + 1) * LANES] = source[i * half : (i + 1) * half, :].astype(f32)
    copy = pltpu.make_async_copy(buffer, out.at[layer], sems.at[0])
    copy.start()
    copy.wait()


def small_pack(sums_turn, sums_back, sums_last, decay_late, decay_early, out):
    per = sums_turn.shape[1] // LANES
    thirds = decay_late.shape[1] // LANES
    out[...] = jnp.zeros_like(out)
    kinds = (
        ((sums_last, 2), (sums_back, 2)),
        ((sums_last, 3), (sums_back, 3)),
        ((sums_back, 1), (sums_turn, 1)),
        ((sums_back, 0), (sums_turn, 0)),
    )
    at = 0
    for kind in kinds:
        for source, row in kind:
            for i in range(per):
                out[at : at + 1, :] = source[row : row + 1, i * LANES : (i + 1) * LANES]
                at += 1
    for side in range(2):
        for source in (decay_late, decay_early):
            for term in range(3):
                for i in range(thirds):
                    row = 3 * side + term
                    out[at : at + 1, :] = source[row : row + 1, i * LANES : (i + 1) * LANES]
                    at += 1


def small_out_kernel(own, got, table, gain, bias, rate, turn, skip, gate):
    layers, _, states = table.shape
    thirds = states // LANES
    width = gain.shape[1]
    per = width // LANES
    at = 0
    for out in (gain, bias, skip, gate):
        for layer in range(layers):
            for i in range(per):
                out[layer : layer + 1, i * LANES : (i + 1) * LANES] = own[at : at + 1, :] + got[at : at + 1, :]
                at += 1
    other = at + layers * 3 * thirds
    for layer in range(layers):
        for i in range(thirds):
            lanes = slice(i * LANES, (i + 1) * LANES)
            rows = [(layer * 3 + t) * thirds + i for t in range(3)]
            term_re, term_im, term_scale = (
                own[at + row : at + row + 1, :] + got[other + row : other + row + 1, :] for row in rows
            )
            re, im, scale, damping, step_size, rotation, square = (
                table[layer, t : t + 1, lanes] for t in range(7)
            )
            grad_re = (term_re * re - term_im * im) / square
            grad_im = (term_re * im + term_im * re) / square
            grad_scale = term_scale / scale
            grad_damping = grad_scale * square / scale - (grad_re * re + grad_im * im)
            grad_rotation = grad_im * re - grad_re * im
            log_rate = grad_damping * damping
            rate[layer, 0:1, lanes] = log_rate
            turn[layer, 0, 0:1, lanes] = grad_rotation * step_size
            turn[layer, 0, 1:2, lanes] = log_rate + grad_rotation * rotation


class Order:
    def __init__(self):
        self.tile = None

    def run(self, kernel, outs, operands, scratch=(), flops=0, name=None, spare=8, after=(), free_outs=0, alias=None,
            semaphores=0, cost=0, far=False):
        whole = pl.BlockSpec(memory_space=pltpu.VMEM)
        free = pl.BlockSpec(memory_space=pl.ANY)
        waits = list(after) + ([] if self.tile is None else [self.tile])
        inputs, results = len(operands), len(outs)
        skipped = len(waits)

        def body(*refs):
            token = refs[skipped + inputs]
            token[...] = jnp.zeros_like(token)
            kernel(*refs[skipped : skipped + inputs], *refs[skipped + inputs + 1 :])

        shapes = [jax.ShapeDtypeStruct((8, LANES), f32)]
        shapes += [jax.ShapeDtypeStruct(shape, dtype) for shape, dtype in outs]
        held = sum(jnp.dtype(dtype).itemsize * functools.reduce(lambda a, b: a * b, shape) for shape, dtype in scratch)
        specs = [free] * skipped + [pl.BlockSpec(memory_space=pltpu.HBM) if far else whole] * inputs
        aliases = {}
        if alias is not None:
            for operand, out in alias.items():
                specs[skipped + operand] = free
                aliases[skipped + operand] = out + 1
        extra = [pltpu.SemaphoreType.DMA((semaphores,))] if semaphores else []
        results = pl.pallas_call(
            body,
            out_shape=shapes,
            in_specs=specs,
            out_specs=[whole] + [free] * free_outs + [whole] * (results - free_outs),
            scratch_shapes=[pltpu.VMEM(shape, dtype) for shape, dtype in scratch] + extra,
            input_output_aliases=aliases,
            compiler_params=pltpu.CompilerParams(vmem_limit_bytes=held + spare * 2**20),
            cost_estimate=pl.CostEstimate(flops=int(1 + cost * 1e9), bytes_accessed=int(1 + cost * 3e6), transcendentals=0),
            name=name,
        )(*waits, *operands)
        self.tile = results[0]
        return results[1:]


def swap(value):
    return lax.ppermute(value, "dir", [(0, 1), (1, 0)])


def across(value, bits):
    count = lax.axis_size("seq")
    return lax.ppermute(value, "seq", [(i, i ^ bits) for i in range(count)])


def beyond(value):
    bit = 4
    while (1 << bit) < lax.axis_size("seq"):
        value = (value.astype(f32) + across(value, 1 << bit).astype(f32)).astype(value.dtype)
        bit += 1
    return value


def exchanged(payload, row_devices):
    count = lax.axis_size("seq")
    group = 2 * row_devices
    groups = None
    if count != row_devices:
        groups = [list(range(i, i + group)) for i in range(0, 2 * count, group)]
    return lax.all_to_all(payload, ("seq", "dir"), 0, 0, tiled=True, axis_index_groups=groups)


def sent(parts, low_bit):
    return [parts[0]] + [across(parts[k], k << low_bit) for k in (1, 2, 3)]


def shared(value, low_bit):
    return [value] + [across(value, k << low_bit) for k in (1, 2, 3)]


def body(
    tokens,
    segment_ids,
    norm_gain,
    norm_bias,
    input_matrix,
    output_matrix,
    rate_params,
    turn_params,
    skip_weight,
    glu_weight,
    glu_bias,
    cotangent,
):
    chip_rows, width = tokens.shape
    rows = chip_rows // 2
    layers = rate_params.shape[0]
    states = rate_params.shape[2]
    row_devices = LENGTH // chip_rows
    order = Order()
    here = functools.partial

    in_own, out_own = input_matrix, output_matrix
    in_oth = swap(input_matrix)
    rate_oth, turn_oth = swap(rate_params), swap(turn_params)
    out_oth = swap(output_matrix)
    segments = segment_ids.reshape(chip_rows // LANES, LANES)

    full = ((rows, width), f32)
    full_low = ((rows, width), bf16)
    columns = ((width // LANES, rows, LANES), f32)
    wide = ((rows, 2 * states), f32)
    wide_low = ((rows, 2 * states), bf16)
    ends = ((8, 2 * states), f32)
    payload_shape = ((2 * row_devices, 8, LANES), f32)
    narrow = ((rows, LANES), f32)
    tile = ((8, LANES), f32)
    sums_shape = ((8, width), f32)
    decay_shape = ((8, states), f32)
    table_shape = ((layers, 16, states), f32)
    places = ((8, 2 * states), f32)
    in_size = width * (2 * states // LANES)
    out_size = 2 * states * (width // LANES)
    glu_size = width // 2 * (width // LANES)
    outer_size = out_size + glu_size
    outer_pack = ((outer_size, LANES), bf16)
    inner_pack = ((in_size, LANES), bf16)
    one = 2.0 * rows * width * 2 * states
    gate = 2.0 * rows * width * width
    scan = 1e9

    x0, normed0, inv0 = order.run(
        here(open_kernel, row_devices),
        [full, full, narrow],
        [tokens],
        [full_low, columns],
        far=True,
        semaphores=1,
        name="open_norm",
        cost=10,
    )
    (
        mixed0, drive_own0, drive_oth0, keep_own, keep_oth, whole, ends_own, ends_oth, payload, table, tiles, ids,
    ) = order.run(
        here(open_second_kernel, row_devices),
        [full_low, wide, wide, narrow, narrow, ((2, 8, LANES), f32), ends, ends, payload_shape, table_shape,
         ((layers, 16, LANES), f32), tile],
        [normed0, segments, norm_gain, norm_bias, rate_params, turn_params, rate_oth, turn_oth, in_own, in_oth],
        [tile],
        name="open_scan",
        after=[out_oth],
    )
    gathered = exchanged(payload, row_devices)
    (
        low_own0, low_oth0, combined0, phi0, sig0, act_low0, x1, normed1, inv1, mixed1, drive_own1, drive_oth1,
        ends_own, ends_oth, payload,
    ) = order.run(
        here(mid_kernel, row_devices),
        [wide_low, wide_low, full, full, full, full_low, full, full, narrow, full_low, wide, wide, ends, ends,
         payload_shape],
        [gathered, ends_own, ends_oth, drive_own0, drive_oth0, keep_own, keep_oth, whole, table, tiles,
         ids, out_own, out_oth, x0, normed0, norm_gain, norm_bias, skip_weight, glu_weight, glu_bias, in_own, in_oth],
        [places, tile, full, wide, wide],
        flops=4 * one + gate + 3 * scan,
        name="mid",
    )
    gathered = exchanged(payload, row_devices)
    (
        low_own1, low_oth1, out1, grad1, combined_grad1, grad_own1, grad_oth1, ends_own, ends_oth, payload,
        sums_turn, mine, theirs,
    ) = order.run(
        here(turn_kernel, row_devices),
        [wide_low, wide_low, full, full, full, wide, wide, ends, ends, payload_shape, sums_shape, outer_pack, outer_pack],
        [gathered, ends_own, ends_oth, drive_own1, drive_oth1, keep_own, keep_oth, whole, table, tiles,
         ids, out_own, out_oth, x1, normed1, norm_gain, norm_bias, skip_weight, glu_weight, glu_bias, cotangent],
        [places, tile, full, full, full, full, columns, wide, wide, full_low, full_low, full_low],
        flops=4 * one + 2 * gate + 4 * scan,
        name="turn",
    )
    first_outer = [mine, swap(theirs)]
    gathered = exchanged(payload, row_devices)
    in_low_own1, in_low_oth1, decay_sums1, mine, theirs = order.run(
        here(scan_kernel, 1, row_devices),
        [wide_low, wide_low, decay_shape, inner_pack, inner_pack],
        [gathered, ends_own, ends_oth, grad_own1, grad_oth1, keep_own, keep_oth, whole, table, tiles,
         ids, low_own1, low_oth1, drive_own1, drive_oth1, mixed1],
        [places, tile, wide, wide],
        name="scan_one",
        after=[first_outer[1]],
    )
    first_inner = [mine, swap(theirs)]
    (
        grad0, combined_grad0, grad_own0, grad_oth0, ends_own, ends_oth, payload, sums_back, mine_outer, theirs_outer,
    ) = order.run(
        here(back_kernel, row_devices),
        [full, full, wide, wide, ends, ends, payload_shape, sums_shape, outer_pack, outer_pack],
        [in_low_own1, in_low_oth1, keep_own, keep_oth, whole, table, tiles, ids, in_own, in_oth, out_own, out_oth, grad1,
         combined_grad1, normed1, inv1, norm_gain, norm_bias, skip_weight, glu_weight, combined0, phi0, sig0, normed0,
         act_low0, low_own0, low_oth0],
        [full, full_low, full_low],
        name="back",
    )
    second_outer = [mine_outer, swap(theirs_outer)]
    outer_half = outer_size // 8
    half = outer_half + in_size // 8
    share_rows = half // 2
    small_rows = -(-(4 * layers * (width // LANES) + 6 * layers * (states // LANES)) // 16) * 16
    small_shape = ((small_rows, LANES), f32)

    def low(count):
        return ((count, LANES), bf16)

    def from_cores(packs, extra, sums, name, after=()):
        a_keep, a_send, b_keep, b_send, _ = order.run(
            here(cores_kernel, outer_half, half),
            [low(2 * half + extra)] * 2 + [low(2 * half)] * 2 + [small_shape],
            packs + sums,
            name=name,
            after=after,
            cost=CORES_COST,
        )
        return [a_keep, across(a_send, 1), b_keep, across(b_send, 2)]

    def from_first(parts, extra, name):
        a_keep, a_send, b_keep, b_send = order.run(
            here(half_kernel, half), [low(half + extra)] * 2 + [low(half)] * 2, parts, name=name
        )
        return [a_keep, across(a_send, 2), b_keep, across(b_send, 1)]

    def from_second(parts, extra, name):
        return sent(
            order.run(here(plane_kernel, half, outer_half), [low(share_rows + extra)] * 4, parts, name=name), 2
        )

    def gathered_half(parts, name, after=()):
        a_half, b_half = order.run(
            here(gather_kernel, outer_half), [low(half)] * 2, parts, name=name, after=after
        )
        return a_half, across(a_half, 2), b_half, across(b_half, 1)

    def gathered_whole(halves, name):
        a_pair, b_pair = order.run(pair_kernel, [low(2 * half)] * 2, list(halves), name=name)
        return [a_pair, across(a_pair, 1), b_pair, across(b_pair, 2)]

    first = from_cores(first_outer + first_inner, 0, [], "first_cores")
    (payload,) = order.run(relay_kernel, [payload_shape], [payload], name="relay", cost=50)
    gathered = exchanged(payload, row_devices)
    in_low_own0, in_low_oth0, decay_sums0, mine, theirs = order.run(
        here(scan_kernel, 0, row_devices),
        [wide_low, wide_low, decay_shape, inner_pack, inner_pack],
        [gathered, ends_own, ends_oth, grad_own0, grad_oth0, keep_own, keep_oth, whole, table, tiles,
         ids, low_own0, low_oth0, drive_own0, drive_oth0, mixed0],
        [places, tile, wide, wide],
        name="scan_zero",
        after=[first[1], first[3], second_outer[1]],
    )
    second_inner = [mine, swap(theirs)]
    first = from_first(first, 0, "first_half")
    halves, sums_last = order.run(
        final_kernel,
        [((2, rows, width), f32), sums_shape],
        [in_low_own0, in_low_oth0, in_own, in_oth, grad0, combined_grad0, normed0, inv0, norm_gain, skip_weight, out1],
        [full, columns, columns],
        name="final_norm",
    )
    first = from_second(first, 0, "first_plane")
    second = from_cores(
        second_outer + second_inner, small_rows, [sums_turn, sums_back, sums_last, decay_sums0, decay_sums1],
        "second_cores",
    )
    (share,) = order.run(planes_kernel, [low(share_rows)], first, name="first_planes")
    first = shared(beyond(share), 2)
    second = from_first(second, small_rows, "second_half")
    second = from_second(second, small_rows, "second_plane")
    first = gathered_half(first, "first_gather")
    share, small = order.run(second_planes_kernel, [low(share_rows), small_shape], second, name="second_planes")
    second = shared(beyond(share), 2)
    first = gathered_whole(first, "first_pair")
    small = beyond(small)
    got_small = swap(small)
    in_shape, out_shape = input_matrix.shape, output_matrix.shape

    def gate_part(quarters, name):
        (value,) = order.run(
            here(gate_part_kernel, outer_half, out_size), [low(glu_size)], quarters, [outer_pack], name=name
        )
        return value

    def gate_out(layer, mine, theirs, old, name):
        return order.run(
            here(gate_kernel, layer), [(glu_weight.shape, f32)], [mine, theirs] + old, [((width, width), f32)],
            name=name, free_outs=1, alias={2: 0} if old else None, semaphores=1,
        )

    def unpack(quarters, layer, old, name):
        return order.run(
            here(unpack_kernel, layer, len(old), outer_half),
            [(out_shape, f32), (in_shape, f32)],
            quarters + old,
            [(out_shape[2:], f32), (in_shape[2:], f32), outer_pack, inner_pack],
            name=name,
            free_outs=2,
            alias={4 + i: i for i in range(len(old))},
            semaphores=2,
        )

    second = gathered_half(second, "second_gather", [first[1], first[3]])
    halves, a_pair, b_pair = order.run(
        last_pair_kernel, [((2, rows, width), f32), low(2 * half), low(2 * half)], list(second) + [halves],
        name="second_pair", free_outs=1, alias={4: 0},
    )
    second = [a_pair, across(a_pair, 1), b_pair, across(b_pair, 2)]
    gate_one = gate_part(first, "gate_one")
    got_one = swap(gate_one)
    results = unpack(first, 1, [], "unpack_one")
    gain_grad, bias_grad, rate_grad, turn_grad, skip_grad, gate_grad = order.run(
        small_out_kernel,
        [((layers, width), f32), ((layers, width), f32), (rate_params.shape, f32), (turn_params.shape, f32),
         ((layers, width), f32), ((layers, width), f32)],
        [small, got_small, table],
        name="small_out",
    )
    whole_rows = ((chip_rows, width), f32)
    block_output, tokens_grad = order.run(
        join_kernel, [whole_rows, whole_rows], [halves, swap(halves)], name="join"
    )
    glu_all = gate_out(1, gate_one, got_one, [], "gate_out_one")
    gate_zero = gate_part(second, "gate_zero")
    got_zero = swap(gate_zero)
    out_all, in_all = unpack(second, 0, list(results), "unpack_zero")
    (glu_all,) = gate_out(0, gate_zero, got_zero, list(glu_all), "gate_out_zero")
    return (
        block_output,
        tokens_grad,
        gain_grad,
        bias_grad,
        in_all,
        out_all,
        rate_grad,
        turn_grad,
        skip_grad,
        glu_all,
        gate_grad,
    )


def solution(mesh):
    return jax.shard_map(
        body,
        mesh=mesh,
        in_specs=(
            P("seq", None),
            P("seq"),
            P(),
            P(),
            P(None, "dir", None, None),
            P(None, "dir", None, None),
            P(None, "dir", None),
            P(None, "dir", None, None),
            P(),
            P(),
            P(),
            P("seq", None),
        ),
        out_specs=(
            P("seq", None),
            P("seq", None),
            P(),
            P(),
            P(None, "dir", None, None),
            P(None, "dir", None, None),
            P(None, "dir", None),
            P(None, "dir", None, None),
            P(),
            P(),
            P(),
        ),
        check_vma=False,
    )
```

```python
import functools

import jax
import jax.numpy as jnp
from jax import lax
from jax.experimental import pallas as pl
from jax.experimental.pallas import tpu as pltpu
from jax.sharding import PartitionSpec as P

LENGTH = 16384
LONGEST_RUN = 8192

eps = 1e-05
inv_root_two = 0.7071067811865476
inv_root_two_pi = 0.3989422804014327

f32 = jnp.float32
bf16 = jnp.bfloat16


LANES = 128
ELEMENT_ROWS = 512
UNROLL = 8
CORES_COST = 0


def core_place(row_devices):
    core = lax.axis_index("dir")
    return core, lax.rem(lax.axis_index("seq"), row_devices) * 2 + core


def dot(a, b):
    return jnp.dot(a, b, preferred_element_type=f32)


def dot_nt(a, b):
    return lax.dot_general(a, b, (((1,), (1,)), ((), ())), preferred_element_type=f32)


def dot_tn(a, b):
    return lax.dot_general(a, b, (((0,), (0,)), ((), ())), preferred_element_type=f32)


def squared(re, im, times):
    for _ in range(times):
        re, im = re * re - im * im, 2.0 * re * im
    return re, im


def over_blocks(rows, step, init=()):
    def one(i, carry):
        return step(pl.multiple_of(i * ELEMENT_ROWS, ELEMENT_ROWS), carry)

    return lax.fori_loop(0, rows // ELEMENT_ROWS, one, init)


def fold(values):
    total = values[0:8]
    for start in range(8, values.shape[0], 8):
        total = total + values[start : start + 8]
    return total


class Lanes:
    def __init__(self, rows_ref, tiles_ref, layer, adjoint, spans, rows):
        states = rows_ref.shape[2]
        self.states = states
        self.rows_ref, self.layer = rows_ref, layer
        flip = -1.0 if adjoint else 1.0
        self.step = []
        self.run = []
        self.block = []
        for side in range(2):
            row = 8 * side
            re = rows_ref[layer, row : row + 1, :]
            im = rows_ref[layer, row + 1 : row + 2, :] * flip
            self.step.append((jnp.broadcast_to(re, (8, states)), jnp.broadcast_to(im, (8, states))))
            self.run.append(squared(re, im, (spans - 1).bit_length()))
            thirds = states // LANES
            tile_re = tiles_ref[layer, 8 * side : 8 * side + thirds, :]
            tile_im = tiles_ref[layer, 8 * side + thirds : 8 * side + 2 * thirds, :] * flip
            self.block.append(squared(tile_re, tile_im, (rows - 1).bit_length()))

    def scaling(self, side):
        row = self.rows_ref[self.layer, 8 * side + 2 : 8 * side + 3, :]
        return jnp.concatenate([row, row], 1)


def sweep(first_forward, drives, masks, lanes, init, visit=None, totals=()):
    states = lanes.states
    span = drives[0].shape[0] // 8

    def step(i, carry):
        values, sums = carry
        up = pl.multiple_of(i * 8, 8)
        down = pl.multiple_of((span - 1 - i) * 8, 8)
        places = (jnp.where(first_forward, up, down), jnp.where(first_forward, down, up))
        new = []
        for side in range(2):
            rows = pl.ds(pl.multiple_of(places[side], 8), 8)
            keep = masks[side][rows, :]
            keep = jnp.concatenate([keep] * (states // LANES), 1)
            step_re, step_im = lanes.step[side]
            step_re, step_im = step_re * keep, step_im * keep
            re, im = values[side]
            drive_re = drives[side][rows, :states]
            drive_im = drives[side][rows, states:]
            re, im = (
                step_re * re - step_im * im + drive_re,
                step_re * im + step_im * re + drive_im,
            )
            new.append((re, im))
            if visit is not None:
                sums = visit(side, rows, re, im, sums)
        return tuple(new), sums

    return lax.fori_loop(0, span, step, (init, totals), unroll=UNROLL)


def run_chain(first_up, lanes, side, ends, whole, start, places):
    states = lanes.states
    power_re, power_im = lanes.run[side]
    re, im = start
    for i in range(8):
        s = jnp.where(first_up, i, 7 - i)
        row = pl.ds(s, 1)
        if places is not None:
            places[row, :states] = re
            places[row, states:] = im
        passes = whole[row, :]
        passes = jnp.concatenate([passes] * (states // LANES), 1)
        pass_re, pass_im = power_re * passes, power_im * passes
        end_re, end_im = ends[row, :states], ends[row, states:]
        re, im = (end_re + pass_re * re - pass_im * im, end_im + pass_re * im + pass_im * re)
    return re, im


def first_pass(running_up, place, drives, masks, wholes, lanes, ids_ref, ends, payload):
    states = lanes.states
    thirds = states // LANES
    nothing = jnp.zeros((8, states), f32)
    zero = (nothing, nothing)
    values, _ = sweep(running_up, drives, masks, lanes, (zero, zero))
    tiles = []
    for side in range(2):
        ends[side][:, :states] = values[side][0]
        ends[side][:, states:] = values[side][1]
        upward = running_up if side == 0 else jnp.logical_not(running_up)
        start = jnp.zeros((1, states), f32)
        re, im = run_chain(upward, lanes, side, ends[side], wholes[side], (start, start), None)
        rows = [part[:, LANES * i : LANES * (i + 1)] for part in (re, im) for i in range(thirds)]
        tiles.append(jnp.concatenate(rows + [ids_ref[0:2, :]], 0))
    for i in range(payload.shape[0]):
        to_later = jnp.logical_xor(running_up, i < place)
        payload[i] = jnp.where(to_later, tiles[0], tiles[1]).astype(payload.dtype)


def entering(upward, place, lanes, side, gathered, ids_ref, small):
    states = lanes.states
    thirds = states // LANES
    count = gathered.shape[0]
    rows = lanes.token_rows
    block_re, block_im = lanes.block[side]
    re = jnp.zeros((thirds, LANES), f32)
    im = jnp.zeros((thirds, LANES), f32)
    key = jnp.where(upward, ids_ref[0:1, :], ids_ref[1:2, :])
    for distance in range(min(count - 1, LONGEST_RUN // rows), 0, -1):
        source = jnp.where(upward, place - distance, place + distance)
        inside = jnp.logical_and(source >= 0, source < count)
        source = jnp.clip(source, 0, count - 1)
        sent = gathered[source].astype(f32)
        sent_re, sent_im = sent[0:thirds], sent[thirds : 2 * thirds]
        sent_key = jnp.where(upward, sent[7:8], sent[6:7])
        joined = jnp.where(jnp.logical_and(sent_key == key, inside), 1.0, 0.0)
        re, im = (
            joined * sent_re + block_re * re - block_im * im,
            joined * sent_im + block_re * im + block_im * re,
        )
    small[0:thirds, :] = re
    small[thirds : 2 * thirds, :] = im
    wide_re = jnp.concatenate([small[i : i + 1, :] for i in range(thirds)], 1)
    wide_im = jnp.concatenate([small[thirds + i : thirds + i + 1, :] for i in range(thirds)], 1)
    return wide_re, wide_im


def second_starts(running_up, place, lanes, gathered, ids_ref, ends, wholes, places, small):
    init = []
    states = lanes.states
    for side in range(2):
        upward = running_up if side == 0 else jnp.logical_not(running_up)
        start = entering(upward, place, lanes, side, gathered, ids_ref, small)
        run_chain(upward, lanes, side, ends[side], wholes[side], start, places)
        init.append((places[:, :states], places[:, states:]))
    return tuple(init)


def make_lanes(rows_ref, tiles_ref, layer, adjoint, token_rows):
    lanes = Lanes(rows_ref, tiles_ref, layer, adjoint, token_rows // 8, token_rows)
    lanes.token_rows = token_rows
    return lanes


def standardise(x):
    width = x.shape[1]
    average = jnp.sum(x, 1, keepdims=True) * (1.0 / width)
    centred = x - average
    inv_scale = lax.rsqrt(jnp.sum(centred * centred, 1, keepdims=True) * (1.0 / width) + eps)
    return centred * inv_scale, inv_scale


def fill_columns(columns, values):
    for i in range(columns.shape[0]):
        columns[i] = values[:, i * LANES : (i + 1) * LANES].astype(columns.dtype)


def tile_order(columns, first, count, span):
    tiles = [
        jnp.concatenate([columns[i, pl.ds(first + j, 8, stride=span), :] for i in range(columns.shape[0])], 1)
        for j in range(count)
    ]
    return jnp.concatenate(tiles, 0)


def store_token_order(columns, first, values, span):
    for j in range(values.shape[0] // 8):
        for i in range(columns.shape[0]):
            columns[i, pl.ds(first + j, 8, stride=span), :] = values[8 * j : 8 * j + 8, i * LANES : (i + 1) * LANES]


def join_columns(out, columns):
    for i in range(columns.shape[0]):
        out[:, i * LANES : (i + 1) * LANES] = columns[i]


def one_minus_exp(x):
    series = jnp.ones_like(x)
    for term in range(12, 1, -1):
        series = 1.0 - x * (1.0 / term) * series
    return jnp.where(x < 0.5, x * series, 1.0 - jnp.exp(-x))


def table_rows(table, layer, base, rate, turn):
    frequency = turn[layer, 0, 0:1, :]
    log_step = turn[layer, 0, 1:2, :]
    step_size = jnp.exp(log_step)
    damping = jnp.exp(rate[layer, 0:1, :] + log_step)
    magnitude = jnp.exp(-damping)
    rotation = frequency * step_size
    square = magnitude * magnitude
    rows = (
        magnitude * jnp.cos(rotation), magnitude * jnp.sin(rotation), jnp.sqrt(one_minus_exp(2.0 * damping)), damping,
        step_size, rotation, square,
    )
    for i, row in enumerate(rows):
        table[layer, base + i : base + i + 1, :] = row


def open_kernel(row_devices, tokens_from, x_out, normed_out, inv_out, tokens, natural, sems):
    copy = pltpu.make_async_copy(
        tokens_from.at[part_rows(lax.axis_index("dir"), tokens.shape[0])], tokens, sems.at[0]
    )
    copy.start()
    copy.wait()
    rows = x_out.shape[0]
    span = rows // 8
    fill_columns(natural, tokens[...].astype(f32))

    def element(start, carry):
        x = tile_order(natural, start // 8, ELEMENT_ROWS // 8, span)
        normed, inv_scale = standardise(x)
        block = pl.ds(start, ELEMENT_ROWS)
        x_out[block, :] = x
        normed_out[block, :] = normed
        inv_out[block, :] = jnp.broadcast_to(inv_scale, (ELEMENT_ROWS, LANES))
        return carry

    over_blocks(rows, element)


def open_second_kernel(
    row_devices,
    normed,
    segments,
    gain,
    bias,
    rate,
    turn,
    rate_oth,
    turn_oth,
    in_own,
    in_oth,
    mixed_low,
    drive_own,
    drive_oth,
    keep_own,
    keep_oth,
    whole_out,
    ends_own,
    ends_oth,
    payload,
    table,
    tiles,
    ids,
    rows8,
):
    core, place = core_place(row_devices)
    rows = normed.shape[0]
    span = rows // 8

    def element(start, carry):
        block = pl.ds(start, ELEMENT_ROWS)
        mixed_low[block, :] = (normed[block, :] * gain[0:1, :] + bias[0:1, :]).astype(bf16)
        return carry

    over_blocks(rows, element)
    table[...] = jnp.zeros_like(table)
    tiles[...] = jnp.zeros_like(tiles)
    thirds = table.shape[2] // LANES
    for layer in range(table.shape[0]):
        table_rows(table, layer, 0, rate, turn)
        table_rows(table, layer, 8, rate_oth, turn_oth)
        for side in range(2):
            for part in range(2):
                for i in range(thirds):
                    at = 8 * side + part * thirds + i
                    tiles[layer, at : at + 1, :] = table[
                        layer, 8 * side + part : 8 * side + part + 1, i * LANES : (i + 1) * LANES
                    ]

    number = segments[...].astype(f32)
    count = number.shape[0]
    lane = lax.broadcasted_iota(jnp.int32, number.shape, 1)
    row = lax.broadcasted_iota(jnp.int32, number.shape, 0)
    back = pltpu.roll(number, 1, 1)
    back = jnp.where(lane == 0, pltpu.roll(back, 1, 0), back)
    ahead = pltpu.roll(number, LANES - 1, 1)
    ahead = jnp.where(lane == LANES - 1, pltpu.roll(ahead, count - 1, 0), ahead)
    edge_first = jnp.logical_and(lane == 0, row == 0)
    edge_last = jnp.logical_and(lane == LANES - 1, row == count - 1)
    up_keep = jnp.where(jnp.logical_or(number == back, edge_first), 1.0, 0.0)
    down_keep = jnp.where(jnp.logical_or(number == ahead, edge_last), 1.0, 0.0)
    per = LANES // span
    used = 8 // per
    for side, out in ((0, keep_own), (1, keep_oth)):
        rows8[0:count, :] = jnp.where(core == side, up_keep, down_keep)
        half = rows8[pl.ds(core * used, used), :]
        runs = jnp.concatenate([half[s // per : s // per + 1] for s in range(8)], 0)
        place = lax.broadcasted_iota(jnp.int32, (8, LANES), 1)
        sub = lax.broadcasted_iota(jnp.int32, (8, LANES), 0)
        first = lax.rem(sub, per) * span
        inside = jnp.logical_and(place >= first, place < first + span)
        least = jnp.min(jnp.where(inside, runs, 1.0), 1, keepdims=True)
        whole_out[side] = jnp.broadcast_to(least, (8, LANES))
        step = lax.broadcasted_iota(jnp.int32, (span, 8, LANES), 0)
        spread = jnp.where(step == (place - first)[None], runs[None], 0.0)
        spread = spread.reshape(span * 8, LANES).astype(bf16)
        out[...] = dot(spread, jnp.ones((LANES, LANES), bf16))
    rows8[0:count, :] = number
    first_row = rows8[pl.ds(core * used, 1), :]
    last_row = rows8[pl.ds(core * used + used - 1, 1), :]
    ids[...] = jnp.zeros_like(ids)
    ids[0:1, :] = jnp.broadcast_to(first_row[:, 0:1], (1, LANES))
    ids[1:2, :] = jnp.broadcast_to(last_row[:, LANES - 1 : LANES], (1, LANES))
    for side, (matrix, drive) in enumerate(((in_own, drive_own), (in_oth, drive_oth))):
        scale = table[0, 8 * side + 2 : 8 * side + 3, :]
        drive[...] = dot(mixed_low[...], matrix[0, 0]) * jnp.concatenate([scale, scale], 1)
    lanes = make_lanes(table, tiles, 0, False, rows)
    first_pass(
        core == 0,
        core_place(row_devices)[1],
        (drive_own, drive_oth),
        (keep_own, keep_oth),
        (whole_out.at[0], whole_out.at[1]),
        lanes,
        ids,
        (ends_own, ends_oth),
        payload,
    )


def forward_states(layer, info, gathered, ends, drives, masks, whole, rows_ref, tiles_ref, ids, states, lows, places, small):
    rows = drives[0].shape[0]
    lanes = make_lanes(rows_ref, tiles_ref, layer, False, rows)
    core, place = info
    running_up = core == 0
    init = second_starts(
        running_up, place, lanes, gathered, ids, ends, (whole.at[0], whole.at[1]), places, small
    )
    width = lanes.states

    def visit(side, where, re, im, sums):
        states[side][where, :width] = re
        states[side][where, width:] = im
        return sums

    sweep(running_up, drives, masks, lanes, init, visit)
    for side in range(2):
        lows[side][...] = states[side][...].astype(bf16)


def mid_kernel(
    row_devices,
    gathered,
    ends_own,
    ends_oth,
    drive_own,
    drive_oth,
    keep_own,
    keep_oth,
    whole,
    rows_ref,
    tiles_ref,
    ids,
    out_own,
    out_oth,
    x_in,
    normed,
    gain,
    bias,
    skip,
    glu,
    glu_bias,
    in_own,
    in_oth,
    low_own,
    low_oth,
    combined_out,
    phi_out,
    sig_out,
    act_low,
    x_out,
    normed_out,
    inv_out,
    mixed_out,
    next_own,
    next_oth,
    next_ends_own,
    next_ends_oth,
    payload,
    places,
    small,
    wide,
    states_own,
    states_oth,
):
    info = core_place(row_devices)
    rows = x_in.shape[0]
    masks = (keep_own, keep_oth)
    forward_states(
        0, info, gathered, (ends_own, ends_oth), (drive_own, drive_oth), masks, whole, rows_ref, tiles_ref,
        ids, (states_own, states_oth), (low_own, low_oth), places, small,
    )
    wide[...] = dot(low_own[...], out_own[0, 0]) + dot(low_oth[...], out_oth[0, 0])

    def element(start, carry):
        block = pl.ds(start, ELEMENT_ROWS)
        mixed = normed[block, :] * gain[0:1, :] + bias[0:1, :]
        combined = wide[block, :] + skip[0:1, :] * mixed
        phi = 0.5 * (1.0 + lax.erf(combined * inv_root_two))
        combined_out[block, :] = combined
        phi_out[block, :] = phi
        act_low[block, :] = (combined * phi).astype(bf16)
        return carry

    over_blocks(rows, element)
    wide[...] = dot(act_low[...], glu[0])

    def element_two(start, carry):
        block = pl.ds(start, ELEMENT_ROWS)
        sig = jax.nn.sigmoid(wide[block, :] + glu_bias[0:1, :])
        sig_out[block, :] = sig
        x = x_in[block, :] + combined_out[block, :] * phi_out[block, :] * sig
        x_out[block, :] = x
        after, inv_scale = standardise(x)
        normed_out[block, :] = after
        inv_out[block, :] = jnp.broadcast_to(inv_scale, (ELEMENT_ROWS, LANES))
        mixed_out[block, :] = (after * gain[1:2, :] + bias[1:2, :]).astype(bf16)
        return carry

    over_blocks(rows, element_two)
    for side, (matrix, out) in enumerate(((in_own, next_own), (in_oth, next_oth))):
        scale = rows_ref[1, 8 * side + 2 : 8 * side + 3, :]
        out[...] = dot(mixed_out[...], matrix[1, 0]) * jnp.concatenate([scale, scale], 1)
    lanes = make_lanes(rows_ref, tiles_ref, 1, False, rows)
    first_pass(
        info[0] == 0,
        info[1],
        (next_own, next_oth),
        masks,
        (whole.at[0], whole.at[1]),
        lanes,
        ids,
        (next_ends_own, next_ends_oth),
        payload,
    )


def backward_half(
    layer, info, grad, combined, phi, sig, normed, gain, bias, skip, glu, out_own, out_oth, masks, whole,
    rows_ref, tiles_ref, ids, gate_low, combined_grad, combined_low, grad_own, grad_oth, ends, payload, sums, wide,
):
    rows = grad.shape[0]
    width = grad.shape[1]
    zero = jnp.zeros((8, width), f32)

    def element(start, carry):
        block = pl.ds(start, ELEMENT_ROWS)
        gate = sig[block, :]
        gate_grad = grad[block, :] * (combined[block, :] * phi[block, :]) * gate * (1.0 - gate)
        gate_low[block, :] = gate_grad.astype(bf16)
        return carry + fold(gate_grad)

    bias_sum = over_blocks(rows, element, zero)
    wide[...] = dot_nt(gate_low[...], glu[layer])

    def element_two(start, carry):
        block = pl.ds(start, ELEMENT_ROWS)
        value = combined[block, :]
        activation_grad = grad[block, :] * sig[block, :] + wide[block, :]
        slope = phi[block, :] + value * (jnp.exp(-0.5 * value * value) * inv_root_two_pi)
        result = activation_grad * slope
        combined_grad[block, :] = result
        combined_low[block, :] = result.astype(bf16)
        mixed = normed[block, :] * gain[layer : layer + 1, :] + bias[layer : layer + 1, :]
        return carry + fold(result * mixed)

    skip_sum = over_blocks(rows, element_two, zero)
    sums[0:1, :] = jnp.sum(bias_sum, 0, keepdims=True)
    sums[1:2, :] = jnp.sum(skip_sum, 0, keepdims=True)
    grad_own[...] = dot_nt(combined_low[...], out_own[layer, 0])
    grad_oth[...] = dot_nt(combined_low[...], out_oth[layer, 0])
    lanes = make_lanes(rows_ref, tiles_ref, layer, True, rows)
    first_pass(
        info[0] == 1,
        info[1],
        (grad_own, grad_oth),
        (masks[1], masks[0]),
        (whole.at[1], whole.at[0]),
        lanes,
        ids,
        ends,
        payload,
    )


def turn_kernel(
    row_devices,
    gathered,
    ends_own,
    ends_oth,
    drive_own,
    drive_oth,
    keep_own,
    keep_oth,
    whole,
    rows_ref,
    tiles_ref,
    ids,
    out_own,
    out_oth,
    x_in,
    normed,
    gain,
    bias,
    skip,
    glu,
    glu_bias,
    cotangent,
    low_own,
    low_oth,
    block_out,
    grad_out,
    combined_grad,
    grad_own,
    grad_oth,
    next_ends_own,
    next_ends_oth,
    payload,
    sums,
    mine,
    theirs,
    places,
    small,
    wide,
    combined,
    phi_rows,
    sig_rows,
    natural,
    states_own,
    states_oth,
    act_low,
    gate_low,
    combined_low,
):
    info = core_place(row_devices)
    rows = x_in.shape[0]
    span = rows // 8
    masks = (keep_own, keep_oth)
    forward_states(
        1, info, gathered, (ends_own, ends_oth), (drive_own, drive_oth), masks, whole, rows_ref, tiles_ref,
        ids, (states_own, states_oth), (low_own, low_oth), places, small,
    )
    wide[...] = dot(low_own[...], out_own[1, 0]) + dot(low_oth[...], out_oth[1, 0])

    def element(start, carry):
        block = pl.ds(start, ELEMENT_ROWS)
        mixed = normed[block, :] * gain[1:2, :] + bias[1:2, :]
        value = wide[block, :] + skip[1:2, :] * mixed
        phi = 0.5 * (1.0 + lax.erf(value * inv_root_two))
        combined[block, :] = value
        phi_rows[block, :] = phi
        act_low[block, :] = (value * phi).astype(bf16)
        return carry

    over_blocks(rows, element)
    wide[...] = dot(act_low[...], glu[1])
    base = pl.multiple_of(info[0] * rows, rows)
    fill_columns(natural, cotangent[pl.ds(base, rows), :])

    def element_two(start, carry):
        block = pl.ds(start, ELEMENT_ROWS)
        sig = jax.nn.sigmoid(wide[block, :] + glu_bias[1:2, :])
        sig_rows[block, :] = sig
        block_out[block, :] = x_in[block, :] + combined[block, :] * phi_rows[block, :] * sig
        grad_out[block, :] = tile_order(natural, start // 8, ELEMENT_ROWS // 8, span)
        return carry

    over_blocks(rows, element_two)
    sums[...] = jnp.zeros_like(sums)
    backward_half(
        1, info, grad_out, combined, phi_rows, sig_rows, normed, gain, bias, skip, glu, out_own, out_oth, masks,
        whole, rows_ref, tiles_ref, ids, gate_low, combined_grad, combined_low, grad_own, grad_oth,
        (next_ends_own, next_ends_oth), payload, sums, wide,
    )
    gradient_pack(act_low, gate_low, combined_low, low_own, low_oth, mine, theirs, wide)


def adjoint_states(
    layer, info, gathered, ends, grads, masks, whole, rows_ref, tiles_ref, ids, states, drives, lows, decay_sums,
    adjoints, places, small,
):
    rows = grads[0].shape[0]
    lanes = make_lanes(rows_ref, tiles_ref, layer, True, rows)
    core, place = info
    running_up = core == 1
    init = second_starts(
        running_up, place, lanes, gathered, ids, ends, (whole.at[1], whole.at[0]), places, small
    )
    width = lanes.states
    zero = jnp.zeros((8, width), f32)
    for side in range(2):
        adjoints[side][...] = states[side][...].astype(f32)

    def visit(side, where, re, im, sums):
        drive_re, drive_im = drives[side][where, :width], drives[side][where, width:]
        moved_re = adjoints[side][where, :width] - drive_re
        moved_im = adjoints[side][where, width:] - drive_im
        adjoints[side][where, :width] = re
        adjoints[side][where, width:] = im
        mine = sums[side]
        mine = (
            mine[0] + (re * moved_re + im * moved_im),
            mine[1] + (im * moved_re - re * moved_im),
            mine[2] + (re * drive_re + im * drive_im),
        )
        return (mine, sums[1]) if side == 0 else (sums[0], mine)

    _, sums = sweep(
        running_up, grads, (masks[1], masks[0]), lanes, init, visit, ((zero, zero, zero), (zero, zero, zero))
    )
    decay_sums[...] = jnp.zeros_like(decay_sums)
    for side in range(2):
        for i in range(3):
            decay_sums[3 * side + i : 3 * side + i + 1, :] = jnp.sum(sums[side][i], 0, keepdims=True)
        lows[side][...] = (adjoints[side][...] * lanes.scaling(side)).astype(bf16)


def norm_backward(
    layer, low_own, low_oth, in_own, in_oth, grad, combined_grad, normed, inv_scale, gain, skip, sums, wide, finish
):
    rows, width = grad.shape
    wide[...] = dot_nt(low_own[...], in_own[layer, 0]) + dot_nt(low_oth[...], in_oth[layer, 0])
    zero = jnp.zeros((8, width), f32)

    def element(start, carry):
        block = pl.ds(start, ELEMENT_ROWS)
        mixed_grad = wide[block, :] + combined_grad[block, :] * skip[layer : layer + 1, :]
        unit = normed[block, :]
        weighted = mixed_grad * unit
        inner = mixed_grad * gain[layer : layer + 1, :]
        mean_one = jnp.sum(inner, 1, keepdims=True) * (1.0 / width)
        mean_two = jnp.sum(weighted * gain[layer : layer + 1, :], 1, keepdims=True) * (1.0 / width)
        spread = jnp.concatenate([inv_scale[block, :]] * (width // LANES), 1)
        finish(start, grad[block, :] + spread * (inner - mean_one - unit * mean_two))
        return carry[0] + fold(weighted), carry[1] + fold(mixed_grad)

    gain_sum, bias_sum = over_blocks(rows, element, (zero, zero))
    sums[2:3, :] = jnp.sum(gain_sum, 0, keepdims=True)
    sums[3:4, :] = jnp.sum(bias_sum, 0, keepdims=True)


def back_kernel(
    row_devices,
    in_low_own,
    in_low_oth,
    keep_own,
    keep_oth,
    whole,
    rows_ref,
    tiles_ref,
    ids,
    in_own,
    in_oth,
    out_own,
    out_oth,
    grad_in,
    combined_grad_in,
    normed_in,
    inv_in,
    gain,
    bias,
    skip,
    glu,
    combined,
    phi,
    sig,
    normed,
    act_low,
    low_own,
    low_oth,
    grad_out,
    combined_grad,
    next_own,
    next_oth,
    next_ends_own,
    next_ends_oth,
    payload,
    sums,
    mine,
    theirs,
    wide,
    gate_low,
    combined_low,
):
    info = core_place(row_devices)
    masks = (keep_own, keep_oth)
    sums[...] = jnp.zeros_like(sums)

    def finish(start, value):
        grad_out[pl.ds(start, ELEMENT_ROWS), :] = value

    norm_backward(
        1, in_low_own, in_low_oth, in_own, in_oth, grad_in, combined_grad_in, normed_in, inv_in, gain, skip, sums, wide,
        finish,
    )
    backward_half(
        0, info, grad_out, combined, phi, sig, normed, gain, bias, skip, glu, out_own, out_oth, masks, whole,
        rows_ref, tiles_ref, ids, gate_low, combined_grad, combined_low, next_own, next_oth,
        (next_ends_own, next_ends_oth), payload, sums, wide,
    )
    gradient_pack(act_low, gate_low, combined_low, low_own, low_oth, mine, theirs, wide)


def scan_kernel(
    layer,
    row_devices,
    gathered,
    ends_own,
    ends_oth,
    grad_own,
    grad_oth,
    keep_own,
    keep_oth,
    whole,
    rows_ref,
    tiles_ref,
    ids,
    states_own,
    states_oth,
    drive_own,
    drive_oth,
    mixed_low,
    low_own,
    low_oth,
    decay_sums,
    mine,
    theirs,
    places,
    small,
    adjoint_own,
    adjoint_oth,
):
    info = core_place(row_devices)
    masks = (keep_own, keep_oth)
    adjoint_states(
        layer, info, gathered, (ends_own, ends_oth), (grad_own, grad_oth), masks, whole, rows_ref, tiles_ref, ids,
        (states_own, states_oth), (drive_own, drive_oth), (low_own, low_oth), decay_sums,
        (adjoint_own, adjoint_oth), places, small,
    )
    store_columns(mine, 0, dot_tn(mixed_low[...], low_own[...]))
    store_columns(theirs, 0, dot_tn(mixed_low[...], low_oth[...]))


def final_kernel(
    low_own, low_oth, in_own, in_oth, grad_in, combined_grad, normed, inv_scale, gain, skip, block_out, halves, sums, wide,
    *columns,
):
    rows = grad_in.shape[0]
    sums[...] = jnp.zeros_like(sums)

    def finish(start, value):
        store_token_order(columns[1], start // 8, value, rows // 8)

    norm_backward(
        0, low_own, low_oth, in_own, in_oth, grad_in, combined_grad, normed, inv_scale, gain, skip, sums, wide, finish
    )
    store_token_order(columns[0], 0, block_out[...], rows // 8)
    for i in range(2):
        join_columns(halves.at[i], columns[i])


def store_columns(out, first, values):
    rows, width = values.shape
    for i in range(width // LANES):
        out[first + i * rows : first + (i + 1) * rows, :] = values[:, i * LANES : (i + 1) * LANES].astype(out.dtype)


def half_rows(core, act_low, gate_low, mine, theirs, first, wide):
    wide[...] = dot_tn(act_low[...], gate_low[...])
    half = wide.shape[0] // 2
    width = wide.shape[1]
    for out, which in ((mine, core), (theirs, 1 - core)):
        rows = pl.ds(pl.multiple_of(which * half, half), half)
        for i in range(width // LANES):
            out[first + i * half : first + (i + 1) * half, :] = wide[rows, i * LANES : (i + 1) * LANES].astype(out.dtype)


def gradient_pack(act_low, gate_low, combined_low, low_own, low_oth, mine, theirs, wide):
    store_columns(theirs, 0, dot_tn(low_oth[...], combined_low[...]))
    store_columns(mine, 0, dot_tn(low_own[...], combined_low[...]))
    size = low_own.shape[1] * (combined_low.shape[1] // LANES)
    half_rows(lax.axis_index("dir"), act_low, gate_low, mine, theirs, size, wide)


def slot(low_bit, parts):
    return jnp.bitwise_and(jnp.right_shift(lax.axis_index("seq"), low_bit), parts - 1)


def paired(values):
    while len(values) > 1:
        values = [a + b for a, b in zip(values[::2], values[1::2])]
    return values[0]


def part_rows(index, rows):
    return pl.ds(pl.multiple_of(index * rows, rows), rows)


def sum_parts(groups, outs, low_bit):
    parts = len(outs)
    mine = slot(low_bit, parts)
    for k, out in enumerate(outs):
        first = 0
        for rows, sources in groups:
            share = rows // parts
            where = part_rows(jnp.bitwise_xor(mine, k), share)
            total = paired([source[where, :].astype(f32) for source in sources])
            out[first : first + share, :] = total.astype(out.dtype)
            first += share


def gather_parts(sizes, sources, low_bit, outs):
    mine = slot(low_bit, len(sources))
    for k, source in enumerate(sources):
        first = 0
        for rows, out in zip(sizes, outs):
            out[part_rows(jnp.bitwise_xor(mine, k), rows), :] = source[first : first + rows, :]
            first += rows


def relay_kernel(payload_in, payload):
    payload[...] = payload_in[...]


def add_rows(out, at, sources, start, rows):
    where = pl.ds(pl.multiple_of(start, rows), rows)
    out[at : at + rows, :] = paired([source[where, :].astype(f32) for source in sources]).astype(out.dtype)


def put_small(outs, first, value):
    for out in outs:
        out[first : first + value.shape[0], :] = value.astype(out.dtype)


def half_groups(outer, inner, side):
    return ((outer // 2, side * (outer // 2)), (inner // 2, side * (inner // 2)))


def cores_kernel(outer_half, half, outer, got_outer, inner, got_inner, *refs):
    small_sums, (a_keep, a_send, b_keep, b_send), small = refs[:-5], refs[-5:-1], refs[-1]
    outer_rows, inner_rows = 2 * outer_half, 2 * (half - outer_half)
    mine = slot(0, 4)
    for side, out, parts in ((0, a_keep, (0, 2)), (0, a_send, (1, 3)), (1, b_keep, (0, 1)), (1, b_send, (2, 3))):
        (rows_one, at_one), (rows_two, at_two) = half_groups(outer_rows, inner_rows, side)
        for place, k in enumerate(parts):
            which = jnp.bitwise_xor(mine, k)
            add_rows(out, place * half, [outer, got_outer], which * outer_rows + at_one, rows_one)
            add_rows(out, place * half + rows_one, [inner, got_inner], which * inner_rows + at_two, rows_two)
    if small_sums:
        small_pack(*small_sums, small)
        put_small((a_keep, a_send), 2 * half, small[...])


def half_kernel(half, a_own, a_got, b_own, b_got, a_keep, a_send, b_keep, b_send):
    for own, got, outs in ((a_own, a_got, (a_keep, a_send)), (b_own, b_got, (b_keep, b_send))):
        for i, out in enumerate(outs):
            add_rows(out, 0, [own, got], i * half, half)
    if a_own.shape[0] > 2 * half:
        put_small((a_keep, a_send), half, a_own[2 * half :, :].astype(f32) + a_got[2 * half :, :].astype(f32))


def plane_kernel(half, outer_half, a_own, a_got, b_own, b_got, *outs):
    groups = []
    for own, got in ((a_own, a_got), (b_own, b_got)):
        groups.append((outer_half, [own.at[0:outer_half], got.at[0:outer_half]]))
        groups.append((half - outer_half, [own.at[outer_half:half], got.at[outer_half:half]]))
    sum_parts(groups, outs, 2)
    if a_own.shape[0] > half:
        put_small(outs, half // 2, a_own[half:, :].astype(f32) + a_got[half:, :].astype(f32))


def planes_kernel(*refs):
    refs[-1][...] = paired([source[...].astype(f32) for source in refs[:-1]]).astype(bf16)


def second_planes_kernel(*refs):
    sources, out, small = refs[:-2], refs[-2], refs[-1]
    rows = out.shape[0]
    out[...] = paired([source[0:rows, :].astype(f32) for source in sources]).astype(bf16)
    small[...] = paired([source[rows:, :].astype(f32) for source in sources])


def gather_kernel(outer_half, *refs):
    sources, outs = refs[:4], refs[4:]
    half = outs[0].shape[0]
    sizes, places = [], []
    for out in outs:
        sizes += [outer_half // 4, (half - outer_half) // 4]
        places += [out.at[0:outer_half], out.at[outer_half:half]]
    gather_parts(sizes, sources, 2, places)


def pair_kernel(a_own, a_got, b_own, b_got, a_out, b_out):
    half = a_own.shape[0]
    for own, got, out in ((a_own, a_got, a_out), (b_own, b_got, b_out)):
        out[0:half, :] = own[...]
        out[half : 2 * half, :] = got[...]


def last_pair_kernel(a_own, a_got, b_own, b_got, through, through_out, a_out, b_out):
    pair_kernel(a_own, a_got, b_own, b_got, a_out, b_out)


def assemble(outer_half, a_own, a_got, b_own, b_got, outer, inner):
    half = a_own.shape[0] // 2
    mine = slot(0, 4)
    for side, sources in ((0, (a_own, a_got, a_own, a_got)), (1, (b_own, b_own, b_got, b_got))):
        second = (0, 0, 1, 1) if side == 0 else (0, 1, 0, 1)
        for k, source in enumerate(sources):
            which = jnp.bitwise_xor(mine, k)
            first = second[k] * half
            rows = outer_half
            outer[part_rows(2 * which + side, rows), :] = source[first : first + rows, :]
            if inner is not None:
                rows = half - outer_half
                inner[part_rows(2 * which + side, rows), :] = source[first + outer_half : first + half, :]


def join_kernel(mine, theirs, *outs):
    core = lax.axis_index("dir")
    rows = mine.shape[1]
    for i, out in enumerate(outs):
        out[part_rows(core, rows), :] = mine[i]
        out[part_rows(1 - core, rows), :] = theirs[i]


def matrix_columns(source, first, out):
    rows, width = out.shape
    for i in range(width // LANES):
        out[:, i * LANES : (i + 1) * LANES] = source[first + i * rows : first + (i + 1) * rows, :].astype(f32)


def gate_part_kernel(outer_half, first, *refs):
    sources, out, whole = refs[:-2], refs[-2], refs[-1]
    assemble(outer_half, *sources, whole, None)
    out[...] = whole[first : first + out.shape[0], :]


def unpack_kernel(layer, olds, outer_half, *refs):
    refs = list(refs)
    take = lambda n: [refs.pop(0) for _ in range(n)]
    sources = take(4)
    take(olds)
    outs = take(2)
    buffers = take(2)
    whole = take(2)
    (sems,) = refs
    assemble(outer_half, *sources, *whole)
    copies = []
    for i in range(2):
        matrix_columns(whole[i], 0, buffers[i])
        copies.append(pltpu.make_async_copy(buffers[i], outs[i].at[layer, 0], sems.at[i]))
        copies[-1].start()
    for copy in copies:
        copy.wait()


def gate_kernel(layer, *refs):
    mine, theirs, (out, buffer, sems) = refs[0], refs[1], refs[-3:]
    core = lax.axis_index("dir")
    half = buffer.shape[0] // 2
    width = buffer.shape[1]
    for source, which in ((mine, core), (theirs, 1 - core)):
        rows = part_rows(which, half)
        for i in range(width // LANES):
            buffer[rows, i * LANES : (i + 1) * LANES] = source[i * half : (i + 1) * half, :].astype(f32)
    copy = pltpu.make_async_copy(buffer, out.at[layer], sems.at[0])
    copy.start()
    copy.wait()


def small_pack(sums_turn, sums_back, sums_last, decay_late, decay_early, out):
    per = sums_turn.shape[1] // LANES
    thirds = decay_late.shape[1] // LANES
    out[...] = jnp.zeros_like(out)
    kinds = (
        ((sums_last, 2), (sums_back, 2)),
        ((sums_last, 3), (sums_back, 3)),
        ((sums_back, 1), (sums_turn, 1)),
        ((sums_back, 0), (sums_turn, 0)),
    )
    at = 0
    for kind in kinds:
        for source, row in kind:
            for i in range(per):
                out[at : at + 1, :] = source[row : row + 1, i * LANES : (i + 1) * LANES]
                at += 1
    for side in range(2):
        for source in (decay_late, decay_early):
            for term in range(3):
                for i in range(thirds):
                    row = 3 * side + term
                    out[at : at + 1, :] = source[row : row + 1, i * LANES : (i + 1) * LANES]
                    at += 1


def small_out_kernel(own, got, table, gain, bias, rate, turn, skip, gate):
    layers, _, states = table.shape
    thirds = states // LANES
    width = gain.shape[1]
    per = width // LANES
    at = 0
    for out in (gain, bias, skip, gate):
        for layer in range(layers):
            for i in range(per):
                out[layer : layer + 1, i * LANES : (i + 1) * LANES] = own[at : at + 1, :] + got[at : at + 1, :]
                at += 1
    other = at + layers * 3 * thirds
    for layer in range(layers):
        for i in range(thirds):
            lanes = slice(i * LANES, (i + 1) * LANES)
            rows = [(layer * 3 + t) * thirds + i for t in range(3)]
            term_re, term_im, term_scale = (
                own[at + row : at + row + 1, :] + got[other + row : other + row + 1, :] for row in rows
            )
            re, im, scale, damping, step_size, rotation, square = (
                table[layer, t : t + 1, lanes] for t in range(7)
            )
            grad_re = (term_re * re - term_im * im) / square
            grad_im = (term_re * im + term_im * re) / square
            grad_scale = term_scale / scale
            grad_damping = grad_scale * square / scale - (grad_re * re + grad_im * im)
            grad_rotation = grad_im * re - grad_re * im
            log_rate = grad_damping * damping
            rate[layer, 0:1, lanes] = log_rate
            turn[layer, 0, 0:1, lanes] = grad_rotation * step_size
            turn[layer, 0, 1:2, lanes] = log_rate + grad_rotation * rotation


class Order:
    def __init__(self):
        self.tile = None

    def run(self, kernel, outs, operands, scratch=(), flops=0, name=None, spare=8, after=(), free_outs=0, alias=None,
            semaphores=0, cost=0, far=False):
        whole = pl.BlockSpec(memory_space=pltpu.VMEM)
        free = pl.BlockSpec(memory_space=pl.ANY)
        waits = list(after) + ([] if self.tile is None else [self.tile])
        inputs, results = len(operands), len(outs)
        skipped = len(waits)

        def body(*refs):
            token = refs[skipped + inputs]
            token[...] = jnp.zeros_like(token)
            kernel(*refs[skipped : skipped + inputs], *refs[skipped + inputs + 1 :])

        shapes = [jax.ShapeDtypeStruct((8, LANES), f32)]
        shapes += [jax.ShapeDtypeStruct(shape, dtype) for shape, dtype in outs]
        held = sum(jnp.dtype(dtype).itemsize * functools.reduce(lambda a, b: a * b, shape) for shape, dtype in scratch)
        specs = [free] * skipped + [pl.BlockSpec(memory_space=pltpu.HBM) if far else whole] * inputs
        aliases = {}
        if alias is not None:
            for operand, out in alias.items():
                specs[skipped + operand] = free
                aliases[skipped + operand] = out + 1
        extra = [pltpu.SemaphoreType.DMA((semaphores,))] if semaphores else []
        results = pl.pallas_call(
            body,
            out_shape=shapes,
            in_specs=specs,
            out_specs=[whole] + [free] * free_outs + [whole] * (results - free_outs),
            scratch_shapes=[pltpu.VMEM(shape, dtype) for shape, dtype in scratch] + extra,
            input_output_aliases=aliases,
            compiler_params=pltpu.CompilerParams(vmem_limit_bytes=held + spare * 2**20),
            cost_estimate=pl.CostEstimate(flops=int(1 + cost * 1e9), bytes_accessed=int(1 + cost * 3e6), transcendentals=0),
            name=name,
        )(*waits, *operands)
        self.tile = results[0]
        return results[1:]


def swap(value):
    return lax.ppermute(value, "dir", [(0, 1), (1, 0)])


def across(value, bits):
    count = lax.axis_size("seq")
    return lax.ppermute(value, "seq", [(i, i ^ bits) for i in range(count)])


def beyond(value):
    bit = 4
    while (1 << bit) < lax.axis_size("seq"):
        value = (value.astype(f32) + across(value, 1 << bit).astype(f32)).astype(value.dtype)
        bit += 1
    return value


def exchanged(payload, row_devices):
    count = lax.axis_size("seq")
    group = 2 * row_devices
    groups = None
    if count != row_devices:
        groups = [list(range(i, i + group)) for i in range(0, 2 * count, group)]
    return lax.all_to_all(payload, ("seq", "dir"), 0, 0, tiled=True, axis_index_groups=groups)


def sent(parts, low_bit):
    return [parts[0]] + [across(parts[k], k << low_bit) for k in (1, 2, 3)]


def shared(value, low_bit):
    return [value] + [across(value, k << low_bit) for k in (1, 2, 3)]


def body(
    tokens,
    segment_ids,
    norm_gain,
    norm_bias,
    input_matrix,
    output_matrix,
    rate_params,
    turn_params,
    skip_weight,
    glu_weight,
    glu_bias,
    cotangent,
):
    chip_rows, width = tokens.shape
    rows = chip_rows // 2
    layers = rate_params.shape[0]
    states = rate_params.shape[2]
    row_devices = LENGTH // chip_rows
    order = Order()
    here = functools.partial

    in_own, out_own = input_matrix, output_matrix
    in_oth = swap(input_matrix)
    rate_oth, turn_oth = swap(rate_params), swap(turn_params)
    out_oth = swap(output_matrix)
    segments = segment_ids.reshape(chip_rows // LANES, LANES)

    full = ((rows, width), f32)
    full_low = ((rows, width), bf16)
    columns = ((width // LANES, rows, LANES), f32)
    wide = ((rows, 2 * states), f32)
    wide_low = ((rows, 2 * states), bf16)
    ends = ((8, 2 * states), f32)
    payload_shape = ((2 * row_devices, 8, LANES), bf16)
    narrow = ((rows, LANES), f32)
    tile = ((8, LANES), f32)
    sums_shape = ((8, width), f32)
    decay_shape = ((8, states), f32)
    table_shape = ((layers, 16, states), f32)
    places = ((8, 2 * states), f32)
    in_size = width * (2 * states // LANES)
    out_size = 2 * states * (width // LANES)
    glu_size = width // 2 * (width // LANES)
    outer_size = out_size + glu_size
    outer_pack = ((outer_size, LANES), bf16)
    inner_pack = ((in_size, LANES), bf16)
    one = 2.0 * rows * width * 2 * states
    gate = 2.0 * rows * width * width
    scan = 1e9

    x0, normed0, inv0 = order.run(
        here(open_kernel, row_devices),
        [full, full, narrow],
        [tokens],
        [full_low, columns],
        far=True,
        semaphores=1,
        name="open_norm",
        cost=10,
    )
    (
        mixed0, drive_own0, drive_oth0, keep_own, keep_oth, whole, ends_own, ends_oth, payload, table, tiles, ids,
    ) = order.run(
        here(open_second_kernel, row_devices),
        [full_low, wide, wide, narrow, narrow, ((2, 8, LANES), f32), ends, ends, payload_shape, table_shape,
         ((layers, 16, LANES), f32), tile],
        [normed0, segments, norm_gain, norm_bias, rate_params, turn_params, rate_oth, turn_oth, in_own, in_oth],
        [tile],
        name="open_scan",
        after=[out_oth],
    )
    gathered = exchanged(payload, row_devices)
    (
        low_own0, low_oth0, combined0, phi0, sig0, act_low0, x1, normed1, inv1, mixed1, drive_own1, drive_oth1,
        ends_own, ends_oth, payload,
    ) = order.run(
        here(mid_kernel, row_devices),
        [wide_low, wide_low, full, full, full, full_low, full, full, narrow, full_low, wide, wide, ends, ends,
         payload_shape],
        [gathered, ends_own, ends_oth, drive_own0, drive_oth0, keep_own, keep_oth, whole, table, tiles,
         ids, out_own, out_oth, x0, normed0, norm_gain, norm_bias, skip_weight, glu_weight, glu_bias, in_own, in_oth],
        [places, tile, full, wide, wide],
        flops=4 * one + gate + 3 * scan,
        name="mid",
    )
    gathered = exchanged(payload, row_devices)
    (
        low_own1, low_oth1, out1, grad1, combined_grad1, grad_own1, grad_oth1, ends_own, ends_oth, payload,
        sums_turn, mine, theirs,
    ) = order.run(
        here(turn_kernel, row_devices),
        [wide_low, wide_low, full, full, full, wide, wide, ends, ends, payload_shape, sums_shape, outer_pack, outer_pack],
        [gathered, ends_own, ends_oth, drive_own1, drive_oth1, keep_own, keep_oth, whole, table, tiles,
         ids, out_own, out_oth, x1, normed1, norm_gain, norm_bias, skip_weight, glu_weight, glu_bias, cotangent],
        [places, tile, full, full, full, full, columns, wide, wide, full_low, full_low, full_low],
        flops=4 * one + 2 * gate + 4 * scan,
        name="turn",
    )
    first_outer = [mine, swap(theirs)]
    gathered = exchanged(payload, row_devices)
    in_low_own1, in_low_oth1, decay_sums1, mine, theirs = order.run(
        here(scan_kernel, 1, row_devices),
        [wide_low, wide_low, decay_shape, inner_pack, inner_pack],
        [gathered, ends_own, ends_oth, grad_own1, grad_oth1, keep_own, keep_oth, whole, table, tiles,
         ids, low_own1, low_oth1, drive_own1, drive_oth1, mixed1],
        [places, tile, wide, wide],
        name="scan_one",
        after=[first_outer[1]],
    )
    first_inner = [mine, swap(theirs)]
    (
        grad0, combined_grad0, grad_own0, grad_oth0, ends_own, ends_oth, payload, sums_back, mine_outer, theirs_outer,
    ) = order.run(
        here(back_kernel, row_devices),
        [full, full, wide, wide, ends, ends, payload_shape, sums_shape, outer_pack, outer_pack],
        [in_low_own1, in_low_oth1, keep_own, keep_oth, whole, table, tiles, ids, in_own, in_oth, out_own, out_oth, grad1,
         combined_grad1, normed1, inv1, norm_gain, norm_bias, skip_weight, glu_weight, combined0, phi0, sig0, normed0,
         act_low0, low_own0, low_oth0],
        [full, full_low, full_low],
        name="back",
    )
    second_outer = [mine_outer, swap(theirs_outer)]
    outer_half = outer_size // 8
    half = outer_half + in_size // 8
    share_rows = half // 2
    small_rows = -(-(4 * layers * (width // LANES) + 6 * layers * (states // LANES)) // 16) * 16
    small_shape = ((small_rows, LANES), f32)

    def low(count):
        return ((count, LANES), bf16)

    def from_cores(packs, extra, sums, name, after=()):
        a_keep, a_send, b_keep, b_send, _ = order.run(
            here(cores_kernel, outer_half, half),
            [low(2 * half + extra)] * 2 + [low(2 * half)] * 2 + [small_shape],
            packs + sums,
            name=name,
            after=after,
            cost=CORES_COST,
        )
        return [a_keep, across(a_send, 1), b_keep, across(b_send, 2)]

    def from_first(parts, extra, name, after=()):
        a_keep, a_send, b_keep, b_send = order.run(
            here(half_kernel, half), [low(half + extra)] * 2 + [low(half)] * 2, parts, name=name, after=after
        )
        return [a_keep, across(a_send, 2), b_keep, across(b_send, 1)]

    def from_second(parts, extra, name, cost=0):
        return sent(
            order.run(
                here(plane_kernel, half, outer_half), [low(share_rows + extra)] * 4, parts, name=name, cost=cost
            ),
            2,
        )

    def gathered_half(parts, name, after=(), cost=0):
        a_half, b_half = order.run(
            here(gather_kernel, outer_half), [low(half)] * 2, parts, name=name, after=after, cost=cost
        )
        return a_half, across(a_half, 2), b_half, across(b_half, 1)

    def gathered_whole(halves, name):
        a_pair, b_pair = order.run(pair_kernel, [low(2 * half)] * 2, list(halves), name=name)
        return [a_pair, across(a_pair, 1), b_pair, across(b_pair, 2)]

    first = from_cores(first_outer + first_inner, 0, [], "first_cores")
    (payload,) = order.run(relay_kernel, [payload_shape], [payload], name="relay", cost=50)
    gathered = exchanged(payload, row_devices)
    first = from_first(first, 0, "first_half", [gathered])
    in_low_own0, in_low_oth0, decay_sums0, mine, theirs = order.run(
        here(scan_kernel, 0, row_devices),
        [wide_low, wide_low, decay_shape, inner_pack, inner_pack],
        [gathered, ends_own, ends_oth, grad_own0, grad_oth0, keep_own, keep_oth, whole, table, tiles,
         ids, low_own0, low_oth0, drive_own0, drive_oth0, mixed0],
        [places, tile, wide, wide],
        name="scan_zero",
        after=[second_outer[1]],
    )
    second_inner = [mine, swap(theirs)]
    halves, sums_last = order.run(
        final_kernel,
        [((2, rows, width), f32), sums_shape],
        [in_low_own0, in_low_oth0, in_own, in_oth, grad0, combined_grad0, normed0, inv0, norm_gain, skip_weight, out1],
        [full, columns, columns],
        name="final_norm",
    )
    first = from_second(first, 0, "first_plane", 50)
    second = from_cores(
        second_outer + second_inner, small_rows, [sums_turn, sums_back, sums_last, decay_sums0, decay_sums1],
        "second_cores",
    )
    (share,) = order.run(planes_kernel, [low(share_rows)], first, name="first_planes", cost=50)
    first = shared(beyond(share), 2)
    second = from_first(second, small_rows, "second_half")
    first = gathered_half(first, "first_gather", cost=50)
    second = from_second(second, small_rows, "second_plane")
    share, small = order.run(second_planes_kernel, [low(share_rows), small_shape], second, name="second_planes")
    second = shared(beyond(share), 2)
    first = gathered_whole(first, "first_pair")
    small = beyond(small)
    got_small = swap(small)
    in_shape, out_shape = input_matrix.shape, output_matrix.shape

    def gate_part(quarters, name):
        (value,) = order.run(
            here(gate_part_kernel, outer_half, out_size), [low(glu_size)], quarters, [outer_pack], name=name
        )
        return value

    def gate_out(layer, mine, theirs, old, name):
        return order.run(
            here(gate_kernel, layer), [(glu_weight.shape, f32)], [mine, theirs] + old, [((width, width), f32)],
            name=name, free_outs=1, alias={2: 0} if old else None, semaphores=1,
        )

    def unpack(quarters, layer, old, name):
        return order.run(
            here(unpack_kernel, layer, len(old), outer_half),
            [(out_shape, f32), (in_shape, f32)],
            quarters + old,
            [(out_shape[2:], f32), (in_shape[2:], f32), outer_pack, inner_pack],
            name=name,
            free_outs=2,
            alias={4 + i: i for i in range(len(old))},
            semaphores=2,
        )

    second = gathered_half(second, "second_gather", cost=50)
    halves, a_pair, b_pair = order.run(
        last_pair_kernel, [((2, rows, width), f32), low(2 * half), low(2 * half)], list(second) + [halves],
        name="second_pair", free_outs=1, alias={4: 0}, after=[first[1], first[3]],
    )
    second = [a_pair, across(a_pair, 1), b_pair, across(b_pair, 2)]
    gate_one = gate_part(first, "gate_one")
    got_one = swap(gate_one)
    results = unpack(first, 1, [], "unpack_one")
    gain_grad, bias_grad, rate_grad, turn_grad, skip_grad, gate_grad = order.run(
        small_out_kernel,
        [((layers, width), f32), ((layers, width), f32), (rate_params.shape, f32), (turn_params.shape, f32),
         ((layers, width), f32), ((layers, width), f32)],
        [small, got_small, table],
        name="small_out",
    )
    whole_rows = ((chip_rows, width), f32)
    block_output, tokens_grad = order.run(
        join_kernel, [whole_rows, whole_rows], [halves, swap(halves)], name="join"
    )
    glu_all = gate_out(1, gate_one, got_one, [], "gate_out_one")
    gate_zero = gate_part(second, "gate_zero")
    got_zero = swap(gate_zero)
    out_all, in_all = unpack(second, 0, list(results), "unpack_zero")
    (glu_all,) = gate_out(0, gate_zero, got_zero, list(glu_all), "gate_out_zero")
    return (
        block_output,
        tokens_grad,
        gain_grad,
        bias_grad,
        in_all,
        out_all,
        rate_grad,
        turn_grad,
        skip_grad,
        glu_all,
        gate_grad,
    )


def solution(mesh):
    return jax.shard_map(
        body,
        mesh=mesh,
        in_specs=(
            P("seq", None),
            P("seq"),
            P(),
            P(),
            P(None, "dir", None, None),
            P(None, "dir", None, None),
            P(None, "dir", None),
            P(None, "dir", None, None),
            P(),
            P(),
            P(),
            P("seq", None),
        ),
        out_specs=(
            P("seq", None),
            P("seq", None),
            P(),
            P(),
            P(None, "dir", None, None),
            P(None, "dir", None, None),
            P(None, "dir", None),
            P(None, "dir", None, None),
            P(),
            P(),
            P(),
        ),
        check_vma=False,
    )
```

```python
import functools

import jax
import jax.numpy as jnp
from jax import lax
from jax.experimental import pallas as pl
from jax.experimental.pallas import tpu as pltpu
from jax.sharding import PartitionSpec as P

LENGTH = 16384
LONGEST_RUN = 8192

eps = 1e-05
inv_root_two = 0.7071067811865476
inv_root_two_pi = 0.3989422804014327

f32 = jnp.float32
bf16 = jnp.bfloat16


LANES = 128
ELEMENT_ROWS = 512
UNROLL = 8
CORES_COST = 0


def core_place(row_devices):
    core = lax.axis_index("dir")
    return core, lax.rem(lax.axis_index("seq"), row_devices) * 2 + core


def dot(a, b):
    return jnp.dot(a, b, preferred_element_type=f32)


def dot_nt(a, b):
    return lax.dot_general(a, b, (((1,), (1,)), ((), ())), preferred_element_type=f32)


def dot_tn(a, b):
    return lax.dot_general(a, b, (((0,), (0,)), ((), ())), preferred_element_type=f32)


def squared(re, im, times):
    for _ in range(times):
        re, im = re * re - im * im, 2.0 * re * im
    return re, im


def over_blocks(rows, step, init=()):
    def one(i, carry):
        return step(pl.multiple_of(i * ELEMENT_ROWS, ELEMENT_ROWS), carry)

    return lax.fori_loop(0, rows // ELEMENT_ROWS, one, init)


def fold(values):
    total = values[0:8]
    for start in range(8, values.shape[0], 8):
        total = total + values[start : start + 8]
    return total


class Lanes:
    def __init__(self, rows_ref, tiles_ref, layer, adjoint, spans, rows):
        states = rows_ref.shape[2]
        self.states = states
        self.rows_ref, self.layer = rows_ref, layer
        flip = -1.0 if adjoint else 1.0
        self.step = []
        self.run = []
        self.block = []
        for side in range(2):
            row = 8 * side
            re = rows_ref[layer, row : row + 1, :]
            im = rows_ref[layer, row + 1 : row + 2, :] * flip
            self.step.append((jnp.broadcast_to(re, (8, states)), jnp.broadcast_to(im, (8, states))))
            self.run.append(squared(re, im, (spans - 1).bit_length()))
            thirds = states // LANES
            tile_re = tiles_ref[layer, 8 * side : 8 * side + thirds, :]
            tile_im = tiles_ref[layer, 8 * side + thirds : 8 * side + 2 * thirds, :] * flip
            self.block.append(squared(tile_re, tile_im, (rows - 1).bit_length()))

    def scaling(self, side):
        row = self.rows_ref[self.layer, 8 * side + 2 : 8 * side + 3, :]
        return jnp.concatenate([row, row], 1)


def sweep(first_forward, drives, masks, lanes, init, visit=None, totals=()):
    states = lanes.states
    span = drives[0].shape[0] // 8

    def step(i, carry):
        values, sums = carry
        up = pl.multiple_of(i * 8, 8)
        down = pl.multiple_of((span - 1 - i) * 8, 8)
        places = (jnp.where(first_forward, up, down), jnp.where(first_forward, down, up))
        new = []
        for side in range(2):
            rows = pl.ds(pl.multiple_of(places[side], 8), 8)
            keep = masks[side][rows, :]
            keep = jnp.concatenate([keep] * (states // LANES), 1)
            step_re, step_im = lanes.step[side]
            step_re, step_im = step_re * keep, step_im * keep
            re, im = values[side]
            drive_re = drives[side][rows, :states]
            drive_im = drives[side][rows, states:]
            re, im = (
                step_re * re - step_im * im + drive_re,
                step_re * im + step_im * re + drive_im,
            )
            new.append((re, im))
            if visit is not None:
                sums = visit(side, rows, re, im, sums)
        return tuple(new), sums

    return lax.fori_loop(0, span, step, (init, totals), unroll=UNROLL if totals else span)


def run_chain(first_up, lanes, side, ends, whole, start, places):
    states = lanes.states
    power_re, power_im = lanes.run[side]
    re, im = start
    for i in range(8):
        s = jnp.where(first_up, i, 7 - i)
        row = pl.ds(s, 1)
        if places is not None:
            places[row, :states] = re
            places[row, states:] = im
        passes = whole[row, :]
        passes = jnp.concatenate([passes] * (states // LANES), 1)
        pass_re, pass_im = power_re * passes, power_im * passes
        end_re, end_im = ends[row, :states], ends[row, states:]
        re, im = (end_re + pass_re * re - pass_im * im, end_im + pass_re * im + pass_im * re)
    return re, im


def first_pass(running_up, place, drives, masks, wholes, lanes, ids_ref, ends, payload):
    states = lanes.states
    thirds = states // LANES
    nothing = jnp.zeros((8, states), f32)
    zero = (nothing, nothing)
    values, _ = sweep(running_up, drives, masks, lanes, (zero, zero))
    tiles = []
    for side in range(2):
        ends[side][:, :states] = values[side][0]
        ends[side][:, states:] = values[side][1]
        upward = running_up if side == 0 else jnp.logical_not(running_up)
        start = jnp.zeros((1, states), f32)
        re, im = run_chain(upward, lanes, side, ends[side], wholes[side], (start, start), None)
        rows = [part[:, LANES * i : LANES * (i + 1)] for part in (re, im) for i in range(thirds)]
        tiles.append(jnp.concatenate(rows + [ids_ref[0:2, :]], 0))
    for i in range(payload.shape[0]):
        to_later = jnp.logical_xor(running_up, i < place)
        payload[i] = jnp.where(to_later, tiles[0], tiles[1]).astype(payload.dtype)


def entering(upward, place, lanes, side, gathered, ids_ref, small):
    states = lanes.states
    thirds = states // LANES
    count = gathered.shape[0]
    rows = lanes.token_rows
    block_re, block_im = lanes.block[side]
    re = jnp.zeros((thirds, LANES), f32)
    im = jnp.zeros((thirds, LANES), f32)
    key = jnp.where(upward, ids_ref[0:1, :], ids_ref[1:2, :])
    for distance in range(min(count - 1, LONGEST_RUN // rows), 0, -1):
        source = jnp.where(upward, place - distance, place + distance)
        inside = jnp.logical_and(source >= 0, source < count)
        source = jnp.clip(source, 0, count - 1)
        sent = gathered[source].astype(f32)
        sent_re, sent_im = sent[0:thirds], sent[thirds : 2 * thirds]
        sent_key = jnp.where(upward, sent[7:8], sent[6:7])
        joined = jnp.where(jnp.logical_and(sent_key == key, inside), 1.0, 0.0)
        re, im = (
            joined * sent_re + block_re * re - block_im * im,
            joined * sent_im + block_re * im + block_im * re,
        )
    small[0:thirds, :] = re
    small[thirds : 2 * thirds, :] = im
    wide_re = jnp.concatenate([small[i : i + 1, :] for i in range(thirds)], 1)
    wide_im = jnp.concatenate([small[thirds + i : thirds + i + 1, :] for i in range(thirds)], 1)
    return wide_re, wide_im


def second_starts(running_up, place, lanes, gathered, ids_ref, ends, wholes, places, small):
    init = []
    states = lanes.states
    for side in range(2):
        upward = running_up if side == 0 else jnp.logical_not(running_up)
        start = entering(upward, place, lanes, side, gathered, ids_ref, small)
        run_chain(upward, lanes, side, ends[side], wholes[side], start, places)
        init.append((places[:, :states], places[:, states:]))
    return tuple(init)


def make_lanes(rows_ref, tiles_ref, layer, adjoint, token_rows):
    lanes = Lanes(rows_ref, tiles_ref, layer, adjoint, token_rows // 8, token_rows)
    lanes.token_rows = token_rows
    return lanes


def standardise(x):
    width = x.shape[1]
    average = jnp.sum(x, 1, keepdims=True) * (1.0 / width)
    centred = x - average
    inv_scale = lax.rsqrt(jnp.sum(centred * centred, 1, keepdims=True) * (1.0 / width) + eps)
    return centred * inv_scale, inv_scale


def fill_columns(columns, values):
    for i in range(columns.shape[0]):
        columns[i] = values[:, i * LANES : (i + 1) * LANES].astype(columns.dtype)


def tile_order(columns, first, count, span):
    tiles = [
        jnp.concatenate([columns[i, pl.ds(first + j, 8, stride=span), :] for i in range(columns.shape[0])], 1)
        for j in range(count)
    ]
    return jnp.concatenate(tiles, 0)


def store_token_order(columns, first, values, span):
    for j in range(values.shape[0] // 8):
        for i in range(columns.shape[0]):
            columns[i, pl.ds(first + j, 8, stride=span), :] = values[8 * j : 8 * j + 8, i * LANES : (i + 1) * LANES]


def join_columns(out, columns):
    for i in range(columns.shape[0]):
        out[:, i * LANES : (i + 1) * LANES] = columns[i]


def one_minus_exp(x):
    series = jnp.ones_like(x)
    for term in range(12, 1, -1):
        series = 1.0 - x * (1.0 / term) * series
    return jnp.where(x < 0.5, x * series, 1.0 - jnp.exp(-x))


def table_rows(table, layer, base, rate, turn):
    frequency = turn[layer, 0, 0:1, :]
    log_step = turn[layer, 0, 1:2, :]
    step_size = jnp.exp(log_step)
    damping = jnp.exp(rate[layer, 0:1, :] + log_step)
    magnitude = jnp.exp(-damping)
    rotation = frequency * step_size
    square = magnitude * magnitude
    rows = (
        magnitude * jnp.cos(rotation), magnitude * jnp.sin(rotation), jnp.sqrt(one_minus_exp(2.0 * damping)), damping,
        step_size, rotation, square,
    )
    for i, row in enumerate(rows):
        table[layer, base + i : base + i + 1, :] = row


def open_kernel(row_devices, tokens_from, x_out, normed_out, inv_out, tokens, natural, sems):
    copy = pltpu.make_async_copy(
        tokens_from.at[part_rows(lax.axis_index("dir"), tokens.shape[0])], tokens, sems.at[0]
    )
    copy.start()
    copy.wait()
    rows = x_out.shape[0]
    span = rows // 8
    fill_columns(natural, tokens[...].astype(f32))

    def element(start, carry):
        x = tile_order(natural, start // 8, ELEMENT_ROWS // 8, span)
        normed, inv_scale = standardise(x)
        block = pl.ds(start, ELEMENT_ROWS)
        x_out[block, :] = x
        normed_out[block, :] = normed
        inv_out[block, :] = jnp.broadcast_to(inv_scale, (ELEMENT_ROWS, LANES))
        return carry

    over_blocks(rows, element)


def open_masks_kernel(
    row_devices, segments, rate, turn, cotangent_from, table, keep_own, keep_oth, whole_out, ids, grad_out, rows8, natural,
    part, sems,
):
    core, _ = core_place(row_devices)
    rows = grad_out.shape[0]
    span = rows // 8
    copy = pltpu.make_async_copy(cotangent_from.at[part_rows(core, rows)], part, sems.at[0])
    copy.start()
    table[...] = jnp.zeros_like(table)
    for layer in range(table.shape[0]):
        table_rows(table, layer, 0, rate, turn)
    number = segments[...].astype(f32)
    count = number.shape[0]
    lane = lax.broadcasted_iota(jnp.int32, number.shape, 1)
    row = lax.broadcasted_iota(jnp.int32, number.shape, 0)
    back = pltpu.roll(number, 1, 1)
    back = jnp.where(lane == 0, pltpu.roll(back, 1, 0), back)
    ahead = pltpu.roll(number, LANES - 1, 1)
    ahead = jnp.where(lane == LANES - 1, pltpu.roll(ahead, count - 1, 0), ahead)
    edge_first = jnp.logical_and(lane == 0, row == 0)
    edge_last = jnp.logical_and(lane == LANES - 1, row == count - 1)
    up_keep = jnp.where(jnp.logical_or(number == back, edge_first), 1.0, 0.0)
    down_keep = jnp.where(jnp.logical_or(number == ahead, edge_last), 1.0, 0.0)
    per = LANES // span
    used = 8 // per
    for side, out in ((0, keep_own), (1, keep_oth)):
        rows8[0:count, :] = jnp.where(core == side, up_keep, down_keep)
        half = rows8[pl.ds(core * used, used), :]
        runs = jnp.concatenate([half[s // per : s // per + 1] for s in range(8)], 0)
        place = lax.broadcasted_iota(jnp.int32, (8, LANES), 1)
        sub = lax.broadcasted_iota(jnp.int32, (8, LANES), 0)
        first = lax.rem(sub, per) * span
        inside = jnp.logical_and(place >= first, place < first + span)
        least = jnp.min(jnp.where(inside, runs, 1.0), 1, keepdims=True)
        whole_out[side] = jnp.broadcast_to(least, (8, LANES))
        step = lax.broadcasted_iota(jnp.int32, (span, 8, LANES), 0)
        spread = jnp.where(step == (place - first)[None], runs[None], 0.0)
        spread = spread.reshape(span * 8, LANES).astype(bf16)
        out[...] = dot(spread, jnp.ones((LANES, LANES), bf16))
    rows8[0:count, :] = number
    first_row = rows8[pl.ds(core * used, 1), :]
    last_row = rows8[pl.ds(core * used + used - 1, 1), :]
    ids[...] = jnp.zeros_like(ids)
    ids[0:1, :] = jnp.broadcast_to(first_row[:, 0:1], (1, LANES))
    ids[1:2, :] = jnp.broadcast_to(last_row[:, LANES - 1 : LANES], (1, LANES))
    copy.wait()
    fill_columns(natural, part[...])
    grad_out[...] = tile_order(natural, 0, span, span)


def open_second_kernel(
    row_devices,
    normed,
    gain,
    bias,
    table_in,
    keep_own,
    keep_oth,
    whole,
    ids,
    rate_oth,
    turn_oth,
    in_own,
    in_oth,
    mixed_low,
    drive_own,
    drive_oth,
    ends_own,
    ends_oth,
    payload,
    table,
    tiles,
):
    core, place = core_place(row_devices)
    rows = normed.shape[0]
    span = rows // 8

    def element(start, carry):
        block = pl.ds(start, ELEMENT_ROWS)
        mixed_low[block, :] = (normed[block, :] * gain[0:1, :] + bias[0:1, :]).astype(bf16)
        return carry

    over_blocks(rows, element)
    table[...] = table_in[...]
    tiles[...] = jnp.zeros_like(tiles)
    thirds = table.shape[2] // LANES
    for layer in range(table.shape[0]):
        table_rows(table, layer, 8, rate_oth, turn_oth)
        for side in range(2):
            for part in range(2):
                for i in range(thirds):
                    at = 8 * side + part * thirds + i
                    tiles[layer, at : at + 1, :] = table[
                        layer, 8 * side + part : 8 * side + part + 1, i * LANES : (i + 1) * LANES
                    ]

    for side, (matrix, drive) in enumerate(((in_own, drive_own), (in_oth, drive_oth))):
        scale = table[0, 8 * side + 2 : 8 * side + 3, :]
        drive[...] = dot(mixed_low[...], matrix[0, 0]) * jnp.concatenate([scale, scale], 1)
    lanes = make_lanes(table, tiles, 0, False, rows)
    first_pass(
        core == 0,
        core_place(row_devices)[1],
        (drive_own, drive_oth),
        (keep_own, keep_oth),
        (whole.at[0], whole.at[1]),
        lanes,
        ids,
        (ends_own, ends_oth),
        payload,
    )


def forward_states(layer, info, gathered, ends, drives, masks, whole, rows_ref, tiles_ref, ids, states, lows, places, small):
    rows = drives[0].shape[0]
    lanes = make_lanes(rows_ref, tiles_ref, layer, False, rows)
    core, place = info
    running_up = core == 0
    init = second_starts(
        running_up, place, lanes, gathered, ids, ends, (whole.at[0], whole.at[1]), places, small
    )
    width = lanes.states

    def visit(side, where, re, im, sums):
        states[side][where, :width] = re
        states[side][where, width:] = im
        return sums

    sweep(running_up, drives, masks, lanes, init, visit)
    for side in range(2):
        lows[side][...] = states[side][...].astype(bf16)


def mid_kernel(
    row_devices,
    gathered,
    ends_own,
    ends_oth,
    drive_own,
    drive_oth,
    keep_own,
    keep_oth,
    whole,
    rows_ref,
    tiles_ref,
    ids,
    out_own,
    out_oth,
    x_in,
    normed,
    gain,
    bias,
    skip,
    glu,
    glu_bias,
    in_own,
    in_oth,
    low_own,
    low_oth,
    combined_out,
    phi_out,
    sig_out,
    act_low,
    x_out,
    normed_out,
    inv_out,
    mixed_out,
    next_own,
    next_oth,
    next_ends_own,
    next_ends_oth,
    payload,
    places,
    small,
    wide,
    states_own,
    states_oth,
):
    info = core_place(row_devices)
    rows = x_in.shape[0]
    masks = (keep_own, keep_oth)
    forward_states(
        0, info, gathered, (ends_own, ends_oth), (drive_own, drive_oth), masks, whole, rows_ref, tiles_ref,
        ids, (states_own, states_oth), (low_own, low_oth), places, small,
    )
    wide[...] = dot(low_own[...], out_own[0, 0]) + dot(low_oth[...], out_oth[0, 0])

    def element(start, carry):
        block = pl.ds(start, ELEMENT_ROWS)
        mixed = normed[block, :] * gain[0:1, :] + bias[0:1, :]
        combined = wide[block, :] + skip[0:1, :] * mixed
        phi = 0.5 * (1.0 + lax.erf(combined * inv_root_two))
        combined_out[block, :] = combined
        phi_out[block, :] = phi
        act_low[block, :] = (combined * phi).astype(bf16)
        return carry

    over_blocks(rows, element)
    wide[...] = dot(act_low[...], glu[0])

    def element_two(start, carry):
        block = pl.ds(start, ELEMENT_ROWS)
        sig = jax.nn.sigmoid(wide[block, :] + glu_bias[0:1, :])
        sig_out[block, :] = sig
        x = x_in[block, :] + combined_out[block, :] * phi_out[block, :] * sig
        x_out[block, :] = x
        after, inv_scale = standardise(x)
        normed_out[block, :] = after
        inv_out[block, :] = jnp.broadcast_to(inv_scale, (ELEMENT_ROWS, LANES))
        mixed_out[block, :] = (after * gain[1:2, :] + bias[1:2, :]).astype(bf16)
        return carry

    over_blocks(rows, element_two)
    for side, (matrix, out) in enumerate(((in_own, next_own), (in_oth, next_oth))):
        scale = rows_ref[1, 8 * side + 2 : 8 * side + 3, :]
        out[...] = dot(mixed_out[...], matrix[1, 0]) * jnp.concatenate([scale, scale], 1)
    lanes = make_lanes(rows_ref, tiles_ref, 1, False, rows)
    first_pass(
        info[0] == 0,
        info[1],
        (next_own, next_oth),
        masks,
        (whole.at[0], whole.at[1]),
        lanes,
        ids,
        (next_ends_own, next_ends_oth),
        payload,
    )


def backward_half(
    layer, info, grad, combined, phi, sig, normed, gain, bias, skip, glu, out_own, out_oth, masks, whole,
    rows_ref, tiles_ref, ids, gate_low, combined_grad, combined_low, grad_own, grad_oth, ends, payload, sums, wide,
):
    rows = grad.shape[0]
    width = grad.shape[1]
    zero = jnp.zeros((8, width), f32)

    def element(start, carry):
        block = pl.ds(start, ELEMENT_ROWS)
        gate = sig[block, :]
        gate_grad = grad[block, :] * (combined[block, :] * phi[block, :]) * gate * (1.0 - gate)
        gate_low[block, :] = gate_grad.astype(bf16)
        return carry + fold(gate_grad)

    bias_sum = over_blocks(rows, element, zero)
    wide[...] = dot_nt(gate_low[...], glu[layer])

    def element_two(start, carry):
        block = pl.ds(start, ELEMENT_ROWS)
        value = combined[block, :]
        activation_grad = grad[block, :] * sig[block, :] + wide[block, :]
        slope = phi[block, :] + value * (jnp.exp(-0.5 * value * value) * inv_root_two_pi)
        result = activation_grad * slope
        combined_grad[block, :] = result
        combined_low[block, :] = result.astype(bf16)
        mixed = normed[block, :] * gain[layer : layer + 1, :] + bias[layer : layer + 1, :]
        return carry + fold(result * mixed)

    skip_sum = over_blocks(rows, element_two, zero)
    sums[0:1, :] = jnp.sum(bias_sum, 0, keepdims=True)
    sums[1:2, :] = jnp.sum(skip_sum, 0, keepdims=True)
    grad_own[...] = dot_nt(combined_low[...], out_own[layer, 0])
    grad_oth[...] = dot_nt(combined_low[...], out_oth[layer, 0])
    lanes = make_lanes(rows_ref, tiles_ref, layer, True, rows)
    first_pass(
        info[0] == 1,
        info[1],
        (grad_own, grad_oth),
        (masks[1], masks[0]),
        (whole.at[1], whole.at[0]),
        lanes,
        ids,
        ends,
        payload,
    )


def turn_kernel(
    row_devices,
    gathered,
    ends_own,
    ends_oth,
    drive_own,
    drive_oth,
    keep_own,
    keep_oth,
    whole,
    rows_ref,
    tiles_ref,
    ids,
    out_own,
    out_oth,
    x_in,
    normed,
    gain,
    bias,
    skip,
    glu,
    glu_bias,
    grad_in,
    low_own,
    low_oth,
    block_out,
    combined_grad,
    grad_own,
    grad_oth,
    next_ends_own,
    next_ends_oth,
    payload,
    sums,
    mine,
    theirs,
    places,
    small,
    wide,
    combined,
    phi_rows,
    sig_rows,
    states_own,
    states_oth,
    act_low,
    gate_low,
    combined_low,
):
    info = core_place(row_devices)
    rows = x_in.shape[0]
    span = rows // 8
    masks = (keep_own, keep_oth)
    forward_states(
        1, info, gathered, (ends_own, ends_oth), (drive_own, drive_oth), masks, whole, rows_ref, tiles_ref,
        ids, (states_own, states_oth), (low_own, low_oth), places, small,
    )
    wide[...] = dot(low_own[...], out_own[1, 0]) + dot(low_oth[...], out_oth[1, 0])

    def element(start, carry):
        block = pl.ds(start, ELEMENT_ROWS)
        mixed = normed[block, :] * gain[1:2, :] + bias[1:2, :]
        value = wide[block, :] + skip[1:2, :] * mixed
        phi = 0.5 * (1.0 + lax.erf(value * inv_root_two))
        combined[block, :] = value
        phi_rows[block, :] = phi
        act_low[block, :] = (value * phi).astype(bf16)
        return carry

    over_blocks(rows, element)
    wide[...] = dot(act_low[...], glu[1])

    def element_two(start, carry):
        block = pl.ds(start, ELEMENT_ROWS)
        sig = jax.nn.sigmoid(wide[block, :] + glu_bias[1:2, :])
        sig_rows[block, :] = sig
        block_out[block, :] = x_in[block, :] + combined[block, :] * phi_rows[block, :] * sig
        return carry

    over_blocks(rows, element_two)
    sums[...] = jnp.zeros_like(sums)
    backward_half(
        1, info, grad_in, combined, phi_rows, sig_rows, normed, gain, bias, skip, glu, out_own, out_oth, masks,
        whole, rows_ref, tiles_ref, ids, gate_low, combined_grad, combined_low, grad_own, grad_oth,
        (next_ends_own, next_ends_oth), payload, sums, wide,
    )
    gradient_pack(act_low, gate_low, combined_low, low_own, low_oth, mine, theirs, wide)


def adjoint_states(
    layer, info, gathered, ends, grads, masks, whole, rows_ref, tiles_ref, ids, states, drives, lows, decay_sums,
    adjoints, places, small,
):
    rows = grads[0].shape[0]
    lanes = make_lanes(rows_ref, tiles_ref, layer, True, rows)
    core, place = info
    running_up = core == 1
    init = second_starts(
        running_up, place, lanes, gathered, ids, ends, (whole.at[1], whole.at[0]), places, small
    )
    width = lanes.states
    zero = jnp.zeros((8, width), f32)
    for side in range(2):
        adjoints[side][...] = states[side][...].astype(f32)

    def visit(side, where, re, im, sums):
        drive_re, drive_im = drives[side][where, :width], drives[side][where, width:]
        moved_re = adjoints[side][where, :width] - drive_re
        moved_im = adjoints[side][where, width:] - drive_im
        adjoints[side][where, :width] = re
        adjoints[side][where, width:] = im
        mine = sums[side]
        mine = (
            mine[0] + (re * moved_re + im * moved_im),
            mine[1] + (im * moved_re - re * moved_im),
            mine[2] + (re * drive_re + im * drive_im),
        )
        return (mine, sums[1]) if side == 0 else (sums[0], mine)

    _, sums = sweep(
        running_up, grads, (masks[1], masks[0]), lanes, init, visit, ((zero, zero, zero), (zero, zero, zero))
    )
    decay_sums[...] = jnp.zeros_like(decay_sums)
    for side in range(2):
        for i in range(3):
            decay_sums[3 * side + i : 3 * side + i + 1, :] = jnp.sum(sums[side][i], 0, keepdims=True)
        lows[side][...] = (adjoints[side][...] * lanes.scaling(side)).astype(bf16)


def norm_backward(
    layer, low_own, low_oth, in_own, in_oth, grad, combined_grad, normed, inv_scale, gain, skip, sums, wide, finish
):
    rows, width = grad.shape
    wide[...] = dot_nt(low_own[...], in_own[layer, 0]) + dot_nt(low_oth[...], in_oth[layer, 0])
    zero = jnp.zeros((8, width), f32)

    def element(start, carry):
        block = pl.ds(start, ELEMENT_ROWS)
        mixed_grad = wide[block, :] + combined_grad[block, :] * skip[layer : layer + 1, :]
        unit = normed[block, :]
        weighted = mixed_grad * unit
        inner = mixed_grad * gain[layer : layer + 1, :]
        mean_one = jnp.sum(inner, 1, keepdims=True) * (1.0 / width)
        mean_two = jnp.sum(weighted * gain[layer : layer + 1, :], 1, keepdims=True) * (1.0 / width)
        spread = jnp.concatenate([inv_scale[block, :]] * (width // LANES), 1)
        finish(start, grad[block, :] + spread * (inner - mean_one - unit * mean_two))
        return carry[0] + fold(weighted), carry[1] + fold(mixed_grad)

    gain_sum, bias_sum = over_blocks(rows, element, (zero, zero))
    sums[2:3, :] = jnp.sum(gain_sum, 0, keepdims=True)
    sums[3:4, :] = jnp.sum(bias_sum, 0, keepdims=True)


def back_kernel(
    row_devices,
    in_low_own,
    in_low_oth,
    keep_own,
    keep_oth,
    whole,
    rows_ref,
    tiles_ref,
    ids,
    in_own,
    in_oth,
    out_own,
    out_oth,
    grad_in,
    combined_grad_in,
    normed_in,
    inv_in,
    gain,
    bias,
    skip,
    glu,
    combined,
    phi,
    sig,
    normed,
    act_low,
    low_own,
    low_oth,
    grad_out,
    combined_grad,
    next_own,
    next_oth,
    next_ends_own,
    next_ends_oth,
    payload,
    sums,
    mine,
    theirs,
    wide,
    gate_low,
    combined_low,
):
    info = core_place(row_devices)
    masks = (keep_own, keep_oth)
    sums[...] = jnp.zeros_like(sums)

    def finish(start, value):
        grad_out[pl.ds(start, ELEMENT_ROWS), :] = value

    norm_backward(
        1, in_low_own, in_low_oth, in_own, in_oth, grad_in, combined_grad_in, normed_in, inv_in, gain, skip, sums, wide,
        finish,
    )
    backward_half(
        0, info, grad_out, combined, phi, sig, normed, gain, bias, skip, glu, out_own, out_oth, masks, whole,
        rows_ref, tiles_ref, ids, gate_low, combined_grad, combined_low, next_own, next_oth,
        (next_ends_own, next_ends_oth), payload, sums, wide,
    )
    gradient_pack(act_low, gate_low, combined_low, low_own, low_oth, mine, theirs, wide)


def scan_kernel(
    layer,
    row_devices,
    gathered,
    ends_own,
    ends_oth,
    grad_own,
    grad_oth,
    keep_own,
    keep_oth,
    whole,
    rows_ref,
    tiles_ref,
    ids,
    states_own,
    states_oth,
    drive_own,
    drive_oth,
    mixed_low,
    low_own,
    low_oth,
    decay_sums,
    mine,
    theirs,
    places,
    small,
    adjoint_own,
    adjoint_oth,
):
    info = core_place(row_devices)
    masks = (keep_own, keep_oth)
    adjoint_states(
        layer, info, gathered, (ends_own, ends_oth), (grad_own, grad_oth), masks, whole, rows_ref, tiles_ref, ids,
        (states_own, states_oth), (drive_own, drive_oth), (low_own, low_oth), decay_sums,
        (adjoint_own, adjoint_oth), places, small,
    )
    store_columns(mine, 0, dot_tn(mixed_low[...], low_own[...]))
    store_columns(theirs, 0, dot_tn(mixed_low[...], low_oth[...]))


def final_kernel(
    low_own, low_oth, in_own, in_oth, grad_in, combined_grad, normed, inv_scale, gain, skip, out, sums, wide
):
    sums[...] = jnp.zeros_like(sums)

    def finish(start, value):
        out[pl.ds(start, ELEMENT_ROWS), :] = value

    norm_backward(
        0, low_own, low_oth, in_own, in_oth, grad_in, combined_grad, normed, inv_scale, gain, skip, sums, wide, finish
    )


def token_order_kernel(block_out, tokens_grad, halves, *columns):
    rows = block_out.shape[0]
    for source, part, out in ((block_out, columns[0], halves.at[0]), (tokens_grad, columns[1], halves.at[1])):
        store_token_order(part, 0, source[...], rows // 8)
        join_columns(out, part)


def store_columns(out, first, values):
    rows, width = values.shape
    for i in range(width // LANES):
        out[first + i * rows : first + (i + 1) * rows, :] = values[:, i * LANES : (i + 1) * LANES].astype(out.dtype)


def half_rows(core, act_low, gate_low, mine, theirs, first, wide):
    wide[...] = dot_tn(act_low[...], gate_low[...])
    half = wide.shape[0] // 2
    width = wide.shape[1]
    for out, which in ((mine, core), (theirs, 1 - core)):
        rows = pl.ds(pl.multiple_of(which * half, half), half)
        for i in range(width // LANES):
            out[first + i * half : first + (i + 1) * half, :] = wide[rows, i * LANES : (i + 1) * LANES].astype(out.dtype)


def gradient_pack(act_low, gate_low, combined_low, low_own, low_oth, mine, theirs, wide):
    store_columns(theirs, 0, dot_tn(low_oth[...], combined_low[...]))
    store_columns(mine, 0, dot_tn(low_own[...], combined_low[...]))
    size = low_own.shape[1] * (combined_low.shape[1] // LANES)
    half_rows(lax.axis_index("dir"), act_low, gate_low, mine, theirs, size, wide)


def slot(low_bit, parts):
    return jnp.bitwise_and(jnp.right_shift(lax.axis_index("seq"), low_bit), parts - 1)


def paired(values):
    while len(values) > 1:
        values = [a + b for a, b in zip(values[::2], values[1::2])]
    return values[0]


def part_rows(index, rows):
    return pl.ds(pl.multiple_of(index * rows, rows), rows)


def sum_parts(groups, outs, low_bit):
    parts = len(outs)
    mine = slot(low_bit, parts)
    for k, out in enumerate(outs):
        first = 0
        for rows, sources in groups:
            share = rows // parts
            where = part_rows(jnp.bitwise_xor(mine, k), share)
            total = paired([source[where, :].astype(f32) for source in sources])
            out[first : first + share, :] = total.astype(out.dtype)
            first += share


def gather_parts(sizes, sources, low_bit, outs):
    mine = slot(low_bit, len(sources))
    for k, source in enumerate(sources):
        first = 0
        for rows, out in zip(sizes, outs):
            out[part_rows(jnp.bitwise_xor(mine, k), rows), :] = source[first : first + rows, :]
            first += rows


def relay_kernel(payload_in, payload):
    payload[...] = payload_in[...]


def add_rows(out, at, sources, start, rows):
    where = pl.ds(pl.multiple_of(start, rows), rows)
    out[at : at + rows, :] = paired([source[where, :].astype(f32) for source in sources]).astype(out.dtype)


def put_small(outs, first, value):
    for out in outs:
        out[first : first + value.shape[0], :] = value.astype(out.dtype)


def half_groups(outer, inner, side):
    return ((outer // 2, side * (outer // 2)), (inner // 2, side * (inner // 2)))


def cores_kernel(outer_half, half, outer, got_outer, inner, got_inner, *refs):
    small_sums, (a_keep, a_send, b_keep, b_send), small = refs[:-5], refs[-5:-1], refs[-1]
    outer_rows, inner_rows = 2 * outer_half, 2 * (half - outer_half)
    mine = slot(0, 4)
    for side, out, parts in ((0, a_keep, (0, 2)), (0, a_send, (1, 3)), (1, b_keep, (0, 1)), (1, b_send, (2, 3))):
        (rows_one, at_one), (rows_two, at_two) = half_groups(outer_rows, inner_rows, side)
        for place, k in enumerate(parts):
            which = jnp.bitwise_xor(mine, k)
            add_rows(out, place * half, [outer, got_outer], which * outer_rows + at_one, rows_one)
            add_rows(out, place * half + rows_one, [inner, got_inner], which * inner_rows + at_two, rows_two)
    if small_sums:
        small_pack(*small_sums, small)
        put_small((a_keep, a_send), 2 * half, small[...])


def half_kernel(half, a_own, a_got, b_own, b_got, a_keep, a_send, b_keep, b_send):
    for own, got, outs in ((a_own, a_got, (a_keep, a_send)), (b_own, b_got, (b_keep, b_send))):
        for i, out in enumerate(outs):
            add_rows(out, 0, [own, got], i * half, half)
    if a_own.shape[0] > 2 * half:
        put_small((a_keep, a_send), half, a_own[2 * half :, :].astype(f32) + a_got[2 * half :, :].astype(f32))


def plane_kernel(half, outer_half, a_own, a_got, b_own, b_got, *outs):
    groups = []
    for own, got in ((a_own, a_got), (b_own, b_got)):
        groups.append((outer_half, [own.at[0:outer_half], got.at[0:outer_half]]))
        groups.append((half - outer_half, [own.at[outer_half:half], got.at[outer_half:half]]))
    sum_parts(groups, outs, 2)
    if a_own.shape[0] > half:
        put_small(outs, half // 2, a_own[half:, :].astype(f32) + a_got[half:, :].astype(f32))


def planes_kernel(*refs):
    refs[-1][...] = paired([source[...].astype(f32) for source in refs[:-1]]).astype(bf16)


def second_planes_kernel(*refs):
    sources, out, small = refs[:-2], refs[-2], refs[-1]
    rows = out.shape[0]
    out[...] = paired([source[0:rows, :].astype(f32) for source in sources]).astype(bf16)
    small[...] = paired([source[rows:, :].astype(f32) for source in sources])


def gather_kernel(outer_half, *refs):
    sources, outs = refs[:4], refs[4:]
    half = outs[0].shape[0]
    sizes, places = [], []
    for out in outs:
        sizes += [outer_half // 4, (half - outer_half) // 4]
        places += [out.at[0:outer_half], out.at[outer_half:half]]
    gather_parts(sizes, sources, 2, places)


def pair_kernel(a_own, a_got, b_own, b_got, a_out, b_out):
    half = a_own.shape[0]
    for own, got, out in ((a_own, a_got, a_out), (b_own, b_got, b_out)):
        out[0:half, :] = own[...]
        out[half : 2 * half, :] = got[...]


def last_pair_kernel(a_own, a_got, b_own, b_got, through, through_out, a_out, b_out):
    pair_kernel(a_own, a_got, b_own, b_got, a_out, b_out)


def assemble(outer_half, a_own, a_got, b_own, b_got, outer, inner):
    half = a_own.shape[0] // 2
    mine = slot(0, 4)
    for side, sources in ((0, (a_own, a_got, a_own, a_got)), (1, (b_own, b_own, b_got, b_got))):
        second = (0, 0, 1, 1) if side == 0 else (0, 1, 0, 1)
        for k, source in enumerate(sources):
            which = jnp.bitwise_xor(mine, k)
            first = second[k] * half
            rows = outer_half
            outer[part_rows(2 * which + side, rows), :] = source[first : first + rows, :]
            if inner is not None:
                rows = half - outer_half
                inner[part_rows(2 * which + side, rows), :] = source[first + outer_half : first + half, :]


def join_kernel(mine, theirs, *outs):
    core = lax.axis_index("dir")
    rows = mine.shape[1]
    for i, out in enumerate(outs):
        out[part_rows(core, rows), :] = mine[i]
        out[part_rows(1 - core, rows), :] = theirs[i]


def matrix_columns(source, first, out):
    rows, width = out.shape
    for i in range(width // LANES):
        out[:, i * LANES : (i + 1) * LANES] = source[first + i * rows : first + (i + 1) * rows, :].astype(f32)


def gate_part_kernel(outer_half, first, *refs):
    sources, out, whole = refs[:-2], refs[-2], refs[-1]
    assemble(outer_half, *sources, whole, None)
    out[...] = whole[first : first + out.shape[0], :]


def unpack_kernel(layer, olds, outer_half, *refs):
    refs = list(refs)
    take = lambda n: [refs.pop(0) for _ in range(n)]
    sources = take(4)
    take(olds)
    outs = take(2)
    buffers = take(2)
    whole = take(2)
    (sems,) = refs
    assemble(outer_half, *sources, *whole)
    copies = []
    for i in range(2):
        matrix_columns(whole[i], 0, buffers[i])
        copies.append(pltpu.make_async_copy(buffers[i], outs[i].at[layer, 0], sems.at[i]))
        copies[-1].start()
    for copy in copies:
        copy.wait()


def gate_kernel(layer, *refs):
    mine, theirs, (out, buffer, sems) = refs[0], refs[1], refs[-3:]
    core = lax.axis_index("dir")
    half = buffer.shape[0] // 2
    width = buffer.shape[1]
    for source, which in ((mine, core), (theirs, 1 - core)):
        rows = part_rows(which, half)
        for i in range(width // LANES):
            buffer[rows, i * LANES : (i + 1) * LANES] = source[i * half : (i + 1) * half, :].astype(f32)
    copy = pltpu.make_async_copy(buffer, out.at[layer], sems.at[0])
    copy.start()
    copy.wait()


def small_pack(sums_turn, sums_back, sums_last, decay_late, decay_early, out):
    per = sums_turn.shape[1] // LANES
    thirds = decay_late.shape[1] // LANES
    out[...] = jnp.zeros_like(out)
    kinds = (
        ((sums_last, 2), (sums_back, 2)),
        ((sums_last, 3), (sums_back, 3)),
        ((sums_back, 1), (sums_turn, 1)),
        ((sums_back, 0), (sums_turn, 0)),
    )
    at = 0
    for kind in kinds:
        for source, row in kind:
            for i in range(per):
                out[at : at + 1, :] = source[row : row + 1, i * LANES : (i + 1) * LANES]
                at += 1
    for side in range(2):
        for source in (decay_late, decay_early):
            for term in range(3):
                for i in range(thirds):
                    row = 3 * side + term
                    out[at : at + 1, :] = source[row : row + 1, i * LANES : (i + 1) * LANES]
                    at += 1


def small_out_kernel(own, got, table, gain, bias, rate, turn, skip, gate):
    layers, _, states = table.shape
    thirds = states // LANES
    width = gain.shape[1]
    per = width // LANES
    at = 0
    for out in (gain, bias, skip, gate):
        for layer in range(layers):
            for i in range(per):
                out[layer : layer + 1, i * LANES : (i + 1) * LANES] = own[at : at + 1, :] + got[at : at + 1, :]
                at += 1
    other = at + layers * 3 * thirds
    for layer in range(layers):
        for i in range(thirds):
            lanes = slice(i * LANES, (i + 1) * LANES)
            rows = [(layer * 3 + t) * thirds + i for t in range(3)]
            term_re, term_im, term_scale = (
                own[at + row : at + row + 1, :] + got[other + row : other + row + 1, :] for row in rows
            )
            re, im, scale, damping, step_size, rotation, square = (
                table[layer, t : t + 1, lanes] for t in range(7)
            )
            grad_re = (term_re * re - term_im * im) / square
            grad_im = (term_re * im + term_im * re) / square
            grad_scale = term_scale / scale
            grad_damping = grad_scale * square / scale - (grad_re * re + grad_im * im)
            grad_rotation = grad_im * re - grad_re * im
            log_rate = grad_damping * damping
            rate[layer, 0:1, lanes] = log_rate
            turn[layer, 0, 0:1, lanes] = grad_rotation * step_size
            turn[layer, 0, 1:2, lanes] = log_rate + grad_rotation * rotation


class Order:
    def __init__(self):
        self.tile = None

    def run(self, kernel, outs, operands, scratch=(), flops=0, name=None, spare=8, after=(), free_outs=0, alias=None,
            semaphores=0, cost=0, far=False, far_last=False):
        whole = pl.BlockSpec(memory_space=pltpu.VMEM)
        free = pl.BlockSpec(memory_space=pl.ANY)
        waits = list(after) + ([] if self.tile is None else [self.tile])
        inputs, results = len(operands), len(outs)
        skipped = len(waits)

        def body(*refs):
            token = refs[skipped + inputs]
            token[...] = jnp.zeros_like(token)
            kernel(*refs[skipped : skipped + inputs], *refs[skipped + inputs + 1 :])

        shapes = [jax.ShapeDtypeStruct((8, LANES), f32)]
        shapes += [jax.ShapeDtypeStruct(shape, dtype) for shape, dtype in outs]
        held = sum(jnp.dtype(dtype).itemsize * functools.reduce(lambda a, b: a * b, shape) for shape, dtype in scratch)
        specs = [free] * skipped + [pl.BlockSpec(memory_space=pltpu.HBM) if far else whole] * inputs
        if far_last:
            specs[-1] = pl.BlockSpec(memory_space=pltpu.HBM)
        aliases = {}
        if alias is not None:
            for operand, out in alias.items():
                specs[skipped + operand] = free
                aliases[skipped + operand] = out + 1
        extra = [pltpu.SemaphoreType.DMA((semaphores,))] if semaphores else []
        results = pl.pallas_call(
            body,
            out_shape=shapes,
            in_specs=specs,
            out_specs=[whole] + [free] * free_outs + [whole] * (results - free_outs),
            scratch_shapes=[pltpu.VMEM(shape, dtype) for shape, dtype in scratch] + extra,
            input_output_aliases=aliases,
            compiler_params=pltpu.CompilerParams(vmem_limit_bytes=held + spare * 2**20),
            cost_estimate=pl.CostEstimate(flops=int(1 + cost * 1e9), bytes_accessed=int(1 + cost * 3e6), transcendentals=0),
            name=name,
        )(*waits, *operands)
        self.tile = results[0]
        return results[1:]


def swap(value):
    return lax.ppermute(value, "dir", [(0, 1), (1, 0)])


def across(value, bits):
    count = lax.axis_size("seq")
    return lax.ppermute(value, "seq", [(i, i ^ bits) for i in range(count)])


def beyond(value):
    bit = 4
    while (1 << bit) < lax.axis_size("seq"):
        value = (value.astype(f32) + across(value, 1 << bit).astype(f32)).astype(value.dtype)
        bit += 1
    return value


def exchanged(payload, row_devices):
    count = lax.axis_size("seq")
    group = 2 * row_devices
    groups = None
    if count != row_devices:
        groups = [list(range(i, i + group)) for i in range(0, 2 * count, group)]
    return lax.all_to_all(payload, ("seq", "dir"), 0, 0, tiled=True, axis_index_groups=groups)


def sent(parts, low_bit):
    return [parts[0]] + [across(parts[k], k << low_bit) for k in (1, 2, 3)]


def shared(value, low_bit):
    return [value] + [across(value, k << low_bit) for k in (1, 2, 3)]


def body(
    tokens,
    segment_ids,
    norm_gain,
    norm_bias,
    input_matrix,
    output_matrix,
    rate_params,
    turn_params,
    skip_weight,
    glu_weight,
    glu_bias,
    cotangent,
):
    chip_rows, width = tokens.shape
    rows = chip_rows // 2
    layers = rate_params.shape[0]
    states = rate_params.shape[2]
    row_devices = LENGTH // chip_rows
    order = Order()
    here = functools.partial

    in_own, out_own = input_matrix, output_matrix
    in_oth = swap(input_matrix)
    rate_oth, turn_oth = swap(rate_params), swap(turn_params)
    out_oth = swap(output_matrix)
    segments = segment_ids.reshape(chip_rows // LANES, LANES)

    full = ((rows, width), f32)
    full_low = ((rows, width), bf16)
    columns = ((width // LANES, rows, LANES), f32)
    wide = ((rows, 2 * states), f32)
    wide_low = ((rows, 2 * states), bf16)
    ends = ((8, 2 * states), f32)
    payload_shape = ((2 * row_devices, 8, LANES), bf16)
    narrow = ((rows, LANES), f32)
    tile = ((8, LANES), f32)
    sums_shape = ((8, width), f32)
    decay_shape = ((8, states), f32)
    table_shape = ((layers, 16, states), f32)
    places = ((8, 2 * states), f32)
    in_size = width * (2 * states // LANES)
    out_size = 2 * states * (width // LANES)
    glu_size = width // 2 * (width // LANES)
    outer_size = out_size + glu_size
    outer_pack = ((outer_size, LANES), bf16)
    inner_pack = ((in_size, LANES), bf16)
    one = 2.0 * rows * width * 2 * states
    gate = 2.0 * rows * width * width
    scan = 1e9

    x0, normed0, inv0 = order.run(
        here(open_kernel, row_devices),
        [full, full, narrow],
        [tokens],
        [full_low, columns],
        far=True,
        semaphores=1,
        name="open_norm",
        cost=10,
    )
    table, keep_own, keep_oth, whole, ids, grad1 = order.run(
        here(open_masks_kernel, row_devices),
        [table_shape, narrow, narrow, ((2, 8, LANES), f32), tile, full],
        [segments, rate_params, turn_params, cotangent],
        [tile, columns, full],
        far_last=True,
        semaphores=1,
        name="open_masks",
    )
    mixed0, drive_own0, drive_oth0, ends_own, ends_oth, payload, table, tiles = order.run(
        here(open_second_kernel, row_devices),
        [full_low, wide, wide, ends, ends, payload_shape, table_shape, ((layers, 16, LANES), f32)],
        [normed0, norm_gain, norm_bias, table, keep_own, keep_oth, whole, ids, rate_oth, turn_oth, in_own, in_oth],
        name="open_scan",
        after=[out_oth],
    )
    gathered = exchanged(payload, row_devices)
    (
        low_own0, low_oth0, combined0, phi0, sig0, act_low0, x1, normed1, inv1, mixed1, drive_own1, drive_oth1,
        ends_own, ends_oth, payload,
    ) = order.run(
        here(mid_kernel, row_devices),
        [wide_low, wide_low, full, full, full, full_low, full, full, narrow, full_low, wide, wide, ends, ends,
         payload_shape],
        [gathered, ends_own, ends_oth, drive_own0, drive_oth0, keep_own, keep_oth, whole, table, tiles,
         ids, out_own, out_oth, x0, normed0, norm_gain, norm_bias, skip_weight, glu_weight, glu_bias, in_own, in_oth],
        [places, tile, full, wide, wide],
        flops=4 * one + gate + 3 * scan,
        name="mid",
    )
    gathered = exchanged(payload, row_devices)
    (
        low_own1, low_oth1, out1, combined_grad1, grad_own1, grad_oth1, ends_own, ends_oth, payload,
        sums_turn, mine, theirs,
    ) = order.run(
        here(turn_kernel, row_devices),
        [wide_low, wide_low, full, full, wide, wide, ends, ends, payload_shape, sums_shape, outer_pack, outer_pack],
        [gathered, ends_own, ends_oth, drive_own1, drive_oth1, keep_own, keep_oth, whole, table, tiles,
         ids, out_own, out_oth, x1, normed1, norm_gain, norm_bias, skip_weight, glu_weight, glu_bias, grad1],
        [places, tile, full, full, full, full, wide, wide, full_low, full_low, full_low],
        flops=4 * one + 2 * gate + 4 * scan,
        name="turn",
    )
    first_outer = [mine, swap(theirs)]
    gathered = exchanged(payload, row_devices)
    in_low_own1, in_low_oth1, decay_sums1, mine, theirs = order.run(
        here(scan_kernel, 1, row_devices),
        [wide_low, wide_low, decay_shape, inner_pack, inner_pack],
        [gathered, ends_own, ends_oth, grad_own1, grad_oth1, keep_own, keep_oth, whole, table, tiles,
         ids, low_own1, low_oth1, drive_own1, drive_oth1, mixed1],
        [places, tile, wide, wide],
        name="scan_one",
        after=[first_outer[1]],
    )
    first_inner = [mine, swap(theirs)]
    (
        grad0, combined_grad0, grad_own0, grad_oth0, ends_own, ends_oth, payload, sums_back, mine_outer, theirs_outer,
    ) = order.run(
        here(back_kernel, row_devices),
        [full, full, wide, wide, ends, ends, payload_shape, sums_shape, outer_pack, outer_pack],
        [in_low_own1, in_low_oth1, keep_own, keep_oth, whole, table, tiles, ids, in_own, in_oth, out_own, out_oth, grad1,
         combined_grad1, normed1, inv1, norm_gain, norm_bias, skip_weight, glu_weight, combined0, phi0, sig0, normed0,
         act_low0, low_own0, low_oth0],
        [full, full_low, full_low],
        name="back",
    )
    second_outer = [mine_outer, swap(theirs_outer)]
    outer_half = outer_size // 8
    half = outer_half + in_size // 8
    share_rows = half // 2
    small_rows = -(-(4 * layers * (width // LANES) + 6 * layers * (states // LANES)) // 16) * 16
    small_shape = ((small_rows, LANES), f32)

    def low(count):
        return ((count, LANES), bf16)

    def from_cores(packs, extra, sums, name, after=()):
        a_keep, a_send, b_keep, b_send, _ = order.run(
            here(cores_kernel, outer_half, half),
            [low(2 * half + extra)] * 2 + [low(2 * half)] * 2 + [small_shape],
            packs + sums,
            name=name,
            after=after,
            cost=CORES_COST,
        )
        return [a_keep, across(a_send, 1), b_keep, across(b_send, 2)]

    def from_first(parts, extra, name, after=()):
        a_keep, a_send, b_keep, b_send = order.run(
            here(half_kernel, half), [low(half + extra)] * 2 + [low(half)] * 2, parts, name=name, after=after
        )
        return [a_keep, across(a_send, 2), b_keep, across(b_send, 1)]

    def from_second(parts, extra, name, cost=0):
        return sent(
            order.run(
                here(plane_kernel, half, outer_half), [low(share_rows + extra)] * 4, parts, name=name, cost=cost
            ),
            2,
        )

    def gathered_half(parts, name, after=(), cost=0):
        a_half, b_half = order.run(
            here(gather_kernel, outer_half), [low(half)] * 2, parts, name=name, after=after, cost=cost
        )
        return a_half, across(a_half, 2), b_half, across(b_half, 1)

    def gathered_whole(halves, name):
        a_pair, b_pair = order.run(pair_kernel, [low(2 * half)] * 2, list(halves), name=name)
        return [a_pair, across(a_pair, 1), b_pair, across(b_pair, 2)]

    first = from_cores(first_outer + first_inner, 0, [], "first_cores")
    (payload,) = order.run(relay_kernel, [payload_shape], [payload], name="relay", cost=50)
    gathered = exchanged(payload, row_devices)
    first = from_first(first, 0, "first_half", [gathered])
    in_low_own0, in_low_oth0, decay_sums0, mine, theirs = order.run(
        here(scan_kernel, 0, row_devices),
        [wide_low, wide_low, decay_shape, inner_pack, inner_pack],
        [gathered, ends_own, ends_oth, grad_own0, grad_oth0, keep_own, keep_oth, whole, table, tiles,
         ids, low_own0, low_oth0, drive_own0, drive_oth0, mixed0],
        [places, tile, wide, wide],
        name="scan_zero",
        after=[second_outer[1]],
    )
    second_inner = [mine, swap(theirs)]
    grad_x, sums_last = order.run(
        final_kernel,
        [full, sums_shape],
        [in_low_own0, in_low_oth0, in_own, in_oth, grad0, combined_grad0, normed0, inv0, norm_gain, skip_weight],
        [full],
        name="final_norm",
    )
    first = from_second(first, 0, "first_plane", 50)
    second = from_cores(
        second_outer + second_inner, small_rows, [sums_turn, sums_back, sums_last, decay_sums0, decay_sums1],
        "second_cores",
    )
    (halves,) = order.run(
        token_order_kernel, [((2, rows, width), f32)], [out1, grad_x], [columns, columns], name="token_order"
    )
    (share,) = order.run(planes_kernel, [low(share_rows)], first, name="first_planes", cost=50)
    first = shared(beyond(share), 2)
    second = from_first(second, small_rows, "second_half")
    first = gathered_half(first, "first_gather", cost=50)
    second = from_second(second, small_rows, "second_plane")
    share, small = order.run(second_planes_kernel, [low(share_rows), small_shape], second, name="second_planes")
    second = shared(beyond(share), 2)
    first = gathered_whole(first, "first_pair")
    small = beyond(small)
    got_small = swap(small)
    in_shape, out_shape = input_matrix.shape, output_matrix.shape

    def gate_part(quarters, name):
        (value,) = order.run(
            here(gate_part_kernel, outer_half, out_size), [low(glu_size)], quarters, [outer_pack], name=name
        )
        return value

    def gate_out(layer, mine, theirs, old, name):
        return order.run(
            here(gate_kernel, layer), [(glu_weight.shape, f32)], [mine, theirs] + old, [((width, width), f32)],
            name=name, free_outs=1, alias={2: 0} if old else None, semaphores=1,
        )

    def unpack(quarters, layer, old, name):
        return order.run(
            here(unpack_kernel, layer, len(old), outer_half),
            [(out_shape, f32), (in_shape, f32)],
            quarters + old,
            [(out_shape[2:], f32), (in_shape[2:], f32), outer_pack, inner_pack],
            name=name,
            free_outs=2,
            alias={4 + i: i for i in range(len(old))},
            semaphores=2,
        )

    second = gathered_half(second, "second_gather", cost=50)
    halves, a_pair, b_pair = order.run(
        last_pair_kernel, [((2, rows, width), f32), low(2 * half), low(2 * half)], list(second) + [halves],
        name="second_pair", free_outs=1, alias={4: 0}, after=[first[1], first[3]],
    )
    second = [a_pair, across(a_pair, 1), b_pair, across(b_pair, 2)]
    gate_one = gate_part(first, "gate_one")
    got_one = swap(gate_one)
    results = unpack(first, 1, [], "unpack_one")
    gain_grad, bias_grad, rate_grad, turn_grad, skip_grad, gate_grad = order.run(
        small_out_kernel,
        [((layers, width), f32), ((layers, width), f32), (rate_params.shape, f32), (turn_params.shape, f32),
         ((layers, width), f32), ((layers, width), f32)],
        [small, got_small, table],
        name="small_out",
    )
    whole_rows = ((chip_rows, width), f32)
    block_output, tokens_grad = order.run(
        join_kernel, [whole_rows, whole_rows], [halves, swap(halves)], name="join"
    )
    glu_all = gate_out(1, gate_one, got_one, [], "gate_out_one")
    gate_zero = gate_part(second, "gate_zero")
    got_zero = swap(gate_zero)
    out_all, in_all = unpack(second, 0, list(results), "unpack_zero")
    (glu_all,) = gate_out(0, gate_zero, got_zero, list(glu_all), "gate_out_zero")
    return (
        block_output,
        tokens_grad,
        gain_grad,
        bias_grad,
        in_all,
        out_all,
        rate_grad,
        turn_grad,
        skip_grad,
        glu_all,
        gate_grad,
    )


def solution(mesh):
    return jax.shard_map(
        body,
        mesh=mesh,
        in_specs=(
            P("seq", None),
            P("seq"),
            P(),
            P(),
            P(None, "dir", None, None),
            P(None, "dir", None, None),
            P(None, "dir", None),
            P(None, "dir", None, None),
            P(),
            P(),
            P(),
            P("seq", None),
        ),
        out_specs=(
            P("seq", None),
            P("seq", None),
            P(),
            P(),
            P(None, "dir", None, None),
            P(None, "dir", None, None),
            P(None, "dir", None),
            P(None, "dir", None, None),
            P(),
            P(),
            P(),
        ),
        check_vma=False,
    )
```

```python
import functools

import jax
import jax.numpy as jnp
from jax import lax
from jax.experimental import pallas as pl
from jax.experimental.pallas import tpu as pltpu
from jax.sharding import PartitionSpec as P

LENGTH = 16384
LONGEST_RUN = 8192

eps = 1e-05
inv_root_two = 0.7071067811865476
inv_root_two_pi = 0.3989422804014327

f32 = jnp.float32
bf16 = jnp.bfloat16


LANES = 128
ELEMENT_ROWS = 512
UNROLL = 16
CORES_COST = 0


def core_place(row_devices):
    core = lax.axis_index("dir")
    return core, lax.rem(lax.axis_index("seq"), row_devices) * 2 + core


def dot(a, b):
    return jnp.dot(a, b, preferred_element_type=f32)


def dot_nt(a, b):
    return lax.dot_general(a, b, (((1,), (1,)), ((), ())), preferred_element_type=f32)


def dot_tn(a, b):
    return lax.dot_general(a, b, (((0,), (0,)), ((), ())), preferred_element_type=f32)


def squared(re, im, times):
    for _ in range(times):
        re, im = re * re - im * im, 2.0 * re * im
    return re, im


def over_blocks(rows, step, init=()):
    def one(i, carry):
        return step(pl.multiple_of(i * ELEMENT_ROWS, ELEMENT_ROWS), carry)

    return lax.fori_loop(0, rows // ELEMENT_ROWS, one, init)


def fold(values):
    total = values[0:8]
    for start in range(8, values.shape[0], 8):
        total = total + values[start : start + 8]
    return total


class Lanes:
    def __init__(self, rows_ref, tiles_ref, layer, adjoint, spans, rows):
        states = rows_ref.shape[2]
        self.states = states
        self.rows_ref, self.layer = rows_ref, layer
        flip = -1.0 if adjoint else 1.0
        self.step = []
        self.run = []
        self.block = []
        for side in range(2):
            row = 8 * side
            re = rows_ref[layer, row : row + 1, :]
            im = rows_ref[layer, row + 1 : row + 2, :] * flip
            self.step.append((jnp.broadcast_to(re, (8, states)), jnp.broadcast_to(im, (8, states))))
            self.run.append(squared(re, im, (spans - 1).bit_length()))
            thirds = states // LANES
            tile_re = tiles_ref[layer, 8 * side : 8 * side + thirds, :]
            tile_im = tiles_ref[layer, 8 * side + thirds : 8 * side + 2 * thirds, :] * flip
            self.block.append(squared(tile_re, tile_im, (rows - 1).bit_length()))

    def scaling(self, side):
        row = self.rows_ref[self.layer, 8 * side + 2 : 8 * side + 3, :]
        return jnp.concatenate([row, row], 1)


def sweep(first_forward, drives, masks, lanes, init, visit=None, totals=()):
    states = lanes.states
    span = drives[0].shape[0] // 8

    def one_side(side, i, values, sums):
        upward = first_forward if side == 0 else jnp.logical_not(first_forward)
        rows = pl.ds(pl.multiple_of(jnp.where(upward, i, span - 1 - i) * 8, 8), 8)
        keep = masks[side][rows, :]
        keep = jnp.concatenate([keep] * (states // LANES), 1)
        step_re, step_im = lanes.step[side]
        step_re, step_im = step_re * keep, step_im * keep
        re, im = values
        drive_re = drives[side][rows, :states]
        drive_im = drives[side][rows, states:]
        re, im = (
            step_re * re - step_im * im + drive_re,
            step_re * im + step_im * re + drive_im,
        )
        if visit is not None:
            sums = visit(side, rows, re, im, sums)
        return (re, im), sums

    if totals:
        values, sums = [], []
        for side in range(2):

            def step(i, carry, side=side):
                return one_side(side, i, *carry)

            value, total = lax.fori_loop(0, span, step, (init[side], totals[side]), unroll=UNROLL)
            values.append(value)
            sums.append(total)
        return tuple(values), tuple(sums)

    def step(i, values):
        return tuple(one_side(side, i, values[side], ())[0] for side in range(2))

    return lax.fori_loop(0, span, step, init, unroll=span), ()


def run_chain(first_up, lanes, side, ends, whole, start, places):
    states = lanes.states
    power_re, power_im = lanes.run[side]
    re, im = start
    for i in range(8):
        s = jnp.where(first_up, i, 7 - i)
        row = pl.ds(s, 1)
        if places is not None:
            places[row, :states] = re
            places[row, states:] = im
        passes = whole[row, :]
        passes = jnp.concatenate([passes] * (states // LANES), 1)
        pass_re, pass_im = power_re * passes, power_im * passes
        end_re, end_im = ends[row, :states], ends[row, states:]
        re, im = (end_re + pass_re * re - pass_im * im, end_im + pass_re * im + pass_im * re)
    return re, im


def first_pass(running_up, place, drives, masks, wholes, lanes, ids_ref, ends, payload):
    states = lanes.states
    thirds = states // LANES
    nothing = jnp.zeros((8, states), f32)
    zero = (nothing, nothing)
    values, _ = sweep(running_up, drives, masks, lanes, (zero, zero))
    tiles = []
    for side in range(2):
        ends[side][:, :states] = values[side][0]
        ends[side][:, states:] = values[side][1]
        upward = running_up if side == 0 else jnp.logical_not(running_up)
        start = jnp.zeros((1, states), f32)
        re, im = run_chain(upward, lanes, side, ends[side], wholes[side], (start, start), None)
        rows = [part[:, LANES * i : LANES * (i + 1)] for part in (re, im) for i in range(thirds)]
        tiles.append(jnp.concatenate(rows + [ids_ref[0:2, :]], 0))
    for i in range(payload.shape[0]):
        to_later = jnp.logical_xor(running_up, i < place)
        payload[i] = jnp.where(to_later, tiles[0], tiles[1]).astype(payload.dtype)


def entering(upward, place, lanes, side, gathered, ids_ref, small):
    states = lanes.states
    thirds = states // LANES
    count = gathered.shape[0]
    rows = lanes.token_rows
    block_re, block_im = lanes.block[side]
    re = jnp.zeros((thirds, LANES), f32)
    im = jnp.zeros((thirds, LANES), f32)
    key = jnp.where(upward, ids_ref[0:1, :], ids_ref[1:2, :])
    for distance in range(min(count - 1, LONGEST_RUN // rows), 0, -1):
        source = jnp.where(upward, place - distance, place + distance)
        inside = jnp.logical_and(source >= 0, source < count)
        source = jnp.clip(source, 0, count - 1)
        sent = gathered[source].astype(f32)
        sent_re, sent_im = sent[0:thirds], sent[thirds : 2 * thirds]
        sent_key = jnp.where(upward, sent[7:8], sent[6:7])
        joined = jnp.where(jnp.logical_and(sent_key == key, inside), 1.0, 0.0)
        re, im = (
            joined * sent_re + block_re * re - block_im * im,
            joined * sent_im + block_re * im + block_im * re,
        )
    small[0:thirds, :] = re
    small[thirds : 2 * thirds, :] = im
    wide_re = jnp.concatenate([small[i : i + 1, :] for i in range(thirds)], 1)
    wide_im = jnp.concatenate([small[thirds + i : thirds + i + 1, :] for i in range(thirds)], 1)
    return wide_re, wide_im


def second_starts(running_up, place, lanes, gathered, ids_ref, ends, wholes, places, small):
    init = []
    states = lanes.states
    for side in range(2):
        upward = running_up if side == 0 else jnp.logical_not(running_up)
        start = entering(upward, place, lanes, side, gathered, ids_ref, small)
        run_chain(upward, lanes, side, ends[side], wholes[side], start, places)
        init.append((places[:, :states], places[:, states:]))
    return tuple(init)


def make_lanes(rows_ref, tiles_ref, layer, adjoint, token_rows):
    lanes = Lanes(rows_ref, tiles_ref, layer, adjoint, token_rows // 8, token_rows)
    lanes.token_rows = token_rows
    return lanes


def standardise(x):
    width = x.shape[1]
    average = jnp.sum(x, 1, keepdims=True) * (1.0 / width)
    centred = x - average
    inv_scale = lax.rsqrt(jnp.sum(centred * centred, 1, keepdims=True) * (1.0 / width) + eps)
    return centred * inv_scale, inv_scale


def fill_columns(columns, values):
    for i in range(columns.shape[0]):
        columns[i] = values[:, i * LANES : (i + 1) * LANES].astype(columns.dtype)


def tile_order(columns, first, count, span):
    tiles = [
        jnp.concatenate([columns[i, pl.ds(first + j, 8, stride=span), :] for i in range(columns.shape[0])], 1)
        for j in range(count)
    ]
    return jnp.concatenate(tiles, 0)


def store_token_order(columns, first, values, span):
    for j in range(values.shape[0] // 8):
        for i in range(columns.shape[0]):
            columns[i, pl.ds(first + j, 8, stride=span), :] = values[8 * j : 8 * j + 8, i * LANES : (i + 1) * LANES]


def join_columns(out, columns):
    for i in range(columns.shape[0]):
        out[:, i * LANES : (i + 1) * LANES] = columns[i]


def one_minus_exp(x):
    series = jnp.ones_like(x)
    for term in range(12, 1, -1):
        series = 1.0 - x * (1.0 / term) * series
    return jnp.where(x < 0.5, x * series, 1.0 - jnp.exp(-x))


def table_rows(table, layer, base, rate, turn):
    frequency = turn[layer, 0, 0:1, :]
    log_step = turn[layer, 0, 1:2, :]
    step_size = jnp.exp(log_step)
    damping = jnp.exp(rate[layer, 0:1, :] + log_step)
    magnitude = jnp.exp(-damping)
    rotation = frequency * step_size
    square = magnitude * magnitude
    rows = (
        magnitude * jnp.cos(rotation), magnitude * jnp.sin(rotation), jnp.sqrt(one_minus_exp(2.0 * damping)), damping,
        step_size, rotation, square,
    )
    for i, row in enumerate(rows):
        table[layer, base + i : base + i + 1, :] = row


def open_kernel(row_devices, tokens_from, x_out, normed_out, inv_out, tokens, natural, sems):
    copy = pltpu.make_async_copy(
        tokens_from.at[part_rows(lax.axis_index("dir"), tokens.shape[0])], tokens, sems.at[0]
    )
    copy.start()
    copy.wait()
    rows = x_out.shape[0]
    span = rows // 8
    fill_columns(natural, tokens[...].astype(f32))

    def element(start, carry):
        x = tile_order(natural, start // 8, ELEMENT_ROWS // 8, span)
        normed, inv_scale = standardise(x)
        block = pl.ds(start, ELEMENT_ROWS)
        x_out[block, :] = x
        normed_out[block, :] = normed
        inv_out[block, :] = jnp.broadcast_to(inv_scale, (ELEMENT_ROWS, LANES))
        return carry

    over_blocks(rows, element)


def open_masks_kernel(
    row_devices, segments, rate, turn, cotangent_from, table, keep_own, keep_oth, whole_out, ids, grad_out, rows8, natural,
    part, sems,
):
    core, _ = core_place(row_devices)
    rows = grad_out.shape[0]
    span = rows // 8
    copy = pltpu.make_async_copy(cotangent_from.at[part_rows(core, rows)], part, sems.at[0])
    copy.start()
    table[...] = jnp.zeros_like(table)
    for layer in range(table.shape[0]):
        table_rows(table, layer, 0, rate, turn)
    number = segments[...].astype(f32)
    count = number.shape[0]
    lane = lax.broadcasted_iota(jnp.int32, number.shape, 1)
    row = lax.broadcasted_iota(jnp.int32, number.shape, 0)
    back = pltpu.roll(number, 1, 1)
    back = jnp.where(lane == 0, pltpu.roll(back, 1, 0), back)
    ahead = pltpu.roll(number, LANES - 1, 1)
    ahead = jnp.where(lane == LANES - 1, pltpu.roll(ahead, count - 1, 0), ahead)
    edge_first = jnp.logical_and(lane == 0, row == 0)
    edge_last = jnp.logical_and(lane == LANES - 1, row == count - 1)
    up_keep = jnp.where(jnp.logical_or(number == back, edge_first), 1.0, 0.0)
    down_keep = jnp.where(jnp.logical_or(number == ahead, edge_last), 1.0, 0.0)
    per = LANES // span
    used = 8 // per
    for side, out in ((0, keep_own), (1, keep_oth)):
        rows8[0:count, :] = jnp.where(core == side, up_keep, down_keep)
        half = rows8[pl.ds(core * used, used), :]
        runs = jnp.concatenate([half[s // per : s // per + 1] for s in range(8)], 0)
        place = lax.broadcasted_iota(jnp.int32, (8, LANES), 1)
        sub = lax.broadcasted_iota(jnp.int32, (8, LANES), 0)
        first = lax.rem(sub, per) * span
        inside = jnp.logical_and(place >= first, place < first + span)
        least = jnp.min(jnp.where(inside, runs, 1.0), 1, keepdims=True)
        whole_out[side] = jnp.broadcast_to(least, (8, LANES))
        step = lax.broadcasted_iota(jnp.int32, (span, 8, LANES), 0)
        spread = jnp.where(step == (place - first)[None], runs[None], 0.0)
        spread = spread.reshape(span * 8, LANES).astype(bf16)
        out[...] = dot(spread, jnp.ones((LANES, LANES), bf16))
    rows8[0:count, :] = number
    first_row = rows8[pl.ds(core * used, 1), :]
    last_row = rows8[pl.ds(core * used + used - 1, 1), :]
    ids[...] = jnp.zeros_like(ids)
    ids[0:1, :] = jnp.broadcast_to(first_row[:, 0:1], (1, LANES))
    ids[1:2, :] = jnp.broadcast_to(last_row[:, LANES - 1 : LANES], (1, LANES))
    copy.wait()
    fill_columns(natural, part[...])
    grad_out[...] = tile_order(natural, 0, span, span)


def open_second_kernel(
    row_devices,
    normed,
    gain,
    bias,
    table_in,
    keep_own,
    keep_oth,
    whole,
    ids,
    rate_oth,
    turn_oth,
    in_own,
    in_oth,
    mixed_low,
    drive_own,
    drive_oth,
    ends_own,
    ends_oth,
    payload,
    table,
    tiles,
):
    core, place = core_place(row_devices)
    rows = normed.shape[0]
    span = rows // 8

    def element(start, carry):
        block = pl.ds(start, ELEMENT_ROWS)
        mixed_low[block, :] = (normed[block, :] * gain[0:1, :] + bias[0:1, :]).astype(bf16)
        return carry

    over_blocks(rows, element)
    table[...] = table_in[...]
    tiles[...] = jnp.zeros_like(tiles)
    thirds = table.shape[2] // LANES
    for layer in range(table.shape[0]):
        table_rows(table, layer, 8, rate_oth, turn_oth)
        for side in range(2):
            for part in range(2):
                for i in range(thirds):
                    at = 8 * side + part * thirds + i
                    tiles[layer, at : at + 1, :] = table[
                        layer, 8 * side + part : 8 * side + part + 1, i * LANES : (i + 1) * LANES
                    ]

    for side, (matrix, drive) in enumerate(((in_own, drive_own), (in_oth, drive_oth))):
        scale = table[0, 8 * side + 2 : 8 * side + 3, :]
        drive[...] = dot(mixed_low[...], matrix[0, 0]) * jnp.concatenate([scale, scale], 1)
    lanes = make_lanes(table, tiles, 0, False, rows)
    first_pass(
        core == 0,
        core_place(row_devices)[1],
        (drive_own, drive_oth),
        (keep_own, keep_oth),
        (whole.at[0], whole.at[1]),
        lanes,
        ids,
        (ends_own, ends_oth),
        payload,
    )


def forward_states(layer, info, gathered, ends, drives, masks, whole, rows_ref, tiles_ref, ids, states, lows, places, small):
    rows = drives[0].shape[0]
    lanes = make_lanes(rows_ref, tiles_ref, layer, False, rows)
    core, place = info
    running_up = core == 0
    init = second_starts(
        running_up, place, lanes, gathered, ids, ends, (whole.at[0], whole.at[1]), places, small
    )
    width = lanes.states

    def visit(side, where, re, im, sums):
        states[side][where, :width] = re
        states[side][where, width:] = im
        return sums

    sweep(running_up, drives, masks, lanes, init, visit)
    for side in range(2):
        lows[side][...] = states[side][...].astype(bf16)


def mid_kernel(
    row_devices,
    gathered,
    ends_own,
    ends_oth,
    drive_own,
    drive_oth,
    keep_own,
    keep_oth,
    whole,
    rows_ref,
    tiles_ref,
    ids,
    out_own,
    out_oth,
    x_in,
    normed,
    gain,
    bias,
    skip,
    glu,
    glu_bias,
    in_own,
    in_oth,
    low_own,
    low_oth,
    combined_out,
    phi_out,
    sig_out,
    act_low,
    x_out,
    normed_out,
    inv_out,
    mixed_out,
    next_own,
    next_oth,
    next_ends_own,
    next_ends_oth,
    payload,
    places,
    small,
    wide,
    states_own,
    states_oth,
):
    info = core_place(row_devices)
    rows = x_in.shape[0]
    masks = (keep_own, keep_oth)
    forward_states(
        0, info, gathered, (ends_own, ends_oth), (drive_own, drive_oth), masks, whole, rows_ref, tiles_ref,
        ids, (states_own, states_oth), (low_own, low_oth), places, small,
    )
    wide[...] = dot(low_own[...], out_own[0, 0]) + dot(low_oth[...], out_oth[0, 0])

    def element(start, carry):
        block = pl.ds(start, ELEMENT_ROWS)
        mixed = normed[block, :] * gain[0:1, :] + bias[0:1, :]
        combined = wide[block, :] + skip[0:1, :] * mixed
        phi = 0.5 * (1.0 + lax.erf(combined * inv_root_two))
        combined_out[block, :] = combined
        phi_out[block, :] = phi
        act_low[block, :] = (combined * phi).astype(bf16)
        return carry

    over_blocks(rows, element)
    wide[...] = dot(act_low[...], glu[0])

    def element_two(start, carry):
        block = pl.ds(start, ELEMENT_ROWS)
        sig = jax.nn.sigmoid(wide[block, :] + glu_bias[0:1, :])
        sig_out[block, :] = sig
        x = x_in[block, :] + combined_out[block, :] * phi_out[block, :] * sig
        x_out[block, :] = x
        after, inv_scale = standardise(x)
        normed_out[block, :] = after
        inv_out[block, :] = jnp.broadcast_to(inv_scale, (ELEMENT_ROWS, LANES))
        mixed_out[block, :] = (after * gain[1:2, :] + bias[1:2, :]).astype(bf16)
        return carry

    over_blocks(rows, element_two)
    for side, (matrix, out) in enumerate(((in_own, next_own), (in_oth, next_oth))):
        scale = rows_ref[1, 8 * side + 2 : 8 * side + 3, :]
        out[...] = dot(mixed_out[...], matrix[1, 0]) * jnp.concatenate([scale, scale], 1)
    lanes = make_lanes(rows_ref, tiles_ref, 1, False, rows)
    first_pass(
        info[0] == 0,
        info[1],
        (next_own, next_oth),
        masks,
        (whole.at[0], whole.at[1]),
        lanes,
        ids,
        (next_ends_own, next_ends_oth),
        payload,
    )


def backward_half(
    layer, info, grad, combined, phi, sig, normed, gain, bias, skip, glu, out_own, out_oth, masks, whole,
    rows_ref, tiles_ref, ids, gate_low, combined_grad, combined_low, grad_own, grad_oth, ends, payload, sums, wide,
):
    rows = grad.shape[0]
    width = grad.shape[1]
    zero = jnp.zeros((8, width), f32)

    def element(start, carry):
        block = pl.ds(start, ELEMENT_ROWS)
        gate = sig[block, :]
        gate_grad = grad[block, :] * (combined[block, :] * phi[block, :]) * gate * (1.0 - gate)
        gate_low[block, :] = gate_grad.astype(bf16)
        return carry + fold(gate_grad)

    bias_sum = over_blocks(rows, element, zero)
    wide[...] = dot_nt(gate_low[...], glu[layer])

    def element_two(start, carry):
        block = pl.ds(start, ELEMENT_ROWS)
        value = combined[block, :]
        activation_grad = grad[block, :] * sig[block, :] + wide[block, :]
        slope = phi[block, :] + value * (jnp.exp(-0.5 * value * value) * inv_root_two_pi)
        result = activation_grad * slope
        combined_grad[block, :] = result
        combined_low[block, :] = result.astype(bf16)
        mixed = normed[block, :] * gain[layer : layer + 1, :] + bias[layer : layer + 1, :]
        return carry + fold(result * mixed)

    skip_sum = over_blocks(rows, element_two, zero)
    sums[0:1, :] = jnp.sum(bias_sum, 0, keepdims=True)
    sums[1:2, :] = jnp.sum(skip_sum, 0, keepdims=True)
    grad_own[...] = dot_nt(combined_low[...], out_own[layer, 0])
    grad_oth[...] = dot_nt(combined_low[...], out_oth[layer, 0])
    lanes = make_lanes(rows_ref, tiles_ref, layer, True, rows)
    first_pass(
        info[0] == 1,
        info[1],
        (grad_own, grad_oth),
        (masks[1], masks[0]),
        (whole.at[1], whole.at[0]),
        lanes,
        ids,
        ends,
        payload,
    )


def turn_kernel(
    row_devices,
    gathered,
    ends_own,
    ends_oth,
    drive_own,
    drive_oth,
    keep_own,
    keep_oth,
    whole,
    rows_ref,
    tiles_ref,
    ids,
    out_own,
    out_oth,
    x_in,
    normed,
    gain,
    bias,
    skip,
    glu,
    glu_bias,
    grad_in,
    low_own,
    low_oth,
    block_out,
    combined_grad,
    grad_own,
    grad_oth,
    next_ends_own,
    next_ends_oth,
    payload,
    sums,
    mine,
    theirs,
    places,
    small,
    wide,
    combined,
    phi_rows,
    sig_rows,
    states_own,
    states_oth,
    act_low,
    gate_low,
    combined_low,
):
    info = core_place(row_devices)
    rows = x_in.shape[0]
    span = rows // 8
    masks = (keep_own, keep_oth)
    forward_states(
        1, info, gathered, (ends_own, ends_oth), (drive_own, drive_oth), masks, whole, rows_ref, tiles_ref,
        ids, (states_own, states_oth), (low_own, low_oth), places, small,
    )
    wide[...] = dot(low_own[...], out_own[1, 0]) + dot(low_oth[...], out_oth[1, 0])

    def element(start, carry):
        block = pl.ds(start, ELEMENT_ROWS)
        mixed = normed[block, :] * gain[1:2, :] + bias[1:2, :]
        value = wide[block, :] + skip[1:2, :] * mixed
        phi = 0.5 * (1.0 + lax.erf(value * inv_root_two))
        combined[block, :] = value
        phi_rows[block, :] = phi
        act_low[block, :] = (value * phi).astype(bf16)
        return carry

    over_blocks(rows, element)
    wide[...] = dot(act_low[...], glu[1])

    def element_two(start, carry):
        block = pl.ds(start, ELEMENT_ROWS)
        sig = jax.nn.sigmoid(wide[block, :] + glu_bias[1:2, :])
        sig_rows[block, :] = sig
        block_out[block, :] = x_in[block, :] + combined[block, :] * phi_rows[block, :] * sig
        return carry

    over_blocks(rows, element_two)
    sums[...] = jnp.zeros_like(sums)
    backward_half(
        1, info, grad_in, combined, phi_rows, sig_rows, normed, gain, bias, skip, glu, out_own, out_oth, masks,
        whole, rows_ref, tiles_ref, ids, gate_low, combined_grad, combined_low, grad_own, grad_oth,
        (next_ends_own, next_ends_oth), payload, sums, wide,
    )
    gradient_pack(act_low, gate_low, combined_low, low_own, low_oth, mine, theirs, wide)


def adjoint_states(
    layer, info, gathered, ends, grads, masks, whole, rows_ref, tiles_ref, ids, states, drives, lows, decay_sums,
    adjoints, places, small,
):
    rows = grads[0].shape[0]
    lanes = make_lanes(rows_ref, tiles_ref, layer, True, rows)
    core, place = info
    running_up = core == 1
    init = second_starts(
        running_up, place, lanes, gathered, ids, ends, (whole.at[1], whole.at[0]), places, small
    )
    width = lanes.states
    zero = jnp.zeros((8, width), f32)
    for side in range(2):
        adjoints[side][...] = states[side][...].astype(f32)

    def visit(side, where, re, im, sums):
        drive_re, drive_im = drives[side][where, :width], drives[side][where, width:]
        moved_re = adjoints[side][where, :width] - drive_re
        moved_im = adjoints[side][where, width:] - drive_im
        adjoints[side][where, :width] = re
        adjoints[side][where, width:] = im
        return (
            sums[0] + (re * moved_re + im * moved_im),
            sums[1] + (im * moved_re - re * moved_im),
            sums[2] + (re * drive_re + im * drive_im),
        )

    _, sums = sweep(
        running_up, grads, (masks[1], masks[0]), lanes, init, visit, ((zero, zero, zero), (zero, zero, zero))
    )
    decay_sums[...] = jnp.zeros_like(decay_sums)
    for side in range(2):
        for i in range(3):
            decay_sums[3 * side + i : 3 * side + i + 1, :] = jnp.sum(sums[side][i], 0, keepdims=True)
        lows[side][...] = (adjoints[side][...] * lanes.scaling(side)).astype(bf16)


def norm_backward(
    layer, low_own, low_oth, in_own, in_oth, grad, combined_grad, normed, inv_scale, gain, skip, sums, wide, finish
):
    rows, width = grad.shape
    wide[...] = dot_nt(low_own[...], in_own[layer, 0]) + dot_nt(low_oth[...], in_oth[layer, 0])
    zero = jnp.zeros((8, width), f32)

    def element(start, carry):
        block = pl.ds(start, ELEMENT_ROWS)
        mixed_grad = wide[block, :] + combined_grad[block, :] * skip[layer : layer + 1, :]
        unit = normed[block, :]
        weighted = mixed_grad * unit
        inner = mixed_grad * gain[layer : layer + 1, :]
        mean_one = jnp.sum(inner, 1, keepdims=True) * (1.0 / width)
        mean_two = jnp.sum(weighted * gain[layer : layer + 1, :], 1, keepdims=True) * (1.0 / width)
        spread = jnp.concatenate([inv_scale[block, :]] * (width // LANES), 1)
        finish(start, grad[block, :] + spread * (inner - mean_one - unit * mean_two))
        return carry[0] + fold(weighted), carry[1] + fold(mixed_grad)

    gain_sum, bias_sum = over_blocks(rows, element, (zero, zero))
    sums[2:3, :] = jnp.sum(gain_sum, 0, keepdims=True)
    sums[3:4, :] = jnp.sum(bias_sum, 0, keepdims=True)


def back_kernel(
    row_devices,
    in_low_own,
    in_low_oth,
    keep_own,
    keep_oth,
    whole,
    rows_ref,
    tiles_ref,
    ids,
    in_own,
    in_oth,
    out_own,
    out_oth,
    grad_in,
    combined_grad_in,
    normed_in,
    inv_in,
    gain,
    bias,
    skip,
    glu,
    combined,
    phi,
    sig,
    normed,
    act_low,
    low_own,
    low_oth,
    grad_out,
    combined_grad,
    next_own,
    next_oth,
    next_ends_own,
    next_ends_oth,
    payload,
    sums,
    mine,
    theirs,
    wide,
    gate_low,
    combined_low,
):
    info = core_place(row_devices)
    masks = (keep_own, keep_oth)
    sums[...] = jnp.zeros_like(sums)

    def finish(start, value):
        grad_out[pl.ds(start, ELEMENT_ROWS), :] = value

    norm_backward(
        1, in_low_own, in_low_oth, in_own, in_oth, grad_in, combined_grad_in, normed_in, inv_in, gain, skip, sums, wide,
        finish,
    )
    backward_half(
        0, info, grad_out, combined, phi, sig, normed, gain, bias, skip, glu, out_own, out_oth, masks, whole,
        rows_ref, tiles_ref, ids, gate_low, combined_grad, combined_low, next_own, next_oth,
        (next_ends_own, next_ends_oth), payload, sums, wide,
    )
    gradient_pack(act_low, gate_low, combined_low, low_own, low_oth, mine, theirs, wide)


def scan_kernel(
    layer,
    row_devices,
    gathered,
    ends_own,
    ends_oth,
    grad_own,
    grad_oth,
    keep_own,
    keep_oth,
    whole,
    rows_ref,
    tiles_ref,
    ids,
    states_own,
    states_oth,
    drive_own,
    drive_oth,
    mixed_low,
    low_own,
    low_oth,
    decay_sums,
    mine,
    theirs,
    places,
    small,
    adjoint_own,
    adjoint_oth,
):
    info = core_place(row_devices)
    masks = (keep_own, keep_oth)
    adjoint_states(
        layer, info, gathered, (ends_own, ends_oth), (grad_own, grad_oth), masks, whole, rows_ref, tiles_ref, ids,
        (states_own, states_oth), (drive_own, drive_oth), (low_own, low_oth), decay_sums,
        (adjoint_own, adjoint_oth), places, small,
    )
    store_columns(mine, 0, dot_tn(mixed_low[...], low_own[...]))
    store_columns(theirs, 0, dot_tn(mixed_low[...], low_oth[...]))


def final_kernel(
    low_own, low_oth, in_own, in_oth, grad_in, combined_grad, normed, inv_scale, gain, skip, out, sums, wide
):
    sums[...] = jnp.zeros_like(sums)

    def finish(start, value):
        out[pl.ds(start, ELEMENT_ROWS), :] = value

    norm_backward(
        0, low_own, low_oth, in_own, in_oth, grad_in, combined_grad, normed, inv_scale, gain, skip, sums, wide, finish
    )


def token_order_kernel(block_out, tokens_grad, halves, *columns):
    rows = block_out.shape[0]
    for source, part, out in ((block_out, columns[0], halves.at[0]), (tokens_grad, columns[1], halves.at[1])):
        store_token_order(part, 0, source[...], rows // 8)
        join_columns(out, part)


def store_columns(out, first, values):
    rows, width = values.shape
    for i in range(width // LANES):
        out[first + i * rows : first + (i + 1) * rows, :] = values[:, i * LANES : (i + 1) * LANES].astype(out.dtype)


def half_rows(core, act_low, gate_low, mine, theirs, first, wide):
    wide[...] = dot_tn(act_low[...], gate_low[...])
    half = wide.shape[0] // 2
    width = wide.shape[1]
    for out, which in ((mine, core), (theirs, 1 - core)):
        rows = pl.ds(pl.multiple_of(which * half, half), half)
        for i in range(width // LANES):
            out[first + i * half : first + (i + 1) * half, :] = wide[rows, i * LANES : (i + 1) * LANES].astype(out.dtype)


def gradient_pack(act_low, gate_low, combined_low, low_own, low_oth, mine, theirs, wide):
    store_columns(theirs, 0, dot_tn(low_oth[...], combined_low[...]))
    store_columns(mine, 0, dot_tn(low_own[...], combined_low[...]))
    size = low_own.shape[1] * (combined_low.shape[1] // LANES)
    half_rows(lax.axis_index("dir"), act_low, gate_low, mine, theirs, size, wide)


def slot(low_bit, parts):
    return jnp.bitwise_and(jnp.right_shift(lax.axis_index("seq"), low_bit), parts - 1)


def paired(values):
    while len(values) > 1:
        values = [a + b for a, b in zip(values[::2], values[1::2])]
    return values[0]


def part_rows(index, rows):
    return pl.ds(pl.multiple_of(index * rows, rows), rows)


def sum_parts(groups, outs, low_bit):
    parts = len(outs)
    mine = slot(low_bit, parts)
    for k, out in enumerate(outs):
        first = 0
        for rows, sources in groups:
            share = rows // parts
            where = part_rows(jnp.bitwise_xor(mine, k), share)
            total = paired([source[where, :].astype(f32) for source in sources])
            out[first : first + share, :] = total.astype(out.dtype)
            first += share


def gather_parts(sizes, sources, low_bit, outs):
    mine = slot(low_bit, len(sources))
    for k, source in enumerate(sources):
        first = 0
        for rows, out in zip(sizes, outs):
            out[part_rows(jnp.bitwise_xor(mine, k), rows), :] = source[first : first + rows, :]
            first += rows


def relay_kernel(payload_in, payload):
    payload[...] = payload_in[...]


def add_rows(out, at, sources, start, rows):
    where = pl.ds(pl.multiple_of(start, rows), rows)
    out[at : at + rows, :] = paired([source[where, :].astype(f32) for source in sources]).astype(out.dtype)


def put_small(outs, first, value):
    for out in outs:
        out[first : first + value.shape[0], :] = value.astype(out.dtype)


def half_groups(outer, inner, side):
    return ((outer // 2, side * (outer // 2)), (inner // 2, side * (inner // 2)))


def cores_kernel(outer_half, half, outer, got_outer, inner, got_inner, *refs):
    small_sums, (a_keep, a_send, b_keep, b_send), small = refs[:-5], refs[-5:-1], refs[-1]
    outer_rows, inner_rows = 2 * outer_half, 2 * (half - outer_half)
    mine = slot(0, 4)
    for side, out, parts in ((0, a_keep, (0, 2)), (0, a_send, (1, 3)), (1, b_keep, (0, 1)), (1, b_send, (2, 3))):
        (rows_one, at_one), (rows_two, at_two) = half_groups(outer_rows, inner_rows, side)
        for place, k in enumerate(parts):
            which = jnp.bitwise_xor(mine, k)
            add_rows(out, place * half, [outer, got_outer], which * outer_rows + at_one, rows_one)
            add_rows(out, place * half + rows_one, [inner, got_inner], which * inner_rows + at_two, rows_two)
    if small_sums:
        small_pack(*small_sums, small)
        put_small((a_keep, a_send), 2 * half, small[...])


def half_kernel(half, a_own, a_got, b_own, b_got, a_keep, a_send, b_keep, b_send):
    for own, got, outs in ((a_own, a_got, (a_keep, a_send)), (b_own, b_got, (b_keep, b_send))):
        for i, out in enumerate(outs):
            add_rows(out, 0, [own, got], i * half, half)
    if a_own.shape[0] > 2 * half:
        put_small((a_keep, a_send), half, a_own[2 * half :, :].astype(f32) + a_got[2 * half :, :].astype(f32))


def plane_kernel(half, outer_half, a_own, a_got, b_own, b_got, *outs):
    groups = []
    for own, got in ((a_own, a_got), (b_own, b_got)):
        groups.append((outer_half, [own.at[0:outer_half], got.at[0:outer_half]]))
        groups.append((half - outer_half, [own.at[outer_half:half], got.at[outer_half:half]]))
    sum_parts(groups, outs, 2)
    if a_own.shape[0] > half:
        put_small(outs, half // 2, a_own[half:, :].astype(f32) + a_got[half:, :].astype(f32))


def planes_kernel(*refs):
    refs[-1][...] = paired([source[...].astype(f32) for source in refs[:-1]]).astype(bf16)


def second_planes_kernel(*refs):
    sources, out, small = refs[:-2], refs[-2], refs[-1]
    rows = out.shape[0]
    out[...] = paired([source[0:rows, :].astype(f32) for source in sources]).astype(bf16)
    small[...] = paired([source[rows:, :].astype(f32) for source in sources])


def gather_kernel(outer_half, *refs):
    sources, outs = refs[:4], refs[4:]
    half = outs[0].shape[0]
    sizes, places = [], []
    for out in outs:
        sizes += [outer_half // 4, (half - outer_half) // 4]
        places += [out.at[0:outer_half], out.at[outer_half:half]]
    gather_parts(sizes, sources, 2, places)


def pair_kernel(a_own, a_got, b_own, b_got, a_out, b_out):
    half = a_own.shape[0]
    for own, got, out in ((a_own, a_got, a_out), (b_own, b_got, b_out)):
        out[0:half, :] = own[...]
        out[half : 2 * half, :] = got[...]


def last_pair_kernel(a_own, a_got, b_own, b_got, through, through_out, a_out, b_out):
    pair_kernel(a_own, a_got, b_own, b_got, a_out, b_out)


def assemble(outer_half, a_own, a_got, b_own, b_got, outer, inner):
    half = a_own.shape[0] // 2
    mine = slot(0, 4)
    for side, sources in ((0, (a_own, a_got, a_own, a_got)), (1, (b_own, b_own, b_got, b_got))):
        second = (0, 0, 1, 1) if side == 0 else (0, 1, 0, 1)
        for k, source in enumerate(sources):
            which = jnp.bitwise_xor(mine, k)
            first = second[k] * half
            rows = outer_half
            outer[part_rows(2 * which + side, rows), :] = source[first : first + rows, :]
            if inner is not None:
                rows = half - outer_half
                inner[part_rows(2 * which + side, rows), :] = source[first + outer_half : first + half, :]


def join_kernel(mine, theirs, *outs):
    core = lax.axis_index("dir")
    rows = mine.shape[1]
    for i, out in enumerate(outs):
        out[part_rows(core, rows), :] = mine[i]
        out[part_rows(1 - core, rows), :] = theirs[i]


def matrix_columns(source, first, out):
    rows, width = out.shape
    for i in range(width // LANES):
        out[:, i * LANES : (i + 1) * LANES] = source[first + i * rows : first + (i + 1) * rows, :].astype(f32)


def gate_part_kernel(outer_half, first, *refs):
    sources, out, whole = refs[:-2], refs[-2], refs[-1]
    assemble(outer_half, *sources, whole, None)
    out[...] = whole[first : first + out.shape[0], :]


def unpack_kernel(layer, olds, outer_half, *refs):
    refs = list(refs)
    take = lambda n: [refs.pop(0) for _ in range(n)]
    sources = take(4)
    take(olds)
    outs = take(2)
    buffers = take(2)
    whole = take(2)
    (sems,) = refs
    assemble(outer_half, *sources, *whole)
    copies = []
    for i in range(2):
        matrix_columns(whole[i], 0, buffers[i])
        copies.append(pltpu.make_async_copy(buffers[i], outs[i].at[layer, 0], sems.at[i]))
        copies[-1].start()
    for copy in copies:
        copy.wait()


def gate_kernel(layer, *refs):
    mine, theirs, (out, buffer, sems) = refs[0], refs[1], refs[-3:]
    core = lax.axis_index("dir")
    half = buffer.shape[0] // 2
    width = buffer.shape[1]
    for source, which in ((mine, core), (theirs, 1 - core)):
        rows = part_rows(which, half)
        for i in range(width // LANES):
            buffer[rows, i * LANES : (i + 1) * LANES] = source[i * half : (i + 1) * half, :].astype(f32)
    copy = pltpu.make_async_copy(buffer, out.at[layer], sems.at[0])
    copy.start()
    copy.wait()


def small_pack(sums_turn, sums_back, sums_last, decay_late, decay_early, out):
    per = sums_turn.shape[1] // LANES
    thirds = decay_late.shape[1] // LANES
    out[...] = jnp.zeros_like(out)
    kinds = (
        ((sums_last, 2), (sums_back, 2)),
        ((sums_last, 3), (sums_back, 3)),
        ((sums_back, 1), (sums_turn, 1)),
        ((sums_back, 0), (sums_turn, 0)),
    )
    at = 0
    for kind in kinds:
        for source, row in kind:
            for i in range(per):
                out[at : at + 1, :] = source[row : row + 1, i * LANES : (i + 1) * LANES]
                at += 1
    for side in range(2):
        for source in (decay_late, decay_early):
            for term in range(3):
                for i in range(thirds):
                    row = 3 * side + term
                    out[at : at + 1, :] = source[row : row + 1, i * LANES : (i + 1) * LANES]
                    at += 1


def small_out_kernel(own, got, table, gain, bias, rate, turn, skip, gate):
    layers, _, states = table.shape
    thirds = states // LANES
    width = gain.shape[1]
    per = width // LANES
    at = 0
    for out in (gain, bias, skip, gate):
        for layer in range(layers):
            for i in range(per):
                out[layer : layer + 1, i * LANES : (i + 1) * LANES] = own[at : at + 1, :] + got[at : at + 1, :]
                at += 1
    other = at + layers * 3 * thirds
    for layer in range(layers):
        for i in range(thirds):
            lanes = slice(i * LANES, (i + 1) * LANES)
            rows = [(layer * 3 + t) * thirds + i for t in range(3)]
            term_re, term_im, term_scale = (
                own[at + row : at + row + 1, :] + got[other + row : other + row + 1, :] for row in rows
            )
            re, im, scale, damping, step_size, rotation, square = (
                table[layer, t : t + 1, lanes] for t in range(7)
            )
            grad_re = (term_re * re - term_im * im) / square
            grad_im = (term_re * im + term_im * re) / square
            grad_scale = term_scale / scale
            grad_damping = grad_scale * square / scale - (grad_re * re + grad_im * im)
            grad_rotation = grad_im * re - grad_re * im
            log_rate = grad_damping * damping
            rate[layer, 0:1, lanes] = log_rate
            turn[layer, 0, 0:1, lanes] = grad_rotation * step_size
            turn[layer, 0, 1:2, lanes] = log_rate + grad_rotation * rotation


class Order:
    def __init__(self):
        self.tile = None

    def run(self, kernel, outs, operands, scratch=(), flops=0, name=None, spare=8, after=(), free_outs=0, alias=None,
            semaphores=0, cost=0, far=False, far_last=False):
        whole = pl.BlockSpec(memory_space=pltpu.VMEM)
        free = pl.BlockSpec(memory_space=pl.ANY)
        waits = list(after) + ([] if self.tile is None else [self.tile])
        inputs, results = len(operands), len(outs)
        skipped = len(waits)

        def body(*refs):
            token = refs[skipped + inputs]
            token[...] = jnp.zeros_like(token)
            kernel(*refs[skipped : skipped + inputs], *refs[skipped + inputs + 1 :])

        shapes = [jax.ShapeDtypeStruct((8, LANES), f32)]
        shapes += [jax.ShapeDtypeStruct(shape, dtype) for shape, dtype in outs]
        held = sum(jnp.dtype(dtype).itemsize * functools.reduce(lambda a, b: a * b, shape) for shape, dtype in scratch)
        specs = [free] * skipped + [pl.BlockSpec(memory_space=pltpu.HBM) if far else whole] * inputs
        if far_last:
            specs[-1] = pl.BlockSpec(memory_space=pltpu.HBM)
        aliases = {}
        if alias is not None:
            for operand, out in alias.items():
                specs[skipped + operand] = free
                aliases[skipped + operand] = out + 1
        extra = [pltpu.SemaphoreType.DMA((semaphores,))] if semaphores else []
        results = pl.pallas_call(
            body,
            out_shape=shapes,
            in_specs=specs,
            out_specs=[whole] + [free] * free_outs + [whole] * (results - free_outs),
            scratch_shapes=[pltpu.VMEM(shape, dtype) for shape, dtype in scratch] + extra,
            input_output_aliases=aliases,
            compiler_params=pltpu.CompilerParams(vmem_limit_bytes=held + spare * 2**20),
            cost_estimate=pl.CostEstimate(flops=int(1 + cost * 1e9), bytes_accessed=int(1 + cost * 3e6), transcendentals=0),
            name=name,
        )(*waits, *operands)
        self.tile = results[0]
        return results[1:]


def swap(value):
    return lax.ppermute(value, "dir", [(0, 1), (1, 0)])


def across(value, bits):
    count = lax.axis_size("seq")
    return lax.ppermute(value, "seq", [(i, i ^ bits) for i in range(count)])


def beyond(value):
    bit = 4
    while (1 << bit) < lax.axis_size("seq"):
        value = (value.astype(f32) + across(value, 1 << bit).astype(f32)).astype(value.dtype)
        bit += 1
    return value


def exchanged(payload, row_devices):
    count = lax.axis_size("seq")
    group = 2 * row_devices
    groups = None
    if count != row_devices:
        groups = [list(range(i, i + group)) for i in range(0, 2 * count, group)]
    return lax.all_to_all(payload, ("seq", "dir"), 0, 0, tiled=True, axis_index_groups=groups)


def sent(parts, low_bit):
    return [parts[0]] + [across(parts[k], k << low_bit) for k in (1, 2, 3)]


def shared(value, low_bit):
    return [value] + [across(value, k << low_bit) for k in (1, 2, 3)]


def body(
    tokens,
    segment_ids,
    norm_gain,
    norm_bias,
    input_matrix,
    output_matrix,
    rate_params,
    turn_params,
    skip_weight,
    glu_weight,
    glu_bias,
    cotangent,
):
    chip_rows, width = tokens.shape
    rows = chip_rows // 2
    layers = rate_params.shape[0]
    states = rate_params.shape[2]
    row_devices = LENGTH // chip_rows
    order = Order()
    here = functools.partial

    in_own, out_own = input_matrix, output_matrix
    in_oth = swap(input_matrix)
    rate_oth, turn_oth = swap(rate_params), swap(turn_params)
    out_oth = swap(output_matrix)
    segments = segment_ids.reshape(chip_rows // LANES, LANES)

    full = ((rows, width), f32)
    full_low = ((rows, width), bf16)
    columns = ((width // LANES, rows, LANES), f32)
    wide = ((rows, 2 * states), f32)
    wide_low = ((rows, 2 * states), bf16)
    ends = ((8, 2 * states), f32)
    payload_shape = ((2 * row_devices, 8, LANES), bf16)
    narrow = ((rows, LANES), f32)
    tile = ((8, LANES), f32)
    sums_shape = ((8, width), f32)
    decay_shape = ((8, states), f32)
    table_shape = ((layers, 16, states), f32)
    places = ((8, 2 * states), f32)
    in_size = width * (2 * states // LANES)
    out_size = 2 * states * (width // LANES)
    glu_size = width // 2 * (width // LANES)
    outer_size = out_size + glu_size
    outer_pack = ((outer_size, LANES), bf16)
    inner_pack = ((in_size, LANES), bf16)
    one = 2.0 * rows * width * 2 * states
    gate = 2.0 * rows * width * width
    scan = 1e9

    x0, normed0, inv0 = order.run(
        here(open_kernel, row_devices),
        [full, full, narrow],
        [tokens],
        [full_low, columns],
        far=True,
        semaphores=1,
        name="open_norm",
        cost=10,
    )
    table, keep_own, keep_oth, whole, ids, grad1 = order.run(
        here(open_masks_kernel, row_devices),
        [table_shape, narrow, narrow, ((2, 8, LANES), f32), tile, full],
        [segments, rate_params, turn_params, cotangent],
        [tile, columns, full],
        far_last=True,
        semaphores=1,
        name="open_masks",
    )
    mixed0, drive_own0, drive_oth0, ends_own, ends_oth, payload, table, tiles = order.run(
        here(open_second_kernel, row_devices),
        [full_low, wide, wide, ends, ends, payload_shape, table_shape, ((layers, 16, LANES), f32)],
        [normed0, norm_gain, norm_bias, table, keep_own, keep_oth, whole, ids, rate_oth, turn_oth, in_own, in_oth],
        name="open_scan",
        after=[out_oth],
    )
    gathered = exchanged(payload, row_devices)
    (
        low_own0, low_oth0, combined0, phi0, sig0, act_low0, x1, normed1, inv1, mixed1, drive_own1, drive_oth1,
        ends_own, ends_oth, payload,
    ) = order.run(
        here(mid_kernel, row_devices),
        [wide_low, wide_low, full, full, full, full_low, full, full, narrow, full_low, wide, wide, ends, ends,
         payload_shape],
        [gathered, ends_own, ends_oth, drive_own0, drive_oth0, keep_own, keep_oth, whole, table, tiles,
         ids, out_own, out_oth, x0, normed0, norm_gain, norm_bias, skip_weight, glu_weight, glu_bias, in_own, in_oth],
        [places, tile, full, wide, wide],
        flops=4 * one + gate + 3 * scan,
        name="mid",
    )
    gathered = exchanged(payload, row_devices)
    (
        low_own1, low_oth1, out1, combined_grad1, grad_own1, grad_oth1, ends_own, ends_oth, payload,
        sums_turn, mine, theirs,
    ) = order.run(
        here(turn_kernel, row_devices),
        [wide_low, wide_low, full, full, wide, wide, ends, ends, payload_shape, sums_shape, outer_pack, outer_pack],
        [gathered, ends_own, ends_oth, drive_own1, drive_oth1, keep_own, keep_oth, whole, table, tiles,
         ids, out_own, out_oth, x1, normed1, norm_gain, norm_bias, skip_weight, glu_weight, glu_bias, grad1],
        [places, tile, full, full, full, full, wide, wide, full_low, full_low, full_low],
        flops=4 * one + 2 * gate + 4 * scan,
        name="turn",
    )
    first_outer = [mine, swap(theirs)]
    gathered = exchanged(payload, row_devices)
    in_low_own1, in_low_oth1, decay_sums1, mine, theirs = order.run(
        here(scan_kernel, 1, row_devices),
        [wide_low, wide_low, decay_shape, inner_pack, inner_pack],
        [gathered, ends_own, ends_oth, grad_own1, grad_oth1, keep_own, keep_oth, whole, table, tiles,
         ids, low_own1, low_oth1, drive_own1, drive_oth1, mixed1],
        [places, tile, wide, wide],
        name="scan_one",
        after=[first_outer[1]],
    )
    first_inner = [mine, swap(theirs)]
    (
        grad0, combined_grad0, grad_own0, grad_oth0, ends_own, ends_oth, payload, sums_back, mine_outer, theirs_outer,
    ) = order.run(
        here(back_kernel, row_devices),
        [full, full, wide, wide, ends, ends, payload_shape, sums_shape, outer_pack, outer_pack],
        [in_low_own1, in_low_oth1, keep_own, keep_oth, whole, table, tiles, ids, in_own, in_oth, out_own, out_oth, grad1,
         combined_grad1, normed1, inv1, norm_gain, norm_bias, skip_weight, glu_weight, combined0, phi0, sig0, normed0,
         act_low0, low_own0, low_oth0],
        [full, full_low, full_low],
        name="back",
    )
    second_outer = [mine_outer, swap(theirs_outer)]
    outer_half = outer_size // 8
    half = outer_half + in_size // 8
    share_rows = half // 2
    small_rows = -(-(4 * layers * (width // LANES) + 6 * layers * (states // LANES)) // 16) * 16
    small_shape = ((small_rows, LANES), f32)

    def low(count):
        return ((count, LANES), bf16)

    def from_cores(packs, extra, sums, name, after=()):
        a_keep, a_send, b_keep, b_send, _ = order.run(
            here(cores_kernel, outer_half, half),
            [low(2 * half + extra)] * 2 + [low(2 * half)] * 2 + [small_shape],
            packs + sums,
            name=name,
            after=after,
            cost=CORES_COST,
        )
        return [a_keep, across(a_send, 1), b_keep, across(b_send, 2)]

    def from_first(parts, extra, name, after=()):
        a_keep, a_send, b_keep, b_send = order.run(
            here(half_kernel, half), [low(half + extra)] * 2 + [low(half)] * 2, parts, name=name, after=after
        )
        return [a_keep, across(a_send, 2), b_keep, across(b_send, 1)]

    def from_second(parts, extra, name, cost=0):
        return sent(
            order.run(
                here(plane_kernel, half, outer_half), [low(share_rows + extra)] * 4, parts, name=name, cost=cost
            ),
            2,
        )

    def gathered_half(parts, name, after=(), cost=0):
        a_half, b_half = order.run(
            here(gather_kernel, outer_half), [low(half)] * 2, parts, name=name, after=after, cost=cost
        )
        return a_half, across(a_half, 2), b_half, across(b_half, 1)

    def gathered_whole(halves, name):
        a_pair, b_pair = order.run(pair_kernel, [low(2 * half)] * 2, list(halves), name=name)
        return [a_pair, across(a_pair, 1), b_pair, across(b_pair, 2)]

    first = from_cores(first_outer + first_inner, 0, [], "first_cores")
    (payload,) = order.run(relay_kernel, [payload_shape], [payload], name="relay", cost=50)
    gathered = exchanged(payload, row_devices)
    first = from_first(first, 0, "first_half", [gathered])
    in_low_own0, in_low_oth0, decay_sums0, mine, theirs = order.run(
        here(scan_kernel, 0, row_devices),
        [wide_low, wide_low, decay_shape, inner_pack, inner_pack],
        [gathered, ends_own, ends_oth, grad_own0, grad_oth0, keep_own, keep_oth, whole, table, tiles,
         ids, low_own0, low_oth0, drive_own0, drive_oth0, mixed0],
        [places, tile, wide, wide],
        name="scan_zero",
        after=[second_outer[1]],
    )
    second_inner = [mine, swap(theirs)]
    grad_x, sums_last = order.run(
        final_kernel,
        [full, sums_shape],
        [in_low_own0, in_low_oth0, in_own, in_oth, grad0, combined_grad0, normed0, inv0, norm_gain, skip_weight],
        [full],
        name="final_norm",
    )
    first = from_second(first, 0, "first_plane", 50)
    second = from_cores(
        second_outer + second_inner, small_rows, [sums_turn, sums_back, sums_last, decay_sums0, decay_sums1],
        "second_cores",
    )
    (halves,) = order.run(
        token_order_kernel, [((2, rows, width), f32)], [out1, grad_x], [columns, columns], name="token_order"
    )
    (share,) = order.run(planes_kernel, [low(share_rows)], first, name="first_planes", cost=50)
    first = shared(beyond(share), 2)
    second = from_first(second, small_rows, "second_half")
    first = gathered_half(first, "first_gather", cost=50)
    second = from_second(second, small_rows, "second_plane")
    share, small = order.run(second_planes_kernel, [low(share_rows), small_shape], second, name="second_planes")
    second = shared(beyond(share), 2)
    first = gathered_whole(first, "first_pair")
    small = beyond(small)
    got_small = swap(small)
    in_shape, out_shape = input_matrix.shape, output_matrix.shape

    def gate_part(quarters, name):
        (value,) = order.run(
            here(gate_part_kernel, outer_half, out_size), [low(glu_size)], quarters, [outer_pack], name=name
        )
        return value

    def gate_out(layer, mine, theirs, old, name):
        return order.run(
            here(gate_kernel, layer), [(glu_weight.shape, f32)], [mine, theirs] + old, [((width, width), f32)],
            name=name, free_outs=1, alias={2: 0} if old else None, semaphores=1,
        )

    def unpack(quarters, layer, old, name):
        return order.run(
            here(unpack_kernel, layer, len(old), outer_half),
            [(out_shape, f32), (in_shape, f32)],
            quarters + old,
            [(out_shape[2:], f32), (in_shape[2:], f32), outer_pack, inner_pack],
            name=name,
            free_outs=2,
            alias={4 + i: i for i in range(len(old))},
            semaphores=2,
        )

    second = gathered_half(second, "second_gather", cost=50)
    halves, a_pair, b_pair = order.run(
        last_pair_kernel, [((2, rows, width), f32), low(2 * half), low(2 * half)], list(second) + [halves],
        name="second_pair", free_outs=1, alias={4: 0}, after=[first[1], first[3]],
    )
    second = [a_pair, across(a_pair, 1), b_pair, across(b_pair, 2)]
    gate_one = gate_part(first, "gate_one")
    got_one = swap(gate_one)
    results = unpack(first, 1, [], "unpack_one")
    gain_grad, bias_grad, rate_grad, turn_grad, skip_grad, gate_grad = order.run(
        small_out_kernel,
        [((layers, width), f32), ((layers, width), f32), (rate_params.shape, f32), (turn_params.shape, f32),
         ((layers, width), f32), ((layers, width), f32)],
        [small, got_small, table],
        name="small_out",
    )
    whole_rows = ((chip_rows, width), f32)
    block_output, tokens_grad = order.run(
        join_kernel, [whole_rows, whole_rows], [halves, swap(halves)], name="join"
    )
    glu_all = gate_out(1, gate_one, got_one, [], "gate_out_one")
    gate_zero = gate_part(second, "gate_zero")
    got_zero = swap(gate_zero)
    out_all, in_all = unpack(second, 0, list(results), "unpack_zero")
    (glu_all,) = gate_out(0, gate_zero, got_zero, list(glu_all), "gate_out_zero")
    return (
        block_output,
        tokens_grad,
        gain_grad,
        bias_grad,
        in_all,
        out_all,
        rate_grad,
        turn_grad,
        skip_grad,
        glu_all,
        gate_grad,
    )


def solution(mesh):
    return jax.shard_map(
        body,
        mesh=mesh,
        in_specs=(
            P("seq", None),
            P("seq"),
            P(),
            P(),
            P(None, "dir", None, None),
            P(None, "dir", None, None),
            P(None, "dir", None),
            P(None, "dir", None, None),
            P(),
            P(),
            P(),
            P("seq", None),
        ),
        out_specs=(
            P("seq", None),
            P("seq", None),
            P(),
            P(),
            P(None, "dir", None, None),
            P(None, "dir", None, None),
            P(None, "dir", None),
            P(None, "dir", None, None),
            P(),
            P(),
            P(),
        ),
        check_vma=False,
    )
```
